512 devices in a mesh: tower: 4 (over x), wide: 128 (over z, y, core).
Axes of the slice: x: 4, y: 4, z: 16, core: 2. Of those that a mesh axis runs over, the one named last changes fastest.
Arguments:
- user_rows: bfloat16 [196608, 512], P('wide', 'tower'), may hold values from -6 to 6
- positive_rows: bfloat16 [196608, 512], P('wide', 'tower'), may hold values from -6 to 6
- centroids: float32 [4096, 512], P('wide'), may hold values from -3.5 to 3.5
- residuals: bfloat16 [4096, 256, 512], P('wide', 'tower'), may hold values from -6 to 6
- block_lists: int32 [1024, 16], P('wide'), may hold values from 0 to 4095, as said below
- block_lengths: int32 [1024], P('wide'), may hold values from 1 to 16, 8192 in all
- cluster_counts: int32 [4096], P('wide'), may hold values from 64 to 4096
- ad_counts: int32 [4096, 256], P('wide'), may hold values from 1 to 256
Outputs:
- user_loss: float32 [196608], P('wide')
- user_grad: float32 [196608, 512], P('wide', 'tower')
- centroid_grad: float32 [4096, 512], P('wide', 'tower')
The draws below stay inside these ranges and needn't reach their ends.
Inputs may be any that keep to these rules, and one draw needn't show every extreme that they name: `block_lists`: on one index of wide, the 128 list entries name different clusters; at most 1 of them lie on one shard (cluster id // 32), and on some shard exactly 1. Entries at or past a block's length are ignored.
All inputs are finite; a program needn't handle non-finite values. No bound on the sum of `block_lengths` on one device may be relied on, other than what follows from the above.
Results may differ from the reference program's by a relative error of at most 0.0035.
Values may be sent and summed in bfloat16 or wider, within the bound.
A program may use at most 128 MiB of HBM per device.

```python
import math
import jax
import jax.numpy as jnp
import numpy as np
from jax import lax

E = 512
TILE = 256
KMAX = 16
UB_DEV = 8
UB = 192
CL_DEV = 32
LOSS_SCALE = 16
TQ = 64
CAP = 1
NBLK = 1024
USERS = 196608
NCL = 4096
N_TOWER = 4
N_WIDE = 128


def shared_lists(key):
    key = jax.random.fold_in(key, 7)
    subkeys = jax.random.split(key, 4)
    candidates = N_WIDE * CAP
    entries = UB_DEV * KMAX
    scores = jax.random.randint(subkeys[0], (N_WIDE, N_WIDE, CL_DEV), 0, 1 << 20) * CL_DEV + jnp.arange(CL_DEV)
    local_ids = jnp.argsort(scores, axis=-1)[..., :CAP]
    shard_ids = jnp.arange(N_WIDE)[None, :, None]
    cluster_ids = (shard_ids * CL_DEV + local_ids).reshape(N_WIDE, candidates)
    priority = jax.random.randint(subkeys[1], (N_WIDE, candidates), 0, 1 << 12) * candidates + jnp.arange(candidates)
    chosen_shard = jax.random.randint(subkeys[2], (N_WIDE, 1), 0, N_WIDE)
    favoured = (jnp.arange(candidates) // CAP)[None, :] == chosen_shard
    priority = priority + favoured.astype(jnp.int32) * ((1 << 12) * candidates)
    picked = jnp.argsort(-priority, axis=-1)[:, :entries]
    chosen_ids = jnp.take_along_axis(cluster_ids, picked, axis=-1)
    mixing = jax.random.randint(subkeys[3], (N_WIDE, entries), 0, 1 << 12) * entries + jnp.arange(entries)
    chosen_ids = jnp.take_along_axis(chosen_ids, jnp.argsort(mixing, axis=-1), axis=-1)
    return chosen_ids.reshape(N_WIDE * UB_DEV, KMAX).astype(jnp.int32)


def draw_block_lists(key, part):
    return shared_lists(key)


def draw_user_rows(key, part):
    key = jax.random.fold_in(key, 3)
    values = jnp.clip(jax.random.normal(key, (USERS, E), jnp.float32), -6.0, 6.0)
    return values.astype(jnp.bfloat16)


def draw_centroids(key, part):
    key = jax.random.fold_in(key, 5)
    values = jnp.clip(0.5 * jax.random.normal(key, (NCL, E), jnp.float32), -2.0, 2.0)
    return values


def place_ends(values, rng, low, largest):
    index_at = [jax.random.randint(jax.random.fold_in(rng, axis), (), 0, length) for axis, length in enumerate(values.shape)]
    longest = values.shape.index(max(values.shape))
    neighbour = index_at[:longest] + [(index_at[longest] + 1) % values.shape[longest]] + index_at[longest + 1:]
    return values.at[tuple(index_at)].set(low).at[tuple(neighbour)].set(largest)


def level_of(key, extent, shards, smallest, top_value):
    factor_of = 1.0
    for dim, shards_of in shards:
        draws = jax.random.uniform(jax.random.fold_in(jax.random.fold_in(key, 6), dim), (shards_of,), jnp.float32, smallest / len(shards), top_value / len(shards))
        factor_of = factor_of * jnp.repeat(jnp.exp(draws), extent[dim] // shards_of).reshape((-1,) + (1,) * (len(extent) - 1 - dim))
    return factor_of


def profile(amount, total, bound, slope):
    loads = [(1 << 20) // math.isqrt(standing ** slope) + 1 for standing in range(2, amount + 1)]
    surplus, counts = total - bound - (amount - 1), [1] * (amount - 1)
    while surplus > 0:
        movable = [i for i in range(amount - 1) if counts[i] < bound]
        pool, left = sum([loads[i] for i in movable]), surplus
        for i in movable:
            extra = min(bound - counts[i], max(1, left * loads[i] // pool), surplus)
            counts[i] = counts[i] + extra
            surplus = surplus - extra
    return np.array([bound] + counts)


def ragged_sizes(key, number_of, total, bound, slope):
    if number_of == 2:
        one = jax.random.randint(key, (), max(1, total - bound), min(bound, total - 1) + 1)
        return jnp.stack([one, total - one])
    lengths = jnp.asarray(profile(number_of, total, bound, slope), jnp.int32)
    twos = (number_of - 1) // 2
    source_of, receiver = lengths[1:1 + 2 * twos:2], lengths[2:2 + 2 * twos:2]
    room = jnp.minimum(source_of - 1, bound - receiver)
    moved = jax.random.randint(jax.random.fold_in(key, 1), (twos,), 0, 1 << 20) % (room + 1)
    lengths = lengths.at[1:1 + 2 * twos:2].set(source_of - moved).at[2:2 + 2 * twos:2].set(receiver + moved)
    return lengths[jax.random.permutation(jax.random.fold_in(key, 2), number_of)]


def centred(own_key, shape, scale, bound, cuts=(), held_as=jnp.bfloat16):
    values = jax.random.normal(own_key, shape, jnp.float32) * scale
    if len(cuts) > 0:
        values = level_of(own_key, shape, cuts, -0.22, 0.18) * values
    return jnp.clip(values, min=-bound, max=bound).astype(held_as)


def setup_inputs(seed: int = 0) -> dict:
    key_of = jax.random.split(jax.random.key(seed), 9)
    return {
        "user_rows": draw_user_rows(jax.random.fold_in(key_of[8], 71), 0),
        "positive_rows": centred(key_of[1], (USERS, E), 1.0, 6.0, ((0, 128), (1, 4))),
        "centroids": draw_centroids(jax.random.fold_in(key_of[8], 71), 0),
        "residuals": centred(key_of[3], (NCL, TILE, E), 1.0, 6.0, ((0, 128), (1, 4))),
        "block_lists": draw_block_lists(jax.random.fold_in(key_of[8], 71), 0),
        "block_lengths": ragged_sizes(key_of[5], NBLK, NBLK * KMAX // 2, KMAX, 2).astype(jnp.int32),
        "cluster_counts": place_ends(jax.random.randint(key_of[6], (NCL,), 64, 4097), jax.random.fold_in(key_of[6], 1), 64, 4096).astype(jnp.int32),
        "ad_counts": place_ends(jax.random.randint(key_of[7], (NCL, TILE), 1, 257), jax.random.fold_in(key_of[7], 1), 1, 256).astype(jnp.int32),
    }


def reference(user_rows, positive_rows, centroids, residuals, block_lists, block_lengths, cluster_counts, ad_counts):
    score_scale = 1.0 / math.sqrt(E)
    ad_weights = ad_counts.astype(jnp.float32)
    expected = cluster_counts.astype(jnp.float32)[:, None] * ad_weights / lax.optimization_barrier(jnp.sum(ad_weights, axis=1, keepdims=True))
    correction = jnp.log(expected).astype(jnp.bfloat16)
    user_blocks = user_rows.reshape(NBLK, UB, E)
    positive_blocks = positive_rows.reshape(NBLK, UB, E)

    def one_block(inputs):
        user_block, positive, listed, length = inputs
        tile_rows = (centroids[listed][:, None, :] + residuals[listed].astype(jnp.float32)).astype(jnp.bfloat16).reshape(KMAX * TILE, E)
        log_correction = correction[listed].reshape(KMAX * TILE).astype(jnp.float32)
        logits = jnp.dot(user_block, tile_rows.T, preferred_element_type=jnp.float32) * score_scale - log_correction[None, :]
        used_slots = jnp.arange(KMAX * TILE) // TILE < length
        logits = jnp.where(used_slots[None, :], logits, -jnp.inf)
        positive_wide = positive.astype(jnp.float32)
        positive_logit = lax.optimization_barrier(jnp.sum(user_block.astype(jnp.float32) * positive_wide, axis=1)) * score_scale
        ceiling = jnp.maximum(lax.optimization_barrier(jnp.max(logits, axis=1)), positive_logit)
        row_total = lax.optimization_barrier(jnp.sum(jnp.exp(logits - ceiling[:, None]), axis=1)) + jnp.exp(positive_logit - ceiling)
        log_total = ceiling + jnp.log(row_total)
        row_loss = log_total - positive_logit
        softmax_probs = jnp.exp(logits - log_total[:, None]).astype(jnp.bfloat16)
        positive_prob = jnp.exp(positive_logit - log_total)
        ad_term = jnp.dot(softmax_probs, tile_rows, preferred_element_type=jnp.float32)
        user_grad = LOSS_SCALE * score_scale * (ad_term + (positive_prob - 1.0)[:, None] * positive_wide)
        quarter_mass = lax.optimization_barrier(jnp.sum(softmax_probs.astype(jnp.float32).reshape(UB, KMAX, N_TOWER, TQ), axis=3)).astype(jnp.bfloat16)
        slot_grad = jnp.einsum('ukq,ue->ke', quarter_mass.astype(jnp.float32), user_block.astype(jnp.float32)) * (LOSS_SCALE * score_scale)
        return (row_loss, user_grad, slot_grad)
    losses, user_grads, slot_grads = lax.map(one_block, (user_blocks, positive_blocks, block_lists, block_lengths))
    centroid_grad = jnp.zeros((NCL, E), jnp.float32).at[block_lists.reshape(NBLK * KMAX)].add(slot_grads.reshape(NBLK * KMAX, E))
    return (losses.reshape(USERS), user_grads.reshape(USERS, E), centroid_grad)
```

```python
import functools
import math

import jax
import jax.numpy as jnp
from jax import lax
from jax.experimental import pallas as pl
from jax.experimental.pallas import tpu as pltpu
from jax.sharding import Mesh, PartitionSpec as P

LOSS_SCALE = 16
AXES = ("x", "z", "y", "c")
SPLIT = (16, 4, 2)
LOW = -1e30
MESH = pl.DeviceIdType.MESH
HBM = pl.BlockSpec(memory_space=pl.ANY)
VMEM = pl.BlockSpec(memory_space=pltpu.VMEM)
SMEM = pl.BlockSpec(memory_space=pltpu.SMEM)
CODE_ROWS = 16


def remote(src, dst, sends, recvs, k, where):
    return pltpu.make_async_remote_copy(
        src_ref=src,
        dst_ref=dst,
        send_sem=sends.at[k],
        recv_sem=recvs.at[k],
        device_id=where,
        device_id_type=MESH,
    )


def greet(peers):
    barrier = pltpu.get_barrier_semaphore()
    for where in peers:
        pl.semaphore_signal(barrier, inc=1, device_id=where, device_id_type=MESH)
    pl.semaphore_wait(barrier, len(peers))


def gather_kernel(
    sizes, tiles, users, positives, codes, shift,
    all_tiles, all_users, own_positives, all_shift, sends, recvs, locals_,
):
    nx, nz, ny, nc = sizes
    x, z, y, c = (lax.axis_index(a) for a in AXES)
    rows = users.shape[0] // nx
    depth = users.shape[1]
    half = tiles.shape[1]
    quarter = half // 2
    at_x = lambda d: lax.rem(x + d + nx, nx)
    at_y = lambda d: lax.rem(y + d + ny, ny)
    at_z = lambda d: lax.rem(z + d + nz, nz)
    to_x = lambda d: {"x": at_x(d)}
    to_y = lambda d: {"y": at_y(d)}
    to_z = lambda d: {"z": at_z(d)}
    sibling = {"c": 1 - c}

    greet(
        [to_x(d) for d in range(1, nx)]
        + [to_y(d) for d in range(1, ny)]
        + [to_z(1), to_z(-1), sibling]
    )

    count = [0]
    sent = []

    def push(src, dst, where, landing):
        k = count[0]
        count[0] += 1
        copy = remote(src, dst, sends, recvs, k, where)
        copy.start()
        sent.append(copy)
        return remote(landing, landing, sends, recvs, k, where)

    columns = lambda i: pl.ds(pl.multiple_of(i * depth, depth), depth)
    part = lambda i: pl.ds(pl.multiple_of(i * rows, rows), rows)
    home = all_users.at[z, c]

    def block(h, a, b):
        return all_tiles.at[at_y(b), at_x(a), h] if h == 0 else all_tiles.at[at_y(a), at_x(b), h]

    first = (to_x, to_y)
    second = (to_y, to_x)
    lower, upper = pl.ds(0, quarter), pl.ds(quarter, quarter)

    arrivals = []
    for d in range(1, nx):
        arrivals.append(
            push(
                users.at[part(at_x(d))], home.at[pl.ds(0, rows), columns(x)], to_x(d),
                home.at[pl.ds(0, rows), columns(at_x(-d))],
            )
        )
    p1 = {}
    for h in (0, 1):
        for d in (1, -1):
            p1[h, d] = push(tiles.at[h], block(h, 0, 0), first[h](d), block(h, -d, 0))
    own = [
        pltpu.make_async_copy(users.at[part(x)], home.at[pl.ds(0, rows), columns(x)], locals_.at[0]),
        pltpu.make_async_copy(codes, home.at[pl.ds(rows, CODE_ROWS)], locals_.at[1]),
        pltpu.make_async_copy(tiles, all_tiles.at[y, x], locals_.at[2]),
        pltpu.make_async_copy(shift, all_shift.at[y], locals_.at[3]),
        pltpu.make_async_copy(positives.at[part(x)], own_positives.at[:, columns(x)], locals_.at[4]),
    ]
    for copy in own:
        copy.start()
    late = []
    p2 = {}
    for h in (0, 1):
        for d in (1, -1):
            p2[h, 0, d] = push(tiles.at[h], block(h, 0, 0), second[h](d), block(h, 0, -d))
    for d in range(1, nx):
        late.append(
            push(
                positives.at[part(at_x(d))], own_positives.at[:, columns(x)], to_x(d),
                own_positives.at[:, columns(at_x(-d))],
            )
        )
    for d in range(1, ny):
        late.append(push(shift, all_shift.at[y], to_y(d), all_shift.at[at_y(-d)]))

    for arrival in arrivals:
        arrival.wait_recv()
    own[0].wait()
    own[1].wait()

    chunk = lambda d: all_users.at[at_z(d), c]
    other = lambda d: all_users.at[at_z(d), 1 - c]
    steps = nz // 2
    up, down = {}, {}

    def ring(s):
        if s > 0:
            up[s - 1].wait_recv()
            if s - 1 in down:
                down[s - 1].wait_recv()
        if s < steps:
            up[s] = push(chunk(-s), chunk(-s), to_z(1), chunk(-s - 1))
        if s < steps - 1:
            down[s] = push(chunk(s), chunk(s), to_z(-1), chunk(s + 1))
        late.append(push(chunk(-s), chunk(-s), sibling, other(-s)))
        if 0 < s < steps:
            late.append(push(chunk(s), chunk(s), sibling, other(s)))

    turns = list(range(steps + 1))
    ring(turns.pop(0))
    while len(turns) > steps - 3 and turns:
        ring(turns.pop(0))

    for h in (0, 1):
        for d in (1, -1):
            p1[h, d].wait_recv()
    q = {}
    for h in (0, 1):
        for d in (1, -1):
            cut = lower if d == 1 else upper
            q[h, d] = push(
                block(h, -d, 0).at[cut], block(h, -d, 0).at[cut], first[h](d), block(h, -2 * d, 0).at[cut]
            )
    for j in (1, -1):
        for h in (0, 1):
            for d in (1, -1):
                p2[h, j, d] = push(block(h, j, 0), block(h, j, 0), second[h](d), block(h, j, -d))
    if turns:
        ring(turns.pop(0))

    def onward(j):
        for h in (0, 1):
            for d in (1, -1):
                p2[h, j, d].wait_recv()
                cut = lower if d == 1 else upper
                late.append(
                    push(
                        block(h, j, -d).at[cut], block(h, j, -d).at[cut], second[h](d),
                        block(h, j, -2 * d).at[cut],
                    )
                )

    onward(0)
    for h in (0, 1):
        for d in (1, -1):
            q[h, d].wait_recv()
    for h in (0, 1):
        for d in (1, -1):
            p2[h, 2, d] = push(block(h, 2, 0), block(h, 2, 0), second[h](d), block(h, 2, -d))
    if turns:
        ring(turns.pop(0))
    onward(1)
    while turns:
        ring(turns.pop(0))
    onward(-1)
    onward(2)
    for arrival in late:
        arrival.wait_recv()
    for copy in own[2:]:
        copy.wait()
    for copy in sent:
        copy.wait_send()
    assert count[0] == sends.shape[0], count[0]


def fetch(users, tiles, list_ref, ubuf, tbuf, usem, tsem, half, e, slot):
    b, tile = list_ref[0, e], list_ref[1, e]
    per = 2 * half
    yp, cl = tile // per, tile % per
    w, i = b // 2, b % 2
    rows = ubuf.shape[1]
    return (
        pltpu.make_async_copy(
            users.at[w, pl.ds(pl.multiple_of(i * rows, rows), rows)], ubuf.at[slot], usem.at[slot]
        ),
        pltpu.make_async_copy(
            tiles.at[yp, :, cl // half, cl % half], tbuf.at[slot], tsem.at[slot]
        ),
    )


def scores(ubuf, tbuf, shift_ref, slot, tile, scale):
    user = ubuf[slot]
    ads = tbuf[slot].reshape(tbuf.shape[1] * tbuf.shape[2], tbuf.shape[3])
    pick = lax.broadcasted_iota(jnp.int32, (shift_ref.shape[0], user.shape[0]), 0) == tile
    shift = lax.dot_general(
        shift_ref[...], pick.astype(jnp.float32).astype(jnp.bfloat16), (((0,), (0,)), ((), ())),
        preferred_element_type=jnp.float32,
    )
    raw = lax.dot_general(ads, user, (((1,), (1,)), ((), ())), preferred_element_type=jnp.float32)
    return user, ads, raw * scale - shift


def stats_kernel(
    half, scale, codes, mine, users, tiles, shift_ref,
    stats, list_ref, zeroed, ubuf, tbuf, zbuf, usem, tsem, zsem,
):
    nw = users.shape[0]
    ny = tiles.shape[0]
    rows = ubuf.shape[1]
    t = mine[0]
    zbuf[...] = jnp.zeros_like(zbuf)
    piece = zbuf.shape[0]
    zeros = [
        pltpu.make_async_copy(zbuf, zeroed.at[pl.ds(k * piece, piece)], zsem.at[k])
        for k in range(zeroed.shape[0] // piece)
    ]
    for copy in zeros:
        copy.start()

    def gather(w, n):
        for i in range(2):
            for yp in range(ny):
                list_ref[0, n] = w * 2 + i
                list_ref[1, n] = yp * (2 * half) + codes[1, w * ny + yp]
                n = n + (codes[0, w * ny + yp] == 2 * t + i).astype(jnp.int32)
        return n

    total = lax.fori_loop(0, nw, gather, jnp.int32(0))
    list_ref[0, total] = -1
    list_ref[1, total] = 0
    list_ref[2, 0] = total
    stats[:, 0:1, :] = jnp.full((stats.shape[0], 1, stats.shape[2]), LOW, jnp.float32)
    stats[:, 1:2, :] = jnp.zeros((stats.shape[0], 1, stats.shape[2]), jnp.float32)
    get = functools.partial(fetch, users, tiles, list_ref, ubuf, tbuf, usem, tsem, half)

    @pl.when(total > 0)
    def _():
        for copy in get(0, 0):
            copy.start()

    def step(e, _):
        slot = e % 2

        @pl.when(e + 1 < total)
        def _():
            for copy in get(e + 1, 1 - slot):
                copy.start()

        for copy in get(e, slot):
            copy.wait()
        b, tile = list_ref[0, e], list_ref[1, e]
        _, _, logits = scores(ubuf, tbuf, shift_ref, slot, tile, scale)
        before = stats[b, 0:1, 0:rows]
        held = stats[b, 1:2, 0:rows]
        top = jnp.maximum(before, jnp.max(logits, axis=0, keepdims=True))
        stats[b, 0:1, 0:rows] = top
        stats[b, 1:2, 0:rows] = held * jnp.exp(before - top) + jnp.sum(
            jnp.exp(logits - top), axis=0, keepdims=True
        )
        return 0

    lax.fori_loop(0, total, step, 0)
    for copy in zeros:
        copy.wait()


def as_row(column):
    n = column.shape[0]
    eye = lax.broadcasted_iota(jnp.int32, (n, n), 0) == lax.broadcasted_iota(jnp.int32, (n, n), 1)
    return jnp.sum(jnp.where(eye, column, 0.0), axis=0, keepdims=True)


def as_column(row):
    n = row.shape[1]
    eye = lax.broadcasted_iota(jnp.int32, (n, n), 0) == lax.broadcasted_iota(jnp.int32, (n, n), 1)
    return jnp.sum(jnp.where(eye, row, 0.0), axis=1, keepdims=True)


def total_kernel(
    sizes, scale, stats, user, positive, totals, losses, factor,
    came, mine, got, lost, s1, r1, s2, r2, s3, r3,
):
    nx, nz, ny, nc = sizes
    x, z, y, c = (lax.axis_index(a) for a in AXES)
    nw = nz * nc
    me = z * nc + c
    rows = user.shape[0] // 2
    barrier = pltpu.get_barrier_semaphore()

    def there(d):
        p = lax.rem(me + d, nw)
        return p, {"z": p // nc, "c": p % nc}

    def hello(d, _):
        pl.semaphore_signal(barrier, inc=1, device_id=there(d)[1], device_id_type=MESH)
        return 0

    lax.fori_loop(1, nw, hello, 0)
    for d in range(1, nx):
        pl.semaphore_signal(
            barrier, inc=1, device_id={"x": lax.rem(x + d, nx)}, device_id_type=MESH
        )
    pl.semaphore_wait(barrier, nw - 1 + nx - 1)

    def out(d, _):
        p, where = there(d)
        remote(stats.at[p], came.at[me], s1, r1, d, where).start()
        return 0

    lax.fori_loop(1, nw, out, 0)
    dots = []
    for i in range(2):
        u = user[i * rows:(i + 1) * rows].astype(jnp.float32)
        v = positive[i * rows:(i + 1) * rows].astype(jnp.float32)
        dots.append(as_row(jnp.sum(u * v, axis=1, keepdims=True)) * scale)

    def landed(d, _):
        p, where = there(nw - d)
        remote(came.at[p], came.at[p], s1, r1, d, where).wait_recv()
        return 0

    lax.fori_loop(1, nw, landed, 0)
    came[pl.ds(me, 1)] = stats[pl.ds(me, 1)]
    mine[...] = jnp.zeros_like(mine)
    factor[...] = jnp.zeros_like(factor)
    lost[pl.ds(x, 1)] = jnp.zeros((1,) + lost.shape[1:], jnp.float32)
    for i in range(2):
        tops = came[:, i, 0:1, 0:rows]
        sums = came[:, i, 1:2, 0:rows]
        ceiling = jnp.maximum(jnp.max(tops, axis=0), dots[i])
        whole = jnp.sum(sums * jnp.exp(tops - ceiling[None]), axis=0) + jnp.exp(dots[i] - ceiling)
        log_total = ceiling + jnp.log(whole)
        mine[i, :, 0:rows] = log_total
        lost[pl.ds(x, 1), i, :, 0:rows] = (log_total - dots[i])[None]
        factor[i, :, 0:rows] = jnp.exp(dots[i] - log_total) - 1.0

    def back(d, _):
        _, where = there(d)
        remote(mine, got.at[me], s2, r2, d, where).start()
        return 0

    lax.fori_loop(1, nw, back, 0)
    for d in range(1, nx):
        remote(lost.at[x], lost.at[x], s3, r3, d, {"x": lax.rem(x + d, nx)}).start()
    got[pl.ds(me, 1)] = mine[...][None]

    def done(d, _):
        p, where = there(nw - d)
        remote(got.at[p], got.at[p], s2, r2, d, where).wait_recv()
        return 0

    lax.fori_loop(1, nw, done, 0)
    totals[...] = got[...]
    for d in range(1, nx):
        frm = lax.rem(x - d + nx, nx)
        remote(lost.at[frm], lost.at[frm], s3, r3, d, {"x": frm}).wait_recv()
    losses[...] = lost[...]

    def left(d, _):
        p, where = there(d)
        remote(stats.at[p], came.at[me], s1, r1, d, where).wait_send()
        remote(mine, got.at[me], s2, r2, d, where).wait_send()
        return 0

    lax.fori_loop(1, nw, left, 0)
    for d in range(1, nx):
        remote(lost.at[x], lost.at[x], s3, r3, d, {"x": lax.rem(x + d, nx)}).wait_send()


def grads_kernel(
    half, scale, list_ref, users, tiles, shift_ref, totals, _zeroed,
    grads, cluster, ubuf, tbuf, acc, gout, usem, tsem, gsem,
):
    rows = ubuf.shape[1]
    parts = tbuf.shape[1]
    total = list_ref[2, 0]
    cluster[...] = jnp.zeros_like(cluster)
    get = functools.partial(fetch, users, tiles, list_ref, ubuf, tbuf, usem, tsem, half)

    @pl.when(total > 0)
    def _():
        for copy in get(0, 0):
            copy.start()

    def put(b, slot):
        return pltpu.make_async_copy(gout.at[slot], grads.at[b], gsem.at[slot])

    def step(e, n):
        slot = e % 2

        @pl.when(e + 1 < total)
        def _():
            for copy in get(e + 1, 1 - slot):
                copy.start()

        for copy in get(e, slot):
            copy.wait()
        b, tile = list_ref[0, e], list_ref[1, e]
        fresh = jnp.logical_or(e == 0, list_ref[0, jnp.maximum(e - 1, 0)] != b)
        last = list_ref[0, e + 1] != b
        user, ads, logits = scores(ubuf, tbuf, shift_ref, slot, tile, scale)
        probs = jnp.exp(logits - totals[b, :, 0:rows]).astype(jnp.bfloat16)
        wide = probs.astype(jnp.float32).reshape(parts, probs.shape[0] // parts, rows)
        mass = jnp.sum(wide, axis=1).astype(jnp.bfloat16)
        slots = jnp.dot(mass, user, preferred_element_type=jnp.float32)
        cluster[pl.ds(tile, 1)] += jnp.sum(slots, axis=0, keepdims=True)[None]
        term = lax.dot_general(probs, ads, (((0,), (0,)), ((), ())), preferred_element_type=jnp.float32)

        @pl.when(fresh)
        def _():
            acc[...] = term

        @pl.when(jnp.logical_not(fresh))
        def _():
            acc[...] += term

        @pl.when(last)
        def _():
            to = n % 2

            @pl.when(n >= 2)
            def _():
                put(0, to).wait()

            gout[to] = acc[...].astype(jnp.bfloat16)
            put(b, to).start()

        return n + last.astype(jnp.int32)

    n = lax.fori_loop(0, total, step, jnp.int32(0))
    for k in range(2):
        @pl.when(n > k)
        def _():
            put(0, k).wait()


def return_kernel(
    sizes, factor_scale, grads, cluster, factor, positive, user_grad, centroid_grad,
    own, sib, up_out, up_in, down_out, down_in, final, landed, parts,
    own_sem, sib_s, sib_r, up_s, up_r, down_s, down_r, fin_s, fin_r, cl_s, cl_r,
):
    nx, nz, ny, nc = sizes
    x, z, y, c = (lax.axis_index(a) for a in AXES)
    at_z = lambda d: lax.rem(z + d + nz, nz)
    above, below = {"z": at_z(1)}, {"z": at_z(-1)}
    sibling = {"c": 1 - c}
    rows, width = own.shape[2], own.shape[3]
    depth = width // nx
    steps = nz // 2
    pairs = [(dx, dy) for dx in range(nx) for dy in range(ny) if dx or dy]
    place = lambda dx, dy: (lax.rem(x + dx + nx, nx), lax.rem(y + dy + ny, ny))
    greet(
        [dict(zip(("x", "y"), place(dx, dy))) for dx, dy in pairs] + [above, below, sibling]
    )
    order = []
    for s in range(steps):
        order.append(steps - s)
        if s < steps - 1:
            order.append(s + 1 - steps)
    order.append(0)
    loads, crossing = {}, {}
    for k, d in enumerate(order):
        loads[d] = pltpu.make_async_copy(grads.at[at_z(d), c], own.at[k], own_sem.at[k])
        loads[d].start()
        crossing[d] = remote(grads.at[at_z(d), 1 - c], sib.at[k], sib_s, sib_r, k, sibling)
        crossing[d].start()
    columns = lambda i: pl.ds(pl.multiple_of(i * depth, depth), depth)
    clusters = []
    for k, (dx, dy) in enumerate(pairs):
        px, py = place(dx, dy)
        copy = remote(
            cluster.at[py, px], parts.at[k], cl_s, cl_r, k, {"x": px, "y": py}
        )
        copy.start()
        clusters.append(copy)
    index = {d: k for k, d in enumerate(order)}

    def both(d, i):
        return own[index[d], i].astype(jnp.float32) + sib[index[d], i].astype(jnp.float32)

    def ready(d):
        loads[d].wait()
        crossing[d].wait_recv()

    ups = lambda s, i: remote(up_out.at[s, i], up_in.at[s, i], up_s, up_r, 2 * s + i, above)
    downs = lambda s, i: remote(down_out.at[s, i], down_in.at[s, i], down_s, down_r, 2 * s + i, below)
    for s in range(steps):
        ready(steps - s)
        if s < steps - 1:
            ready(s + 1 - steps)
        for i in range(2):
            value = both(steps - s, i)
            if s > 0:
                ups(s - 1, i).wait_recv()
                value = value + up_in[s - 1, i].astype(jnp.float32)
            up_out[s, i] = value.astype(jnp.bfloat16)
            ups(s, i).start()
            if s < steps - 1:
                value = both(s + 1 - steps, i)
                if s > 0:
                    downs(s - 1, i).wait_recv()
                    value = value + down_in[s - 1, i].astype(jnp.float32)
                down_out[s, i] = value.astype(jnp.bfloat16)
                downs(s, i).start()
    ready(0)
    for i in range(2):
        downs(steps - 2, i).wait_recv()
        ups(steps - 1, i).wait_recv()
        value = (
            both(0, i)
            + up_in[steps - 1, i].astype(jnp.float32)
            + down_in[steps - 2, i].astype(jnp.float32)
        )
        wide = positive[i * rows:(i + 1) * rows].astype(jnp.float32)
        value = (value + as_column(factor[i, :, 0:rows]) * wide) * factor_scale
        for k in range(nx):
            final[k, i * rows:(i + 1) * rows] = value[:, k * depth:(k + 1) * depth]
    ends = []
    for d in range(1, nx):
        px = lax.rem(x + d, nx)
        copy = remote(final.at[px], landed.at[x], fin_s, fin_r, d, {"x": px})
        copy.start()
        ends.append(copy)
    whole = cluster[y, x]
    for k in range(len(pairs)):
        clusters[k].wait_recv()
        whole = whole + parts[k]
    centroid_grad[...] = whole * factor_scale
    user_grad[pl.ds(x, 1)] = final[pl.ds(x, 1)]
    for d in range(1, nx):
        frm = lax.rem(x - d + nx, nx)
        remote(landed.at[frm], landed.at[frm], fin_s, fin_r, d, {"x": frm}).wait_recv()
        user_grad[pl.ds(frm, 1)] = landed[pl.ds(frm, 1)]
    for copy in list(crossing.values()) + clusters + ends:
        copy.wait_send()
    for i in range(2):
        for s in range(steps):
            ups(s, i).wait_send()
        for s in range(steps - 1):
            downs(s, i).wait_send()


def params(identity=None, megabytes=48):
    return pltpu.CompilerParams(
        collective_id=identity,
        has_side_effects=identity is not None,
        vmem_limit_bytes=megabytes * 1024 * 1024,
    )


def local(
    sizes, user_rows, positive_rows, centroids, residuals, block_lists, block_lengths,
    cluster_counts, ad_counts,
):
    nx, nz, ny, nc = sizes
    x, z, y, c = (lax.axis_index(a) for a in AXES)
    nw, shards = nz * nc, nz * ny * nc
    per, width = centroids.shape
    quarter = residuals.shape[1]
    tile = ad_counts.shape[1]
    blocks, listed = block_lists.shape
    rows = user_rows.shape[0] // blocks
    half = per // 2
    scale = 1.0 / math.sqrt(width)
    sds = jax.ShapeDtypeStruct
    dma = pltpu.SemaphoreType.DMA
    bf16, f32 = jnp.bfloat16, jnp.float32

    ad_rows = (centroids[:, None, :] + residuals.astype(f32)).astype(bf16)
    weights = ad_counts.astype(f32)
    expected = (
        cluster_counts.astype(f32)[:, None] * weights / jnp.sum(weights, axis=1, keepdims=True)
    )
    shift = jnp.log(expected).astype(bf16)
    flat = block_lists.reshape(blocks * listed)
    used = jnp.arange(listed)[None, :] < block_lengths[:, None]
    name = jnp.where(used, jnp.arange(blocks)[:, None] + 1, 0).reshape(blocks * listed)
    match = flat[:, None] // per == jnp.arange(shards)[None, :]
    block_of = jnp.sum(jnp.where(match, name[:, None], 0), axis=0) - 1
    place_of = jnp.sum(jnp.where(match, (flat % per)[:, None], 0), axis=0)
    codes = jnp.stack([block_of, place_of]).astype(f32).astype(bf16)
    codes = jnp.pad(codes, ((0, CODE_ROWS - 2), (0, width - shards)))

    steps = nz // 2
    copies = 2 * (nx - 1) + (ny - 1) + 8 + 4 + 12 + 16 + (nz - 1) + nz
    mine = 2 * rows
    all_tiles, all_users, positives, all_shift = pl.pallas_call(
        functools.partial(gather_kernel, sizes),
        out_shape=(
            sds((ny, nx, 2, half, quarter, width), bf16),
            sds((nz, nc, mine + CODE_ROWS, width), bf16),
            sds((mine, width), bf16),
            sds((ny, per, tile), bf16),
        ),
        in_specs=[HBM] * 5,
        out_specs=[HBM] * 4,
        scratch_shapes=[dma((copies,)), dma((copies,)), dma((5,))],
        compiler_params=params(0, 4),
        name="gather",
    )(ad_rows.reshape(2, half, quarter, width), user_rows, positive_rows, codes, shift)

    picked = all_users[:, :, mine:mine + 2, :shards].reshape(nw, 2, nz, ny, nc)
    picked = lax.dynamic_index_in_dim(picked, z, 2, keepdims=False)
    picked = lax.dynamic_index_in_dim(picked, c, 3, keepdims=False)
    places = jnp.swapaxes(picked, 0, 1).reshape(2, nw * ny).astype(jnp.int32)
    flat_users = all_users.reshape(nw, mine + CODE_ROWS, width)
    flat_shift = all_shift.reshape(ny * per, tile)
    lanes = -(-rows // 128) * 128
    buffers = [pltpu.VMEM((2, rows, width), bf16), pltpu.VMEM((2, nx, quarter, width), bf16)]
    stats, entries, zeroed = pl.pallas_call(
        functools.partial(stats_kernel, half, scale),
        out_shape=(
            sds((2 * nw, 2, lanes), f32),
            sds((3, nw * ny + 8), jnp.int32),
            sds((2 * nw, rows, width), bf16),
        ),
        in_specs=[SMEM, SMEM, HBM, HBM, VMEM],
        out_specs=[VMEM, SMEM, HBM],
        scratch_shapes=buffers
        + [pltpu.VMEM((4, rows, width), bf16), dma((2,)), dma((2,)), dma((nw // 2,))],
        compiler_params=params(),
        name="stats",
    )(places, x.astype(jnp.int32).reshape(1), flat_users, all_tiles, flat_shift)

    own_users = lax.dynamic_index_in_dim(flat_users, z * nc + c, 0, keepdims=False)[:mine]
    totals, losses, factor = pl.pallas_call(
        functools.partial(total_kernel, sizes, scale),
        out_shape=(
            sds((nw, 2, 1, lanes), f32),
            sds((nx, 2, 1, lanes), f32),
            sds((2, 1, lanes), f32),
        ),
        in_specs=[VMEM] * 3,
        out_specs=[VMEM] * 3,
        scratch_shapes=[
            pltpu.VMEM((nw, 2, 2, lanes), f32),
            pltpu.VMEM((2, 1, lanes), f32),
            pltpu.VMEM((nw, 2, 1, lanes), f32),
            pltpu.VMEM((nx, 2, 1, lanes), f32),
        ]
        + [dma((nw,))] * 4
        + [dma((nx,))] * 2,
        compiler_params=params(1, 24),
        name="totals",
    )(stats.reshape(nw, 2, 2, lanes), own_users, positives)

    grads, cluster = pl.pallas_call(
        functools.partial(grads_kernel, half, scale),
        out_shape=(sds((2 * nw, rows, width), bf16), sds((ny * per, 1, width), f32)),
        in_specs=[SMEM, HBM, HBM, VMEM, VMEM, HBM],
        out_specs=[HBM, VMEM],
        input_output_aliases={5: 0},
        scratch_shapes=buffers
        + [
            pltpu.VMEM((rows, width), f32), pltpu.VMEM((2, rows, width), bf16),
            dma((2,)), dma((2,)), dma((2,)),
        ],
        compiler_params=params(),
        name="grads",
    )(entries, flat_users, all_tiles, flat_shift, totals.reshape(2 * nw, 1, lanes), zeroed)

    depth = width // nx
    cluster = jnp.swapaxes(cluster.reshape(ny, per, nx, depth), 1, 2)
    ring = lambda n: pltpu.VMEM((n, 2, rows, width), bf16)
    user_grad, centroid_grad = pl.pallas_call(
        functools.partial(return_kernel, sizes, LOSS_SCALE * scale),
        out_shape=(sds((nx, mine, depth), f32), sds((per, depth), f32)),
        in_specs=[HBM, VMEM, VMEM, VMEM],
        out_specs=[VMEM, VMEM],
        scratch_shapes=[
            ring(nz), ring(nz), ring(steps), ring(steps), ring(steps - 1), ring(steps - 1),
            pltpu.VMEM((nx, mine, depth), f32),
            pltpu.VMEM((nx, mine, depth), f32),
            pltpu.VMEM((nx * ny - 1, per, depth), f32),
            dma((nz,)), dma((nz,)), dma((nz,)),
            dma((2 * steps,)), dma((2 * steps,)), dma((2 * steps,)), dma((2 * steps,)),
            dma((nx,)), dma((nx,)), dma((nx * ny,)), dma((nx * ny,)),
        ],
        compiler_params=params(2, 48),
        name="return",
    )(grads.reshape(nz, nc, 2, rows, width), cluster, factor, positives)
    return (
        losses[:, :, 0, :rows].reshape(blocks * rows),
        user_grad.reshape(blocks * rows, depth),
        centroid_grad,
    )


def build(mesh, sizes):
    return jax.shard_map(
        functools.partial(local, sizes),
        mesh=mesh,
        in_specs=(
            P(("z", "y", "c"), "x"),
            P(("z", "y", "c"), "x"),
            P(("z", "y", "c"), None),
            P(("z", "y", "c"), "x", None),
            P(("z", "y", "c"), None),
            P(("z", "y", "c")),
            P(("z", "y", "c")),
            P(("z", "y", "c"), None),
        ),
        out_specs=(P(("z", "y", "c")), P(("z", "y", "c"), "x"), P(("z", "y", "c"), "x")),
        check_vma=False,
    )


def solution(mesh):
    sizes = (mesh.shape["tower"],) + SPLIT
    return build(Mesh(mesh.devices.reshape(sizes), AXES), sizes)
```

```python
import functools
import math

import jax
import jax.numpy as jnp
from jax import lax
from jax.experimental import pallas as pl
from jax.experimental.pallas import tpu as pltpu
from jax.sharding import Mesh, PartitionSpec as P

LOSS_SCALE = 16
AXES = ("x", "z", "y", "c")
SPLIT = (16, 4, 2)
LOW = -1e30
MESH = pl.DeviceIdType.MESH
HBM = pl.BlockSpec(memory_space=pl.ANY)
VMEM = pl.BlockSpec(memory_space=pltpu.VMEM)
SMEM = pl.BlockSpec(memory_space=pltpu.SMEM)
CODE_ROWS = 16
SLOTS = 8


def remote(src, dst, sends, recvs, k, where):
    return pltpu.make_async_remote_copy(
        src_ref=src,
        dst_ref=dst,
        send_sem=sends.at[k],
        recv_sem=recvs.at[k],
        device_id=where,
        device_id_type=MESH,
    )


def greet(peers):
    barrier = pltpu.get_barrier_semaphore()
    for where in peers:
        pl.semaphore_signal(barrier, inc=1, device_id=where, device_id_type=MESH)
    pl.semaphore_wait(barrier, len(peers))


def gather_kernel(
    sizes, tiles, users, positives, codes, shift,
    all_tiles, all_users, own_positives, all_shift, zeroed, sends, recvs, locals_, zbuf, zsem,
):
    nx, nz, ny, nc = sizes
    x, z, y, c = (lax.axis_index(a) for a in AXES)
    rows = users.shape[0] // nx
    depth = users.shape[1]
    half = tiles.shape[1]
    quarter = half // 2
    at_x = lambda d: lax.rem(x + d + nx, nx)
    at_y = lambda d: lax.rem(y + d + ny, ny)
    at_z = lambda d: lax.rem(z + d + nz, nz)
    to_x = lambda d: {"x": at_x(d)}
    to_y = lambda d: {"y": at_y(d)}
    to_z = lambda d: {"z": at_z(d)}
    sibling = {"c": 1 - c}

    greet(
        [to_x(d) for d in range(1, nx)]
        + [to_y(d) for d in range(1, ny)]
        + [to_z(1), to_z(-1), sibling]
    )

    count = [0]
    sent = []

    def push(src, dst, where, landing):
        k = count[0]
        count[0] += 1
        copy = remote(src, dst, sends, recvs, k, where)
        copy.start()
        sent.append(copy)
        return remote(landing, landing, sends, recvs, k, where)

    columns = lambda i: pl.ds(pl.multiple_of(i * depth, depth), depth)
    part = lambda i: pl.ds(pl.multiple_of(i * rows, rows), rows)
    home = all_users.at[z, c]

    def block(h, a, b):
        return all_tiles.at[at_y(b), at_x(a), h] if h == 0 else all_tiles.at[at_y(a), at_x(b), h]

    first = (to_x, to_y)
    second = (to_y, to_x)
    lower, upper = pl.ds(0, quarter), pl.ds(quarter, quarter)

    arrivals = []
    for d in range(1, nx):
        arrivals.append(
            push(
                users.at[part(at_x(d))], home.at[pl.ds(0, rows), columns(x)], to_x(d),
                home.at[pl.ds(0, rows), columns(at_x(-d))],
            )
        )
    p1 = {}
    for h in (0, 1):
        for d in (1, -1):
            p1[h, d] = push(tiles.at[h], block(h, 0, 0), first[h](d), block(h, -d, 0))
    own = [
        pltpu.make_async_copy(users.at[part(x)], home.at[pl.ds(0, rows), columns(x)], locals_.at[0]),
        pltpu.make_async_copy(codes, home.at[pl.ds(rows, CODE_ROWS)], locals_.at[1]),
        pltpu.make_async_copy(tiles, all_tiles.at[y, x], locals_.at[2]),
        pltpu.make_async_copy(shift, all_shift.at[y], locals_.at[3]),
        pltpu.make_async_copy(positives.at[part(x)], own_positives.at[:, columns(x)], locals_.at[4]),
    ]
    for copy in own:
        copy.start()
    zbuf[...] = jnp.zeros_like(zbuf)
    piece = zbuf.shape[0]
    zeros = [
        pltpu.make_async_copy(zbuf, zeroed.at[pl.ds(k * piece, piece)], zsem.at[k])
        for k in range(zeroed.shape[0] // piece)
    ]
    for copy in zeros:
        copy.start()
    late = []
    p2 = {}
    for h in (0, 1):
        for d in (1, -1):
            p2[h, 0, d] = push(tiles.at[h], block(h, 0, 0), second[h](d), block(h, 0, -d))
    for d in range(1, nx):
        late.append(
            push(
                positives.at[part(at_x(d))], own_positives.at[:, columns(x)], to_x(d),
                own_positives.at[:, columns(at_x(-d))],
            )
        )
    for d in range(1, ny):
        late.append(push(shift, all_shift.at[y], to_y(d), all_shift.at[at_y(-d)]))

    for arrival in arrivals:
        arrival.wait_recv()
    own[0].wait()
    own[1].wait()

    chunk = lambda d: all_users.at[at_z(d), c]
    other = lambda d: all_users.at[at_z(d), 1 - c]
    steps = nz // 2
    up, down = {}, {}

    def ring(s):
        if s > 0:
            up[s - 1].wait_recv()
            if s - 1 in down:
                down[s - 1].wait_recv()
        if s < steps:
            up[s] = push(chunk(-s), chunk(-s), to_z(1), chunk(-s - 1))
        if s < steps - 1:
            down[s] = push(chunk(s), chunk(s), to_z(-1), chunk(s + 1))
        late.append(push(chunk(-s), chunk(-s), sibling, other(-s)))
        if 0 < s < steps:
            late.append(push(chunk(s), chunk(s), sibling, other(s)))

    turns = list(range(steps + 1))
    ring(turns.pop(0))
    while len(turns) > steps - 3 and turns:
        ring(turns.pop(0))

    for h in (0, 1):
        for d in (1, -1):
            p1[h, d].wait_recv()
    q = {}
    for h in (0, 1):
        for d in (1, -1):
            cut = lower if d == 1 else upper
            q[h, d] = push(
                block(h, -d, 0).at[cut], block(h, -d, 0).at[cut], first[h](d), block(h, -2 * d, 0).at[cut]
            )
    for j in (1, -1):
        for h in (0, 1):
            for d in (1, -1):
                p2[h, j, d] = push(block(h, j, 0), block(h, j, 0), second[h](d), block(h, j, -d))
    if turns:
        ring(turns.pop(0))

    def onward(j):
        for h in (0, 1):
            for d in (1, -1):
                p2[h, j, d].wait_recv()
                cut = lower if d == 1 else upper
                late.append(
                    push(
                        block(h, j, -d).at[cut], block(h, j, -d).at[cut], second[h](d),
                        block(h, j, -2 * d).at[cut],
                    )
                )

    onward(0)
    for h in (0, 1):
        for d in (1, -1):
            q[h, d].wait_recv()
    for h in (0, 1):
        for d in (1, -1):
            p2[h, 2, d] = push(block(h, 2, 0), block(h, 2, 0), second[h](d), block(h, 2, -d))
    if turns:
        ring(turns.pop(0))
    onward(1)
    while turns:
        ring(turns.pop(0))
    onward(-1)
    onward(2)
    for arrival in late:
        arrival.wait_recv()
    for copy in own[2:] + zeros:
        copy.wait()
    for copy in sent:
        copy.wait_send()
    assert count[0] == sends.shape[0], count[0]


def fetch(users, tiles, list_ref, ubuf, tbuf, usem, tsem, half, e, slot):
    b, tile = list_ref[0, e], list_ref[1, e]
    per = 2 * half
    yp, cl = tile // per, tile % per
    w, i = b // 2, b % 2
    rows = ubuf.shape[1]
    return (
        pltpu.make_async_copy(
            users.at[w, pl.ds(pl.multiple_of(i * rows, rows), rows)], ubuf.at[slot], usem.at[slot]
        ),
        pltpu.make_async_copy(
            tiles.at[yp, :, cl // half, cl % half], tbuf.at[slot], tsem.at[slot]
        ),
    )


def scores(ubuf, tbuf, shift_ref, slot, tile, scale):
    user = ubuf[slot]
    ads = tbuf[slot].reshape(tbuf.shape[1] * tbuf.shape[2], tbuf.shape[3])
    pick = lax.broadcasted_iota(jnp.int32, (shift_ref.shape[0], user.shape[0]), 0) == tile
    shift = lax.dot_general(
        shift_ref[...], pick.astype(jnp.float32).astype(jnp.bfloat16), (((0,), (0,)), ((), ())),
        preferred_element_type=jnp.float32,
    )
    raw = lax.dot_general(ads, user, (((1,), (1,)), ((), ())), preferred_element_type=jnp.float32)
    return user, ads, raw * scale - shift


def stats_kernel(
    half, scale, codes, mine, users, tiles, shift_ref,
    stats, list_ref, ubuf, tbuf, usem, tsem,
):
    nw = users.shape[0]
    ny = tiles.shape[0]
    rows = ubuf.shape[1]
    t = mine[0]
    def gather(w, n):
        for i in range(2):
            for yp in range(ny):
                list_ref[0, n] = w * 2 + i
                list_ref[1, n] = yp * (2 * half) + codes[1, w * ny + yp]
                n = n + (codes[0, w * ny + yp] == 2 * t + i).astype(jnp.int32)
        return n

    total = lax.fori_loop(0, nw, gather, jnp.int32(0))
    list_ref[0, total] = -1
    list_ref[1, total] = 0
    list_ref[2, 0] = total
    stats[:, :, :, 0] = jnp.full(stats.shape[:3] + stats.shape[4:], LOW, jnp.float32)
    stats[:, :, :, 1] = jnp.zeros(stats.shape[:3] + stats.shape[4:], jnp.float32)
    get = functools.partial(fetch, users, tiles, list_ref, ubuf, tbuf, usem, tsem, half)

    ahead = ubuf.shape[0] - 1
    for k in range(ahead):
        @pl.when(total > k)
        def _():
            for copy in get(k, k):
                copy.start()

    def step(e, _):
        slot = e % (ahead + 1)

        @pl.when(e + ahead < total)
        def _():
            for copy in get(e + ahead, (e + ahead) % (ahead + 1)):
                copy.start()

        for copy in get(e, slot):
            copy.wait()
        b, tile = list_ref[0, e], list_ref[1, e]
        _, _, logits = scores(ubuf, tbuf, shift_ref, slot, tile, scale)
        at = ((b // 2) % 2, b // 4, b % 2)
        before = stats[at + (0, slice(None), pl.ds(0, rows))]
        held = stats[at + (1, slice(None), pl.ds(0, rows))]
        top = jnp.maximum(before, jnp.max(logits, axis=0, keepdims=True))
        stats[at + (0, slice(None), pl.ds(0, rows))] = top
        stats[at + (1, slice(None), pl.ds(0, rows))] = held * jnp.exp(before - top) + jnp.sum(
            jnp.exp(logits - top), axis=0, keepdims=True
        )
        return 0

    lax.fori_loop(0, total, step, 0)


def as_row(column):
    n = column.shape[0]
    eye = lax.broadcasted_iota(jnp.int32, (n, n), 0) == lax.broadcasted_iota(jnp.int32, (n, n), 1)
    return jnp.sum(jnp.where(eye, column, 0.0), axis=0, keepdims=True)


def as_column(row):
    n = row.shape[1]
    eye = lax.broadcasted_iota(jnp.int32, (n, n), 0) == lax.broadcasted_iota(jnp.int32, (n, n), 1)
    return jnp.sum(jnp.where(eye, row, 0.0), axis=1, keepdims=True)


def total_kernel(
    sizes, scale, stats, user, positive, totals, losses, factor,
    across, joined, came, mine, got, beside, lost, s0, r0, s1, r1, s2, r2, s3, r3,
):
    nx, nz, ny, nc = sizes
    x, z, y, c = (lax.axis_index(a) for a in AXES)
    rows = user.shape[0] // 2
    barrier = pltpu.get_barrier_semaphore()
    sibling = {"c": 1 - c}

    def there(d):
        p = lax.rem(z + d, nz)
        return p, {"z": p}

    def hello(d, _):
        pl.semaphore_signal(barrier, inc=1, device_id=there(d)[1], device_id_type=MESH)
        return 0

    pl.semaphore_signal(barrier, inc=1, device_id=sibling, device_id_type=MESH)
    lax.fori_loop(1, nz, hello, 0)
    for d in range(1, nx):
        pl.semaphore_signal(
            barrier, inc=1, device_id={"x": lax.rem(x + d, nx)}, device_id_type=MESH
        )
    pl.semaphore_wait(barrier, nz - 1 + nx - 1 + 1)

    over = remote(stats.at[1 - c], across, s0, r0, 0, sibling)
    over.start()
    dots = []
    for i in range(2):
        u = user[i * rows:(i + 1) * rows].astype(jnp.float32)
        v = positive[i * rows:(i + 1) * rows].astype(jnp.float32)
        dots.append(as_row(jnp.sum(u * v, axis=1, keepdims=True)) * scale)
    over.wait_recv()
    here = stats[pl.ds(c, 1)][0]
    there_ = across[...]
    tops = jnp.maximum(here[:, :, 0], there_[:, :, 0])
    joined[:, :, 0] = tops
    joined[:, :, 1] = here[:, :, 1] * jnp.exp(here[:, :, 0] - tops) + there_[:, :, 1] * jnp.exp(
        there_[:, :, 0] - tops
    )

    def out(d, _):
        p, where = there(d)
        remote(joined.at[p], came.at[z], s1, r1, d, where).start()
        return 0

    lax.fori_loop(1, nz, out, 0)
    mine[...] = jnp.zeros_like(mine)
    factor[...] = jnp.zeros_like(factor)
    lost[pl.ds(x, 1)] = jnp.zeros((1,) + lost.shape[1:], jnp.float32)
    came[pl.ds(z, 1)] = joined[pl.ds(z, 1)]

    def landed(d, _):
        p, where = there(nz - d)
        remote(came.at[p], came.at[p], s1, r1, d, where).wait_recv()
        return 0

    lax.fori_loop(1, nz, landed, 0)
    for i in range(2):
        tops = came[:, i, 0, :, 0:rows]
        sums = came[:, i, 1, :, 0:rows]
        ceiling = jnp.maximum(jnp.max(tops, axis=0), dots[i])
        whole = jnp.sum(sums * jnp.exp(tops - ceiling[None]), axis=0) + jnp.exp(dots[i] - ceiling)
        log_total = ceiling + jnp.log(whole)
        mine[i, :, 0:rows] = log_total
        lost[pl.ds(x, 1), i, :, 0:rows] = (log_total - dots[i])[None]
        factor[i, :, 0:rows] = jnp.exp(dots[i] - log_total) - 1.0

    def back(d, _):
        _, where = there(d)
        remote(mine, got.at[z], s2, r2, d, where).start()
        return 0

    lax.fori_loop(1, nz, back, 0)
    for d in range(1, nx):
        remote(lost.at[x], lost.at[x], s3, r3, d, {"x": lax.rem(x + d, nx)}).start()
    got[pl.ds(z, 1)] = mine[...][None]

    def done(d, _):
        p, where = there(nz - d)
        remote(got.at[p], got.at[p], s2, r2, d, where).wait_recv()
        return 0

    lax.fori_loop(1, nz, done, 0)
    give = remote(got, beside, s0, r0, 1, sibling)
    give.start()
    totals[pl.ds(c, 1)] = got[...][None]
    for d in range(1, nx):
        frm = lax.rem(x - d + nx, nx)
        remote(lost.at[frm], lost.at[frm], s3, r3, d, {"x": frm}).wait_recv()
    losses[...] = lost[...]
    give.wait_recv()
    totals[pl.ds(1 - c, 1)] = beside[...][None]

    def left(d, _):
        p, where = there(d)
        remote(joined.at[p], came.at[z], s1, r1, d, where).wait_send()
        remote(mine, got.at[z], s2, r2, d, where).wait_send()
        return 0

    lax.fori_loop(1, nz, left, 0)
    for d in range(1, nx):
        remote(lost.at[x], lost.at[x], s3, r3, d, {"x": lax.rem(x + d, nx)}).wait_send()
    over.wait_send()
    give.wait_send()


def grads_kernel(
    half, scale, list_ref, users, tiles, shift_ref, totals, _zeroed,
    grads, cluster, ubuf, tbuf, usem, tsem, acc, gout, gsem,
):
    rows = ubuf.shape[1]
    parts = tbuf.shape[1]
    total = list_ref[2, 0]
    cluster[...] = jnp.zeros_like(cluster)
    get = functools.partial(fetch, users, tiles, list_ref, ubuf, tbuf, usem, tsem, half)

    ahead = ubuf.shape[0] - 1
    for k in range(ahead):
        @pl.when(total > k)
        def _():
            for copy in get(k, k):
                copy.start()

    def put(b, slot):
        return pltpu.make_async_copy(gout.at[slot], grads.at[b], gsem.at[slot])

    def step(e, n):
        slot = e % (ahead + 1)

        @pl.when(e + ahead < total)
        def _():
            for copy in get(e + ahead, (e + ahead) % (ahead + 1)):
                copy.start()

        for copy in get(e, slot):
            copy.wait()
        b, tile = list_ref[0, e], list_ref[1, e]
        fresh = jnp.logical_or(e == 0, list_ref[0, jnp.maximum(e - 1, 0)] != b)
        last = list_ref[0, e + 1] != b
        user, ads, logits = scores(ubuf, tbuf, shift_ref, slot, tile, scale)
        probs = jnp.exp(logits - totals[(b // 2) % 2, b // 4, b % 2, :, 0:rows]).astype(jnp.bfloat16)
        wide = probs.astype(jnp.float32).reshape(parts, probs.shape[0] // parts, rows)
        mass = jnp.sum(wide, axis=1).astype(jnp.bfloat16)
        slots = jnp.dot(mass, user, preferred_element_type=jnp.float32)
        cluster[pl.ds(tile, 1)] += jnp.sum(slots, axis=0, keepdims=True)[None]
        term = lax.dot_general(probs, ads, (((0,), (0,)), ((), ())), preferred_element_type=jnp.float32)

        @pl.when(fresh)
        def _():
            acc[...] = term

        @pl.when(jnp.logical_not(fresh))
        def _():
            acc[...] += term

        @pl.when(last)
        def _():
            to = n % 2

            @pl.when(n >= 2)
            def _():
                put(0, to).wait()

            gout[to] = acc[...].astype(jnp.bfloat16)
            put(b, to).start()

        return n + last.astype(jnp.int32)

    n = lax.fori_loop(0, total, step, jnp.int32(0))
    for k in range(2):
        @pl.when(n > k)
        def _():
            put(0, k).wait()


def return_kernel(
    sizes, factor_scale, grads, cluster, factor, positive, user_grad, centroid_grad,
    own, sib, long_out, long_in, short_out, short_in, final, landed, parts,
    own_sem, sib_s, sib_r, long_s, long_r, short_s, short_r, fin_s, fin_r, cl_s, cl_r,
):
    nx, nz, ny, nc = sizes
    x, z, y, c = (lax.axis_index(a) for a in AXES)
    at_z = lambda d: lax.rem(z + d + nz, nz)
    above, below = {"z": at_z(1)}, {"z": at_z(-1)}
    sibling = {"c": 1 - c}
    rows, width = own.shape[2], own.shape[3]
    depth = width // nx
    steps = nz // 2
    pairs = [(dx, dy) for dx in range(nx) for dy in range(ny) if dx or dy]
    place = lambda dx, dy: (lax.rem(x + dx + nx, nx), lax.rem(y + dy + ny, ny))
    greet(
        [dict(zip(("x", "y"), place(dx, dy))) for dx, dy in pairs] + [above, below, sibling]
    )
    order = []
    for s in range(steps):
        order.append(steps - s)
        if s > 0:
            order.append(s - steps)
    order.append(0)
    loads, crossing = {}, {}
    for k, d in enumerate(order):
        loads[d] = pltpu.make_async_copy(grads.at[at_z(d), c], own.at[k], own_sem.at[k])
        loads[d].start()
        crossing[d] = remote(grads.at[at_z(d), 1 - c], sib.at[k], sib_s, sib_r, k, sibling)
        crossing[d].start()
    columns = lambda i: pl.ds(pl.multiple_of(i * depth, depth), depth)
    clusters = []
    for k, (dx, dy) in enumerate(pairs):
        px, py = place(dx, dy)
        copy = remote(
            cluster.at[py, px], parts.at[k], cl_s, cl_r, k, {"x": px, "y": py}
        )
        copy.start()
        clusters.append(copy)
    index = {d: k for k, d in enumerate(order)}

    def both(d, i):
        return own[index[d], i].astype(jnp.float32) + sib[index[d], i].astype(jnp.float32)

    def ready(d):
        loads[d].wait()
        crossing[d].wait_recv()

    away = lambda i: above if i == 0 else below
    back = lambda i: below if i == 0 else above
    longs = lambda s, i: remote(
        long_out.at[s, i], long_in.at[s, i], long_s, long_r, 2 * s + i, away(i)
    )
    shorts = lambda s, i: remote(
        short_out.at[s - 1, i], short_in.at[s - 1, i], short_s, short_r, 2 * s + i, back(i)
    )
    for s in range(steps):
        ready(steps - s)
        if s > 0:
            ready(s - steps)
        for i in range(2):
            sign = 1 if i == 0 else -1
            value = both(sign * (steps - s) if s > 0 else steps, i)
            if s > 0:
                longs(s - 1, i).wait_recv()
                value = value + long_in[s - 1, i].astype(jnp.float32)
            long_out[s, i] = value.astype(jnp.bfloat16)
            longs(s, i).start()
            if s > 0:
                value = both(sign * (s - steps), i)
                if s > 1:
                    shorts(s - 1, i).wait_recv()
                    value = value + short_in[s - 2, i].astype(jnp.float32)
                short_out[s - 1, i] = value.astype(jnp.bfloat16)
                shorts(s, i).start()
    ready(0)
    for i in range(2):
        shorts(steps - 1, i).wait_recv()
        longs(steps - 1, i).wait_recv()
        value = (
            both(0, i)
            + long_in[steps - 1, i].astype(jnp.float32)
            + short_in[steps - 2, i].astype(jnp.float32)
        )
        wide = positive[i * rows:(i + 1) * rows].astype(jnp.float32)
        value = (value + as_column(factor[i, :, 0:rows]) * wide) * factor_scale
        for k in range(nx):
            final[k, i * rows:(i + 1) * rows] = value[:, k * depth:(k + 1) * depth]
    ends = []
    for d in range(1, nx):
        px = lax.rem(x + d, nx)
        copy = remote(final.at[px], landed.at[x], fin_s, fin_r, d, {"x": px})
        copy.start()
        ends.append(copy)
    whole = cluster[y, x]
    for k in range(len(pairs)):
        clusters[k].wait_recv()
        whole = whole + parts[k]
    centroid_grad[...] = whole * factor_scale
    user_grad[pl.ds(x, 1)] = final[pl.ds(x, 1)]
    for d in range(1, nx):
        frm = lax.rem(x - d + nx, nx)
        remote(landed.at[frm], landed.at[frm], fin_s, fin_r, d, {"x": frm}).wait_recv()
        user_grad[pl.ds(frm, 1)] = landed[pl.ds(frm, 1)]
    for copy in list(crossing.values()) + clusters + ends:
        copy.wait_send()
    for i in range(2):
        for s in range(steps):
            longs(s, i).wait_send()
        for s in range(1, steps):
            shorts(s, i).wait_send()


def params(identity=None, megabytes=48):
    return pltpu.CompilerParams(
        collective_id=identity,
        has_side_effects=identity is not None,
        vmem_limit_bytes=megabytes * 1024 * 1024,
    )


def lanes_of(rows):
    return -(-rows // 128) * 128


def buffers_of(rows, width, nx, quarter):
    return [
        pltpu.VMEM((SLOTS, rows, width), jnp.bfloat16),
        pltpu.VMEM((SLOTS, nx, quarter, width), jnp.bfloat16),
        pltpu.SemaphoreType.DMA((SLOTS,)),
        pltpu.SemaphoreType.DMA((SLOTS,)),
    ]


def stats_call(nw, ny, half, scale, rows, width, nx, quarter):
    sds = jax.ShapeDtypeStruct
    return pl.pallas_call(
        functools.partial(stats_kernel, half, scale),
        out_shape=(
            sds((2, nw // 2, 2, 2, 1, lanes_of(rows)), jnp.float32),
            sds((3, nw * ny + 8), jnp.int32),
        ),
        in_specs=[SMEM, SMEM, HBM, HBM, VMEM],
        out_specs=[VMEM, SMEM],
        scratch_shapes=buffers_of(rows, width, nx, quarter),
        compiler_params=params(None, 58),
        name="stats",
    )


def grads_call(nw, ny, half, scale, rows, width, nx, quarter):
    sds = jax.ShapeDtypeStruct
    return pl.pallas_call(
        functools.partial(grads_kernel, half, scale),
        out_shape=(
            sds((2 * nw, rows, width), jnp.bfloat16),
            sds((2 * ny * half, 1, width), jnp.float32),
        ),
        in_specs=[SMEM, HBM, HBM, VMEM, VMEM, HBM],
        out_specs=[HBM, VMEM],
        input_output_aliases={5: 0},
        scratch_shapes=buffers_of(rows, width, nx, quarter)
        + [
            pltpu.VMEM((rows, width), jnp.float32),
            pltpu.VMEM((2, rows, width), jnp.bfloat16),
            pltpu.SemaphoreType.DMA((2,)),
        ],
        compiler_params=params(None, 58),
        name="grads",
    )


def totals_call(sizes, scale, rows):
    nx, nz, ny, nc = sizes
    lanes = lanes_of(rows)
    sds = lambda *shape: jax.ShapeDtypeStruct(shape, jnp.float32)
    buffer = lambda *shape: pltpu.VMEM(shape, jnp.float32)
    dma = pltpu.SemaphoreType.DMA
    return pl.pallas_call(
        functools.partial(total_kernel, sizes, scale),
        out_shape=(
            sds(nc, nz, 2, 1, lanes),
            sds(nx, 2, 1, lanes),
            sds(2, 1, lanes),
        ),
        in_specs=[VMEM] * 3,
        out_specs=[VMEM] * 3,
        scratch_shapes=[
            buffer(nz, 2, 2, 1, lanes),
            buffer(nz, 2, 2, 1, lanes),
            buffer(nz, 2, 2, 1, lanes),
            buffer(2, 1, lanes),
            buffer(nz, 2, 1, lanes),
            buffer(nz, 2, 1, lanes),
            buffer(nx, 2, 1, lanes),
        ]
        + [dma((2,))] * 2
        + [dma((nz,))] * 4
        + [dma((nx,))] * 2,
        compiler_params=params(1, 24),
        name="totals",
    )


def local(
    sizes, user_rows, positive_rows, centroids, residuals, block_lists, block_lengths,
    cluster_counts, ad_counts,
):
    nx, nz, ny, nc = sizes
    x, z, y, c = (lax.axis_index(a) for a in AXES)
    nw, shards = nz * nc, nz * ny * nc
    per, width = centroids.shape
    quarter = residuals.shape[1]
    tile = ad_counts.shape[1]
    blocks, listed = block_lists.shape
    rows = user_rows.shape[0] // blocks
    half = per // 2
    scale = 1.0 / math.sqrt(width)
    sds = jax.ShapeDtypeStruct
    dma = pltpu.SemaphoreType.DMA
    bf16, f32 = jnp.bfloat16, jnp.float32

    ad_rows = (centroids[:, None, :] + residuals.astype(f32)).astype(bf16)
    weights = ad_counts.astype(f32)
    expected = (
        cluster_counts.astype(f32)[:, None] * weights / jnp.sum(weights, axis=1, keepdims=True)
    )
    shift = jnp.log(expected).astype(bf16)
    flat = block_lists.reshape(blocks * listed)
    used = jnp.arange(listed)[None, :] < block_lengths[:, None]
    name = jnp.where(used, jnp.arange(blocks)[:, None] + 1, 0).reshape(blocks * listed)
    match = flat[:, None] // per == jnp.arange(shards)[None, :]
    block_of = jnp.sum(jnp.where(match, name[:, None], 0), axis=0) - 1
    place_of = jnp.sum(jnp.where(match, (flat % per)[:, None], 0), axis=0)
    codes = jnp.stack([block_of, place_of]).astype(f32).astype(bf16)
    codes = jnp.pad(codes, ((0, CODE_ROWS - 2), (0, width - shards)))

    steps = nz // 2
    copies = 2 * (nx - 1) + (ny - 1) + 8 + 4 + 12 + 16 + (nz - 1) + nz
    mine = 2 * rows
    all_tiles, all_users, positives, all_shift, zeroed = pl.pallas_call(
        functools.partial(gather_kernel, sizes),
        out_shape=(
            sds((ny, nx, 2, half, quarter, width), bf16),
            sds((nz, nc, mine + CODE_ROWS, width), bf16),
            sds((mine, width), bf16),
            sds((ny, per, tile), bf16),
            sds((2 * nw, rows, width), bf16),
        ),
        in_specs=[HBM] * 5,
        out_specs=[HBM] * 5,
        scratch_shapes=[
            dma((copies,)), dma((copies,)), dma((5,)),
            pltpu.VMEM((4, rows, width), bf16), dma((nw // 2,)),
        ],
        compiler_params=params(0, 58),
        name="gather",
    )(ad_rows.reshape(2, half, quarter, width), user_rows, positive_rows, codes, shift)

    picked = all_users[:, :, mine:mine + 2, :shards].reshape(nw, 2, nz, ny, nc)
    picked = lax.dynamic_index_in_dim(picked, z, 2, keepdims=False)
    picked = lax.dynamic_index_in_dim(picked, c, 3, keepdims=False)
    places = jnp.swapaxes(picked, 0, 1).reshape(2, nw * ny).astype(jnp.int32)
    flat_users = all_users.reshape(nw, mine + CODE_ROWS, width)
    flat_shift = all_shift.reshape(ny * per, tile)
    stats, entries = stats_call(nw, ny, half, scale, rows, width, nx, quarter)(
        places, x.astype(jnp.int32).reshape(1), flat_users, all_tiles, flat_shift
    )

    own_users = lax.dynamic_index_in_dim(flat_users, z * nc + c, 0, keepdims=False)[:mine]
    totals, losses, factor = totals_call(sizes, scale, rows)(stats, own_users, positives)

    grads, cluster = grads_call(nw, ny, half, scale, rows, width, nx, quarter)(
        entries, flat_users, all_tiles, flat_shift, totals, zeroed
    )

    depth = width // nx
    cluster = jnp.swapaxes(cluster.reshape(ny, per, nx, depth), 1, 2)
    ring = lambda n: pltpu.VMEM((n, 2, rows, width), bf16)
    user_grad, centroid_grad = pl.pallas_call(
        functools.partial(return_kernel, sizes, LOSS_SCALE * scale),
        out_shape=(sds((nx, mine, depth), f32), sds((per, depth), f32)),
        in_specs=[HBM, VMEM, VMEM, VMEM],
        out_specs=[VMEM, VMEM],
        scratch_shapes=[
            ring(nz), ring(nz), ring(steps), ring(steps), ring(steps - 1), ring(steps - 1),
            pltpu.VMEM((nx, mine, depth), f32),
            pltpu.VMEM((nx, mine, depth), f32),
            pltpu.VMEM((nx * ny - 1, per, depth), f32),
            dma((nz,)), dma((nz,)), dma((nz,)),
            dma((2 * steps,)), dma((2 * steps,)), dma((2 * steps,)), dma((2 * steps,)),
            dma((nx,)), dma((nx,)), dma((nx * ny,)), dma((nx * ny,)),
        ],
        compiler_params=params(2, 48),
        name="return",
    )(grads.reshape(nz, nc, 2, rows, width), cluster, factor, positives)
    return (
        losses[:, :, 0, :rows].reshape(blocks * rows),
        user_grad.reshape(blocks * rows, depth),
        centroid_grad,
    )


def build(mesh, sizes):
    return jax.shard_map(
        functools.partial(local, sizes),
        mesh=mesh,
        in_specs=(
            P(("z", "y", "c"), "x"),
            P(("z", "y", "c"), "x"),
            P(("z", "y", "c"), None),
            P(("z", "y", "c"), "x", None),
            P(("z", "y", "c"), None),
            P(("z", "y", "c")),
            P(("z", "y", "c")),
            P(("z", "y", "c"), None),
        ),
        out_specs=(P(("z", "y", "c")), P(("z", "y", "c"), "x"), P(("z", "y", "c"), "x")),
        check_vma=False,
    )


def solution(mesh):
    sizes = (mesh.shape["tower"],) + SPLIT
    return build(Mesh(mesh.devices.reshape(sizes), AXES), sizes)
```

```python
import functools
import math

import jax
import jax.numpy as jnp
from jax import lax
from jax.experimental import pallas as pl
from jax.experimental.pallas import tpu as pltpu
from jax.sharding import Mesh, PartitionSpec as P

LOSS_SCALE = 16
AXES = ("x", "z", "y", "c")
SPLIT = (16, 4, 2)
LOW = -1e30
LOG2E = math.log2(math.e)
LN2 = math.log(2.0)
MESH = pl.DeviceIdType.MESH
HBM = pl.BlockSpec(memory_space=pl.ANY)
VMEM = pl.BlockSpec(memory_space=pltpu.VMEM)
SMEM = pl.BlockSpec(memory_space=pltpu.SMEM)
CODE_ROWS = 16
SLOTS = 8
MASS_ROWS = 8


def remote(src, dst, sends, recvs, k, where):
    return pltpu.make_async_remote_copy(
        src_ref=src,
        dst_ref=dst,
        send_sem=sends.at[k],
        recv_sem=recvs.at[k],
        device_id=where,
        device_id_type=MESH,
    )


def greet(peers):
    barrier = pltpu.get_barrier_semaphore()
    for where in peers:
        pl.semaphore_signal(barrier, inc=1, device_id=where, device_id_type=MESH)
    pl.semaphore_wait(barrier, len(peers))


def gather_kernel(
    sizes, tiles, users, positives, codes, shift,
    all_tiles, all_users, own_positives, all_shift, zeroed, sends, recvs, locals_, zbuf, zsem,
):
    nx, nz, ny, nc = sizes
    x, z, y, c = (lax.axis_index(a) for a in AXES)
    rows = users.shape[0] // nx
    depth = users.shape[1]
    half = tiles.shape[1]
    quarter = half // 2
    at_x = lambda d: lax.rem(x + d + nx, nx)
    at_y = lambda d: lax.rem(y + d + ny, ny)
    at_z = lambda d: lax.rem(z + d + nz, nz)
    to_x = lambda d: {"x": at_x(d)}
    to_y = lambda d: {"y": at_y(d)}
    to_z = lambda d: {"z": at_z(d)}
    sibling = {"c": 1 - c}

    greet(
        [to_x(d) for d in range(1, nx)]
        + [to_y(d) for d in range(1, ny)]
        + [to_z(1), to_z(-1), sibling]
    )

    count = [0]
    sent = []

    def push(src, dst, where, landing):
        k = count[0]
        count[0] += 1
        copy = remote(src, dst, sends, recvs, k, where)
        copy.start()
        sent.append(copy)
        return remote(landing, landing, sends, recvs, k, where)

    columns = lambda i: pl.ds(pl.multiple_of(i * depth, depth), depth)
    part = lambda i: pl.ds(pl.multiple_of(i * rows, rows), rows)
    home = all_users.at[z, c]

    def block(h, a, b):
        return all_tiles.at[at_y(b), at_x(a), h] if h == 0 else all_tiles.at[at_y(a), at_x(b), h]

    first = (to_x, to_y)
    second = (to_y, to_x)
    lower, upper = pl.ds(0, quarter), pl.ds(quarter, quarter)

    arrivals = []
    for d in range(1, nx):
        arrivals.append(
            push(
                users.at[part(at_x(d))], home.at[pl.ds(0, rows), columns(x)], to_x(d),
                home.at[pl.ds(0, rows), columns(at_x(-d))],
            )
        )
    p1 = {}
    for h in (0, 1):
        for d in (1, -1):
            p1[h, d] = push(tiles.at[h], block(h, 0, 0), first[h](d), block(h, -d, 0))
    own = [
        pltpu.make_async_copy(users.at[part(x)], home.at[pl.ds(0, rows), columns(x)], locals_.at[0]),
        pltpu.make_async_copy(codes, home.at[pl.ds(rows, CODE_ROWS)], locals_.at[1]),
        pltpu.make_async_copy(tiles, all_tiles.at[y, x], locals_.at[2]),
        pltpu.make_async_copy(shift, all_shift.at[y], locals_.at[3]),
        pltpu.make_async_copy(positives.at[part(x)], own_positives.at[:, columns(x)], locals_.at[4]),
    ]
    for copy in own:
        copy.start()
    zbuf[...] = jnp.zeros_like(zbuf)
    piece = zbuf.shape[0]
    zeros = [
        pltpu.make_async_copy(zbuf, zeroed.at[pl.ds(k * piece, piece)], zsem.at[k])
        for k in range(zeroed.shape[0] // piece)
    ]
    for copy in zeros:
        copy.start()
    late = []
    p2 = {}
    for h in (0, 1):
        for d in (1, -1):
            p2[h, 0, d] = push(tiles.at[h], block(h, 0, 0), second[h](d), block(h, 0, -d))
    for d in range(1, nx):
        late.append(
            push(
                positives.at[part(at_x(d))], own_positives.at[:, columns(x)], to_x(d),
                own_positives.at[:, columns(at_x(-d))],
            )
        )
    for d in range(1, ny):
        late.append(push(shift, all_shift.at[y], to_y(d), all_shift.at[at_y(-d)]))

    for arrival in arrivals:
        arrival.wait_recv()
    own[0].wait()
    own[1].wait()

    chunk = lambda d: all_users.at[at_z(d), c]
    other = lambda d: all_users.at[at_z(d), 1 - c]
    steps = nz // 2
    up, down = {}, {}

    def ring(s):
        if s > 0:
            up[s - 1].wait_recv()
            if s - 1 in down:
                down[s - 1].wait_recv()
        if s < steps:
            up[s] = push(chunk(-s), chunk(-s), to_z(1), chunk(-s - 1))
        if s < steps - 1:
            down[s] = push(chunk(s), chunk(s), to_z(-1), chunk(s + 1))
        late.append(push(chunk(-s), chunk(-s), sibling, other(-s)))
        if 0 < s < steps:
            late.append(push(chunk(s), chunk(s), sibling, other(s)))

    turns = list(range(steps + 1))
    ring(turns.pop(0))
    while len(turns) > steps - 3 and turns:
        ring(turns.pop(0))

    for h in (0, 1):
        for d in (1, -1):
            p1[h, d].wait_recv()
    q = {}
    for h in (0, 1):
        for d in (1, -1):
            cut = lower if d == 1 else upper
            q[h, d] = push(
                block(h, -d, 0).at[cut], block(h, -d, 0).at[cut], first[h](d), block(h, -2 * d, 0).at[cut]
            )
    for j in (1, -1):
        for h in (0, 1):
            for d in (1, -1):
                p2[h, j, d] = push(block(h, j, 0), block(h, j, 0), second[h](d), block(h, j, -d))
    if turns:
        ring(turns.pop(0))

    def onward(j):
        for h in (0, 1):
            for d in (1, -1):
                p2[h, j, d].wait_recv()
                cut = lower if d == 1 else upper
                late.append(
                    push(
                        block(h, j, -d).at[cut], block(h, j, -d).at[cut], second[h](d),
                        block(h, j, -2 * d).at[cut],
                    )
                )

    onward(0)
    for h in (0, 1):
        for d in (1, -1):
            q[h, d].wait_recv()
    for h in (0, 1):
        for d in (1, -1):
            p2[h, 2, d] = push(block(h, 2, 0), block(h, 2, 0), second[h](d), block(h, 2, -d))
    if turns:
        ring(turns.pop(0))
    onward(1)
    while turns:
        ring(turns.pop(0))
    onward(-1)
    onward(2)
    for arrival in late:
        arrival.wait_recv()
    for copy in own[2:] + zeros:
        copy.wait()
    for copy in sent:
        copy.wait_send()
    assert count[0] == sends.shape[0], count[0]


def fetch(users, tiles, list_ref, ubuf, tbuf, usem, tsem, half, e, slot):
    b, tile = list_ref[0, e], list_ref[1, e]
    per = 2 * half
    yp, cl = tile // per, tile % per
    w, i = b // 2, b % 2
    rows = ubuf.shape[1]
    return (
        pltpu.make_async_copy(
            users.at[w, pl.ds(pl.multiple_of(i * rows, rows), rows)], ubuf.at[slot], usem.at[slot]
        ),
        pltpu.make_async_copy(
            tiles.at[yp, :, cl // half, cl % half], tbuf.at[slot], tsem.at[slot]
        ),
    )


def scores(ubuf, tbuf, shift_ref, slot, tile, scale):
    user = ubuf[slot]
    ads = tbuf[slot].reshape(tbuf.shape[1] * tbuf.shape[2], tbuf.shape[3])
    pick = lax.broadcasted_iota(jnp.int32, (shift_ref.shape[0], user.shape[0]), 0) == tile
    shift = lax.dot_general(
        shift_ref[...], pick.astype(jnp.float32).astype(jnp.bfloat16), (((0,), (0,)), ((), ())),
        preferred_element_type=jnp.float32,
    )
    raw = lax.dot_general(ads, user, (((1,), (1,)), ((), ())), preferred_element_type=jnp.float32)
    return user, ads, raw * scale - shift


def flash_kernel(
    half, scale, codes, mine, users, tiles, shift_ref, _zeroed,
    stats, masses, grads, list_ref, ubuf, tbuf, usem, tsem, acc, gout, gsem,
):
    nw = users.shape[0]
    ny = tiles.shape[0]
    rows = ubuf.shape[1]
    parts = tbuf.shape[1]
    t = mine[0]

    def gather(w, n):
        for i in range(2):
            for yp in range(ny):
                list_ref[0, n] = w * 2 + i
                list_ref[1, n] = yp * (2 * half) + codes[1, w * ny + yp]
                n = n + (codes[0, w * ny + yp] == 2 * t + i).astype(jnp.int32)
        return n

    total = lax.fori_loop(0, nw, gather, jnp.int32(0))
    list_ref[0, total] = -1
    list_ref[1, total] = 0
    get = functools.partial(fetch, users, tiles, list_ref, ubuf, tbuf, usem, tsem, half)
    ahead = ubuf.shape[0] - 1
    for k in range(ahead):
        @pl.when(total > k)
        def _():
            for copy in get(k, k):
                copy.start()

    stats[:, :, :, 0] = jnp.full(stats.shape[:3] + stats.shape[4:], LOW, jnp.float32)
    stats[:, :, :, 1] = jnp.zeros(stats.shape[:3] + stats.shape[4:], jnp.float32)
    masses[...] = jnp.zeros_like(masses)

    def put(b, slot):
        return pltpu.make_async_copy(gout.at[slot], grads.at[b], gsem.at[slot])

    def step(e, n):
        slot = e % (ahead + 1)

        @pl.when(e + ahead < total)
        def _():
            for copy in get(e + ahead, (e + ahead) % (ahead + 1)):
                copy.start()

        for copy in get(e, slot):
            copy.wait()
        b, tile = list_ref[0, e], list_ref[1, e]
        fresh = jnp.logical_or(e == 0, list_ref[0, jnp.maximum(e - 1, 0)] != b)
        last = list_ref[0, e + 1] != b
        at = ((b // 2) % 2, b // 4, b % 2)
        user, ads, logits = scores(ubuf, tbuf, shift_ref, slot, tile, scale)
        logits = logits * LOG2E
        before = stats[at + (0, slice(None), pl.ds(0, rows))]
        held = stats[at + (1, slice(None), pl.ds(0, rows))]
        top = jnp.maximum(before, jnp.ceil(jnp.max(logits, axis=0, keepdims=True)))
        carry = jnp.exp2(before - top)
        terms = jnp.exp2(logits - top)
        stats[at + (0, slice(None), pl.ds(0, rows))] = top
        stats[at + (1, slice(None), pl.ds(0, rows))] = held * carry + jnp.sum(
            terms, axis=0, keepdims=True
        )
        probs = terms.astype(jnp.bfloat16)
        wide = probs.astype(jnp.float32).reshape(parts, probs.shape[0] // parts, rows)
        mass = jnp.sum(wide, axis=1)
        term = lax.dot_general(probs, ads, (((0,), (0,)), ((), ())), preferred_element_type=jnp.float32)

        @pl.when(fresh)
        def _():
            acc[...] = term

        @pl.when(jnp.logical_not(fresh))
        def _():
            acc[...] = acc[...] * as_column(carry) + term
            masses[b, :, :, 0:rows] = masses[b, :, :, 0:rows] * carry[None]

        masses[b, tile // (2 * half), 0:parts, 0:rows] = mass

        @pl.when(last)
        def _():
            to = n % 2

            @pl.when(n >= 2)
            def _():
                put(0, to).wait()

            gout[to] = acc[...].astype(jnp.bfloat16)
            put(b, to).start()

        return n + last.astype(jnp.int32)

    n = lax.fori_loop(0, total, step, jnp.int32(0))
    for k in range(2):
        @pl.when(n > k)
        def _():
            put(0, k).wait()


def as_row(column):
    n = column.shape[0]
    eye = lax.broadcasted_iota(jnp.int32, (n, n), 0) == lax.broadcasted_iota(jnp.int32, (n, n), 1)
    return jnp.sum(jnp.where(eye, column, 0.0), axis=0, keepdims=True)


def as_column(row):
    n = row.shape[1]
    eye = lax.broadcasted_iota(jnp.int32, (n, n), 0) == lax.broadcasted_iota(jnp.int32, (n, n), 1)
    return jnp.sum(jnp.where(eye, row, 0.0), axis=1, keepdims=True)


def diagonal(row):
    n = row.shape[1]
    eye = lax.broadcasted_iota(jnp.int32, (n, n), 0) == lax.broadcasted_iota(jnp.int32, (n, n), 1)
    return jnp.where(eye, row, 0.0).astype(jnp.bfloat16)


def return_kernel(
    sizes, scale, factor_scale, grads, stats, masses, names, users, positive,
    user_grad, centroid_grad, losses,
    own, sib, long_out, long_in, short_out, short_in,
    klong_out, klong_in, kshort_out, kshort_in,
    final, landed, parts, cluster, everyone, terms,
    across, joined, came, mine, got, beside, lost, factor,
    own_sem, sib_s, sib_r, long_s, long_r, short_s, short_r,
    kl_s, kl_r, ks_s, ks_r, fin_s, fin_r, cl_s, cl_r,
    s0, r0, s1, r1, s2, r2, s3, r3, usem,
):
    nx, nz, ny, nc = sizes
    x, z, y, c = (lax.axis_index(a) for a in AXES)
    at_z = lambda d: lax.rem(z + d + nz, nz)
    above, below = {"z": at_z(1)}, {"z": at_z(-1)}
    sibling = {"c": 1 - c}
    rows, width = own.shape[2], own.shape[3]
    per, depth = cluster.shape[2], cluster.shape[3]
    steps = nz // 2
    pairs = [(dx, dy) for dx in range(nx) for dy in range(ny) if dx or dy]
    place = lambda dx, dy: (lax.rem(x + dx + nx, nx), lax.rem(y + dy + ny, ny))
    greet(
        [{"z": at_z(d)} for d in range(1, nz)]
        + [dict(zip(("x", "y"), place(dx, dy))) for dx, dy in pairs]
        + [sibling]
    )
    over = remote(stats.at[1 - c], across, s0, r0, 0, sibling)
    over.start()
    order = []
    for s in range(steps):
        order.append(steps - s)
        if s > 0:
            order.append(s - steps)
    order.append(0)
    index = {d: k for k, d in enumerate(order)}
    loads = [
        pltpu.make_async_copy(grads.at[at_z(d), c], own.at[k], own_sem.at[k])
        for k, d in enumerate(order)
    ]
    crossing = [
        remote(grads.at[at_z(d), 1 - c], sib.at[k], sib_s, sib_r, k, sibling)
        for k, d in enumerate(order)
    ]

    def begin(ks):
        for k in ks:
            loads[k].start()
            crossing[k].start()

    def ready(d):
        loads[index[d]].wait()
        crossing[index[d]].wait_recv()

    def merged(d, i, extra):
        k = index[d]
        items = [
            (stats[c, at_z(d), i, 0, :, pl.ds(0, rows)], own[k, i]),
            (across[at_z(d), i, 0, :, pl.ds(0, rows)], sib[k, i]),
        ] + extra
        top = items[0][0]
        for level, _ in items[1:]:
            top = jnp.maximum(top, level)
        whole = 0.0
        for level, value in items:
            whole = whole + jnp.dot(
                diagonal(jnp.exp2(level - top)), value, preferred_element_type=jnp.float32
            )
        return whole, top

    away = lambda i: above if i == 0 else below
    back = lambda i: below if i == 0 else above
    longs = lambda s, i: (
        remote(long_out.at[s, i], long_in.at[s, i], long_s, long_r, 2 * s + i, away(i)),
        remote(klong_out.at[s, i], klong_in.at[s, i], kl_s, kl_r, 2 * s + i, away(i)),
    )
    shorts = lambda s, i: (
        remote(short_out.at[s - 1, i], short_in.at[s - 1, i], short_s, short_r, 2 * s + i, back(i)),
        remote(kshort_out.at[s - 1, i], kshort_in.at[s - 1, i], ks_s, ks_r, 2 * s + i, back(i)),
    )

    def arrive(copies):
        for copy in copies:
            copy.wait_recv()

    def send_stats():
        begin(range(min(3, nz), nz))
        pltpu.make_async_copy(users.at[:, pl.ds(0, 2 * rows)], everyone, usem.at[0]).start()
        here = stats[pl.ds(c, 1)][0]
        there = across[...]
        tops = jnp.maximum(here[:, :, 0], there[:, :, 0])
        joined[:, :, 0] = tops
        joined[:, :, 1] = here[:, :, 1] * jnp.exp2(here[:, :, 0] - tops) + there[
            :, :, 1
        ] * jnp.exp2(there[:, :, 0] - tops)

        def out(d, _):
            p = lax.rem(z + d, nz)
            remote(joined.at[p], came.at[z], s1, r1, d, {"z": p}).start()
            return 0

        lax.fori_loop(1, nz, out, 0)
        came[pl.ds(z, 1)] = joined[pl.ds(z, 1)]
        mine[...] = jnp.zeros_like(mine)
        factor[...] = jnp.zeros_like(factor)
        lost[pl.ds(x, 1)] = jnp.zeros((1,) + lost.shape[1:], jnp.float32)

    def total():
        pltpu.make_async_copy(users.at[:, pl.ds(0, 2 * rows)], everyone, usem.at[0]).wait()

        def come(d, _):
            p = lax.rem(z + nz - d, nz)
            remote(came.at[p], came.at[p], s1, r1, d, {"z": p}).wait_recv()
            return 0

        lax.fori_loop(1, nz, come, 0)
        for i in range(2):
            u = everyone[z * nc + c, i * rows:(i + 1) * rows].astype(jnp.float32)
            v = positive[i * rows:(i + 1) * rows].astype(jnp.float32)
            dot = as_row(jnp.sum(u * v, axis=1, keepdims=True)) * (scale * LOG2E)
            tops = came[:, i, 0, :, 0:rows]
            sums = came[:, i, 1, :, 0:rows]
            ceiling = jnp.maximum(jnp.max(tops, axis=0), dot)
            whole = jnp.log(
                jnp.sum(sums * jnp.exp2(tops - ceiling[None]), axis=0) + jnp.exp2(dot - ceiling)
            )
            log_total = ceiling + whole * LOG2E
            mine[i, :, 0:rows] = log_total
            lost[pl.ds(x, 1), i, :, 0:rows] = (whole + (ceiling - dot) * LN2)[None]
            factor[i, :, 0:rows] = jnp.exp2(dot - log_total) - 1.0

        def give(d, _):
            p = lax.rem(z + d, nz)
            remote(mine, got.at[z], s2, r2, d, {"z": p}).start()
            return 0

        lax.fori_loop(1, nz, give, 0)
        for d in range(1, nx):
            remote(lost.at[x], lost.at[x], s3, r3, d, {"x": lax.rem(x + d, nx)}).start()
        got[pl.ds(z, 1)] = mine[...][None]

    beside_copy = remote(got, beside, s0, r0, 1, sibling)

    def spread():
        def done(d, _):
            p = lax.rem(z + nz - d, nz)
            remote(got.at[p], got.at[p], s2, r2, d, {"z": p}).wait_recv()
            return 0

        lax.fori_loop(1, nz, done, 0)
        beside_copy.start()

    def weigh(core, logs, first, count):
        def one(k, _):
            w = k * nc + core
            both = 0.0
            for i in range(2):
                level = stats[core, k, i, 0, :, pl.ds(0, rows)]
                share = jnp.exp2(level - logs[k, i, :, pl.ds(0, rows)])
                mass = masses[2 * w + i, :, :, pl.ds(0, rows)] * share[None]
                mass = mass.reshape(mass.shape[0] * mass.shape[1], rows).astype(jnp.bfloat16)
                both = both + jnp.dot(
                    mass, everyone[w, i * rows:(i + 1) * rows], preferred_element_type=jnp.float32
                )
            terms[w] = both
            return 0

        lax.fori_loop(first, first + count, one, 0)

    def cluster_copy(k):
        px, py = place(*pairs[k])
        return remote(cluster.at[py, px], parts.at[k], cl_s, cl_r, k, {"x": px, "y": py})

    def clusters():
        flat = terms[...].reshape(terms.shape[0] * terms.shape[1], width)
        pick = lax.broadcasted_iota(jnp.int32, (ny * per, flat.shape[0]), 0) == names[...]
        summed = jnp.dot(
            pick.astype(jnp.float32), flat, precision=lax.Precision.HIGHEST,
            preferred_element_type=jnp.float32,
        )
        for py in range(ny):
            for px in range(nx):
                cluster[py, px] = summed[py * per:(py + 1) * per, px * depth:(px + 1) * depth]
        for k in range(len(pairs)):
            cluster_copy(k).start()

    part = nz // 2
    tasks = [
        (0, send_stats),
        (2, total),
        (4, spread),
        (4, lambda: weigh(c, got, 0, part)),
        (5, lambda: weigh(c, got, part, nz - part)),
        (6, beside_copy.wait_recv),
        (6, lambda: weigh(1 - c, beside, 0, part)),
        (7, lambda: weigh(1 - c, beside, part, nz - part)),
        (7, clusters),
    ]

    begin(range(min(3, nz)))
    for levels in (klong_out, kshort_out):
        levels[...] = jnp.zeros_like(levels)
    over.wait_recv()
    for s in range(steps):
        ready(steps - s)
        if s > 0:
            ready(s - steps)
        for i in range(2):
            sign = 1 if i == 0 else -1
            extra = []
            if s > 0:
                arrive(longs(s - 1, i))
                extra = [(klong_in[s - 1, i, :, 0:rows], long_in[s - 1, i])]
            value, top = merged(sign * (steps - s) if s > 0 else steps, i, extra)
            long_out[s, i] = value.astype(jnp.bfloat16)
            klong_out[s, i, :, 0:rows] = top
            for copy in longs(s, i):
                copy.start()
            if s > 0:
                extra = []
                if s > 1:
                    arrive(shorts(s - 1, i))
                    extra = [(kshort_in[s - 2, i, :, 0:rows], short_in[s - 2, i])]
                value, top = merged(sign * (s - steps), i, extra)
                short_out[s - 1, i] = value.astype(jnp.bfloat16)
                kshort_out[s - 1, i, :, 0:rows] = top
                for copy in shorts(s, i):
                    copy.start()
        while tasks and (tasks[0][0] == s or s == steps - 1):
            tasks.pop(0)[1]()
    ready(0)
    for i in range(2):
        arrive(shorts(steps - 1, i))
        arrive(longs(steps - 1, i))
        value, top = merged(
            0, i,
            [
                (klong_in[steps - 1, i, :, 0:rows], long_in[steps - 1, i]),
                (kshort_in[steps - 2, i, :, 0:rows], short_in[steps - 2, i]),
            ],
        )
        wide = positive[i * rows:(i + 1) * rows].astype(jnp.float32)
        value = value * as_column(jnp.exp2(top - mine[i, :, 0:rows]))
        value = (value + as_column(factor[i, :, 0:rows]) * wide) * factor_scale
        for k in range(nx):
            final[k, i * rows:(i + 1) * rows] = value[:, k * depth:(k + 1) * depth]
    ends = []
    for d in range(1, nx):
        px = lax.rem(x + d, nx)
        copy = remote(final.at[px], landed.at[x], fin_s, fin_r, d, {"x": px})
        copy.start()
        ends.append(copy)
    whole = cluster[y, x]
    for k in range(len(pairs)):
        cluster_copy(k).wait_recv()
        whole = whole + parts[k]
    centroid_grad[...] = whole * factor_scale
    user_grad[pl.ds(x, 1)] = final[pl.ds(x, 1)]
    for d in range(1, nx):
        frm = lax.rem(x - d + nx, nx)
        remote(lost.at[frm], lost.at[frm], s3, r3, d, {"x": frm}).wait_recv()
    losses[...] = lost[...]
    for d in range(1, nx):
        frm = lax.rem(x - d + nx, nx)
        remote(landed.at[frm], landed.at[frm], fin_s, fin_r, d, {"x": frm}).wait_recv()
        user_grad[pl.ds(frm, 1)] = landed[pl.ds(frm, 1)]

    for copy in crossing + [cluster_copy(k) for k in range(len(pairs))] + ends + [over, beside_copy]:
        copy.wait_send()
    for i in range(2):
        for s in range(steps):
            for copy in longs(s, i) + (shorts(s, i) if s > 0 else ()):
                copy.wait_send()

    def left(d, _):
        p = lax.rem(z + d, nz)
        remote(joined.at[p], came.at[z], s1, r1, d, {"z": p}).wait_send()
        remote(mine, got.at[z], s2, r2, d, {"z": p}).wait_send()
        return 0

    lax.fori_loop(1, nz, left, 0)
    for d in range(1, nx):
        remote(lost.at[x], lost.at[x], s3, r3, d, {"x": lax.rem(x + d, nx)}).wait_send()


def params(identity=None, megabytes=48):
    return pltpu.CompilerParams(
        collective_id=identity,
        has_side_effects=identity is not None,
        vmem_limit_bytes=megabytes * 1024 * 1024,
    )


def lanes_of(rows):
    return -(-rows // 128) * 128


def buffers_of(rows, width, nx, quarter):
    return [
        pltpu.VMEM((SLOTS, rows, width), jnp.bfloat16),
        pltpu.VMEM((SLOTS, nx, quarter, width), jnp.bfloat16),
        pltpu.SemaphoreType.DMA((SLOTS,)),
        pltpu.SemaphoreType.DMA((SLOTS,)),
    ]


def flash_call(nw, ny, half, scale, rows, width, nx, quarter):
    sds = jax.ShapeDtypeStruct
    lanes = lanes_of(rows)
    return pl.pallas_call(
        functools.partial(flash_kernel, half, scale),
        out_shape=(
            sds((2, nw // 2, 2, 2, 1, lanes), jnp.float32),
            sds((2 * nw, ny, MASS_ROWS, lanes), jnp.float32),
            sds((2 * nw, rows, width), jnp.bfloat16),
        ),
        in_specs=[SMEM, SMEM, HBM, HBM, VMEM, HBM],
        out_specs=[VMEM, VMEM, HBM],
        input_output_aliases={5: 2},
        scratch_shapes=[pltpu.SMEM((2, nw * ny + 8), jnp.int32)]
        + buffers_of(rows, width, nx, quarter)
        + [
            pltpu.VMEM((rows, width), jnp.float32),
            pltpu.VMEM((2, rows, width), jnp.bfloat16),
            pltpu.SemaphoreType.DMA((2,)),
        ],
        compiler_params=params(None, 58),
        name="flash",
    )


def return_call(sizes, scale, rows, width, per):
    nx, nz, ny, nc = sizes
    lanes, depth, steps, nw = lanes_of(rows), width // nx, nz // 2, nz * nc
    sds = lambda *shape: jax.ShapeDtypeStruct(shape, jnp.float32)
    buffer = lambda *shape: pltpu.VMEM(shape, jnp.float32)
    ring = lambda n: pltpu.VMEM((n, 2, rows, width), jnp.bfloat16)
    dma = pltpu.SemaphoreType.DMA
    return pl.pallas_call(
        functools.partial(return_kernel, sizes, scale, LOSS_SCALE * scale),
        out_shape=(sds(nx, 2 * rows, depth), sds(per, depth), sds(nx, 2, 1, lanes)),
        in_specs=[HBM, VMEM, VMEM, VMEM, HBM, VMEM],
        out_specs=[VMEM] * 3,
        scratch_shapes=[
            ring(nz), ring(nz), ring(steps), ring(steps), ring(steps - 1), ring(steps - 1),
            buffer(steps, 2, 1, lanes), buffer(steps, 2, 1, lanes),
            buffer(steps - 1, 2, 1, lanes), buffer(steps - 1, 2, 1, lanes),
            buffer(nx, 2 * rows, depth), buffer(nx, 2 * rows, depth),
            buffer(max(nx * ny - 1, 1), per, depth), buffer(ny, nx, per, depth),
            pltpu.VMEM((nw, 2 * rows, width), jnp.bfloat16),
            buffer(nw, ny * MASS_ROWS, width),
            buffer(nz, 2, 2, 1, lanes), buffer(nz, 2, 2, 1, lanes), buffer(nz, 2, 2, 1, lanes),
            buffer(2, 1, lanes), buffer(nz, 2, 1, lanes), buffer(nz, 2, 1, lanes),
            buffer(nx, 2, 1, lanes), buffer(2, 1, lanes),
            dma((nz,)), dma((nz,)), dma((nz,)),
        ]
        + [dma((2 * steps,))] * 8
        + [dma((nx,))] * 2
        + [dma((nx * ny,))] * 2
        + [dma((2,))] * 2
        + [dma((nz,))] * 4
        + [dma((nx,))] * 2
        + [dma((1,))],
        compiler_params=params(2, 58),
        name="return",
    )


def local(
    sizes, user_rows, positive_rows, centroids, residuals, block_lists, block_lengths,
    cluster_counts, ad_counts,
):
    nx, nz, ny, nc = sizes
    x, z, y, c = (lax.axis_index(a) for a in AXES)
    nw, shards = nz * nc, nz * ny * nc
    per, width = centroids.shape
    quarter = residuals.shape[1]
    tile = ad_counts.shape[1]
    blocks, listed = block_lists.shape
    rows = user_rows.shape[0] // blocks
    half = per // 2
    scale = 1.0 / math.sqrt(width)
    sds = jax.ShapeDtypeStruct
    dma = pltpu.SemaphoreType.DMA
    bf16, f32 = jnp.bfloat16, jnp.float32

    ad_rows = (centroids[:, None, :] + residuals.astype(f32)).astype(bf16)
    weights = ad_counts.astype(f32)
    expected = (
        cluster_counts.astype(f32)[:, None] * weights / jnp.sum(weights, axis=1, keepdims=True)
    )
    shift = jnp.log(expected).astype(bf16)
    flat = block_lists.reshape(blocks * listed)
    used = jnp.arange(listed)[None, :] < block_lengths[:, None]
    name = jnp.where(used, jnp.arange(blocks)[:, None] + 1, 0).reshape(blocks * listed)
    match = flat[:, None] // per == jnp.arange(shards)[None, :]
    block_of = jnp.sum(jnp.where(match, name[:, None], 0), axis=0) - 1
    place_of = jnp.sum(jnp.where(match, (flat % per)[:, None], 0), axis=0)
    codes = jnp.stack([block_of, place_of]).astype(f32).astype(bf16)
    codes = jnp.pad(codes, ((0, CODE_ROWS - 2), (0, width - shards)))

    steps = nz // 2
    copies = 2 * (nx - 1) + (ny - 1) + 8 + 4 + 12 + 16 + (nz - 1) + nz
    mine = 2 * rows
    all_tiles, all_users, positives, all_shift, zeroed = pl.pallas_call(
        functools.partial(gather_kernel, sizes),
        out_shape=(
            sds((ny, nx, 2, half, quarter, width), bf16),
            sds((nz, nc, mine + CODE_ROWS, width), bf16),
            sds((mine, width), bf16),
            sds((ny, per, tile), bf16),
            sds((2 * nw, rows, width), bf16),
        ),
        in_specs=[HBM] * 5,
        out_specs=[HBM] * 5,
        scratch_shapes=[
            dma((copies,)), dma((copies,)), dma((5,)),
            pltpu.VMEM((4, rows, width), bf16), dma((nw // 2,)),
        ],
        compiler_params=params(0, 58),
        name="gather",
    )(ad_rows.reshape(2, half, quarter, width), user_rows, positive_rows, codes, shift)

    picked = all_users[:, :, mine:mine + 2, :shards].reshape(nw, 2, nz, ny, nc)
    picked = lax.dynamic_index_in_dim(picked, z, 2, keepdims=False)
    picked = lax.dynamic_index_in_dim(picked, c, 3, keepdims=False)
    places = jnp.swapaxes(picked, 0, 1).reshape(2, nw * ny).astype(jnp.int32)
    flat_users = all_users.reshape(nw, mine + CODE_ROWS, width)
    flat_shift = all_shift.reshape(ny * per, tile)
    stats, masses, grads = flash_call(nw, ny, half, scale, rows, width, nx, quarter)(
        places, x.astype(jnp.int32).reshape(1), flat_users, all_tiles, flat_shift, zeroed
    )
    depth = width // nx
    names = places[1].reshape(nw, ny) + per * jnp.arange(ny)[None, :]
    names = jnp.repeat(names.reshape(1, nw * ny), MASS_ROWS, axis=1)
    user_grad, centroid_grad, losses = return_call(sizes, scale, rows, width, per)(
        grads.reshape(nz, nc, 2, rows, width), stats, masses, names, flat_users, positives
    )
    return (
        losses[:, :, 0, :rows].reshape(blocks * rows),
        user_grad.reshape(blocks * rows, depth),
        centroid_grad,
    )


def build(mesh, sizes):
    return jax.shard_map(
        functools.partial(local, sizes),
        mesh=mesh,
        in_specs=(
            P(("z", "y", "c"), "x"),
            P(("z", "y", "c"), "x"),
            P(("z", "y", "c"), None),
            P(("z", "y", "c"), "x", None),
            P(("z", "y", "c"), None),
            P(("z", "y", "c")),
            P(("z", "y", "c")),
            P(("z", "y", "c"), None),
        ),
        out_specs=(P(("z", "y", "c")), P(("z", "y", "c"), "x"), P(("z", "y", "c"), "x")),
        check_vma=False,
    )


def solution(mesh):
    sizes = (mesh.shape["tower"],) + SPLIT
    return build(Mesh(mesh.devices.reshape(sizes), AXES), sizes)
```

```python
import functools
import math

import jax
import jax.numpy as jnp
from jax import lax
from jax.experimental import pallas as pl
from jax.experimental.pallas import tpu as pltpu
from jax.sharding import Mesh, PartitionSpec as P

LOSS_SCALE = 16
AXES = ("x", "z", "y", "c")
SPLIT = (16, 4, 2)
LOW = -1e30
LOG2E = math.log2(math.e)
LN2 = math.log(2.0)
MESH = pl.DeviceIdType.MESH
HBM = pl.BlockSpec(memory_space=pl.ANY)
VMEM = pl.BlockSpec(memory_space=pltpu.VMEM)
SMEM = pl.BlockSpec(memory_space=pltpu.SMEM)
CODE_ROWS = 16
SLOTS = 8
MASS_ROWS = 8


def remote(src, dst, sends, recvs, k, where):
    return pltpu.make_async_remote_copy(
        src_ref=src,
        dst_ref=dst,
        send_sem=sends.at[k],
        recv_sem=recvs.at[k],
        device_id=where,
        device_id_type=MESH,
    )


def greet(peers):
    barrier = pltpu.get_barrier_semaphore()
    for where in peers:
        pl.semaphore_signal(barrier, inc=1, device_id=where, device_id_type=MESH)
    pl.semaphore_wait(barrier, len(peers))


def gather_kernel(
    sizes, tiles, users, codes, shift,
    all_tiles, all_users, all_shift, zeroed, sends, recvs, locals_, zbuf, zsem,
):
    nx, nz, ny, nc = sizes
    x, z, y, c = (lax.axis_index(a) for a in AXES)
    rows = users.shape[0] // nx
    depth = users.shape[1]
    half = tiles.shape[1]
    quarter = half // 2
    at_x = lambda d: lax.rem(x + d + nx, nx)
    at_y = lambda d: lax.rem(y + d + ny, ny)
    at_z = lambda d: lax.rem(z + d + nz, nz)
    to_x = lambda d: {"x": at_x(d)}
    to_y = lambda d: {"y": at_y(d)}
    to_z = lambda d: {"z": at_z(d)}
    sibling = {"c": 1 - c}

    greet(
        [to_x(d) for d in range(1, nx)]
        + [to_y(d) for d in range(1, ny)]
        + [to_z(1), to_z(-1), sibling]
    )

    count = [0]
    sent = []

    def push(src, dst, where, landing):
        k = count[0]
        count[0] += 1
        copy = remote(src, dst, sends, recvs, k, where)
        copy.start()
        sent.append(copy)
        return remote(landing, landing, sends, recvs, k, where)

    columns = lambda i: pl.ds(pl.multiple_of(i * depth, depth), depth)
    part = lambda i: pl.ds(pl.multiple_of(i * rows, rows), rows)
    home = all_users.at[z, c]

    def block(h, a, b):
        return all_tiles.at[at_y(b), at_x(a), h] if h == 0 else all_tiles.at[at_y(a), at_x(b), h]

    first = (to_x, to_y)
    second = (to_y, to_x)
    lower, upper = pl.ds(0, quarter), pl.ds(quarter, quarter)

    arrivals = []
    for d in range(1, nx):
        arrivals.append(
            push(
                users.at[part(at_x(d))], home.at[pl.ds(0, rows), columns(x)], to_x(d),
                home.at[pl.ds(0, rows), columns(at_x(-d))],
            )
        )
    p1 = {}
    for h in (0, 1):
        for d in (1, -1):
            p1[h, d] = push(tiles.at[h], block(h, 0, 0), first[h](d), block(h, -d, 0))
    own = [
        pltpu.make_async_copy(users.at[part(x)], home.at[pl.ds(0, rows), columns(x)], locals_.at[0]),
        pltpu.make_async_copy(codes, home.at[pl.ds(rows, CODE_ROWS)], locals_.at[1]),
        pltpu.make_async_copy(tiles, all_tiles.at[y, x], locals_.at[2]),
        pltpu.make_async_copy(shift, all_shift.at[y], locals_.at[3]),
    ]
    for copy in own:
        copy.start()
    zbuf[...] = jnp.zeros_like(zbuf)
    piece = zbuf.shape[0]
    zeros = [
        pltpu.make_async_copy(zbuf, zeroed.at[pl.ds(k * piece, piece)], zsem.at[k])
        for k in range(zeroed.shape[0] // piece)
    ]
    for copy in zeros:
        copy.start()
    late = []
    p2 = {}
    for h in (0, 1):
        for d in (1, -1):
            p2[h, 0, d] = push(tiles.at[h], block(h, 0, 0), second[h](d), block(h, 0, -d))
    for d in range(1, ny):
        late.append(push(shift, all_shift.at[y], to_y(d), all_shift.at[at_y(-d)]))

    for arrival in arrivals:
        arrival.wait_recv()
    own[0].wait()
    own[1].wait()

    chunk = lambda d: all_users.at[at_z(d), c]
    other = lambda d: all_users.at[at_z(d), 1 - c]
    steps = nz // 2
    up, down = {}, {}

    def ring(s):
        if s > 0:
            up[s - 1].wait_recv()
            if s - 1 in down:
                down[s - 1].wait_recv()
        if s < steps:
            up[s] = push(chunk(-s), chunk(-s), to_z(1), chunk(-s - 1))
        if s < steps - 1:
            down[s] = push(chunk(s), chunk(s), to_z(-1), chunk(s + 1))
        late.append(push(chunk(-s), chunk(-s), sibling, other(-s)))
        if 0 < s < steps:
            late.append(push(chunk(s), chunk(s), sibling, other(s)))

    turns = list(range(steps + 1))
    ring(turns.pop(0))
    while len(turns) > steps - 3 and turns:
        ring(turns.pop(0))

    for h in (0, 1):
        for d in (1, -1):
            p1[h, d].wait_recv()
    q = {}
    for h in (0, 1):
        for d in (1, -1):
            cut = lower if d == 1 else upper
            q[h, d] = push(
                block(h, -d, 0).at[cut], block(h, -d, 0).at[cut], first[h](d), block(h, -2 * d, 0).at[cut]
            )
    for j in (1, -1):
        for h in (0, 1):
            for d in (1, -1):
                p2[h, j, d] = push(block(h, j, 0), block(h, j, 0), second[h](d), block(h, j, -d))
    if turns:
        ring(turns.pop(0))

    def onward(j):
        for h in (0, 1):
            for d in (1, -1):
                p2[h, j, d].wait_recv()
                cut = lower if d == 1 else upper
                late.append(
                    push(
                        block(h, j, -d).at[cut], block(h, j, -d).at[cut], second[h](d),
                        block(h, j, -2 * d).at[cut],
                    )
                )

    onward(0)
    for h in (0, 1):
        for d in (1, -1):
            q[h, d].wait_recv()
    for h in (0, 1):
        for d in (1, -1):
            p2[h, 2, d] = push(block(h, 2, 0), block(h, 2, 0), second[h](d), block(h, 2, -d))
    if turns:
        ring(turns.pop(0))
    onward(1)
    while turns:
        ring(turns.pop(0))
    onward(-1)
    onward(2)
    for arrival in late:
        arrival.wait_recv()
    for copy in own[2:] + zeros:
        copy.wait()
    for copy in sent:
        copy.wait_send()
    assert count[0] == sends.shape[0], count[0]


def fetch(users, tiles, list_ref, ubuf, tbuf, usem, tsem, half, e, slot):
    b, tile = list_ref[0, e], list_ref[1, e]
    per = 2 * half
    yp, cl = tile // per, tile % per
    w, i = b // 2, b % 2
    rows = ubuf.shape[1]
    return (
        pltpu.make_async_copy(
            users.at[w, pl.ds(pl.multiple_of(i * rows, rows), rows)], ubuf.at[slot], usem.at[slot]
        ),
        pltpu.make_async_copy(
            tiles.at[yp, :, cl // half, cl % half], tbuf.at[slot], tsem.at[slot]
        ),
    )


def scores(ubuf, tbuf, shift_ref, slot, tile, scale):
    user = ubuf[slot]
    ads = tbuf[slot].reshape(tbuf.shape[1] * tbuf.shape[2], tbuf.shape[3])
    pick = lax.broadcasted_iota(jnp.int32, (shift_ref.shape[0], user.shape[0]), 0) == tile
    shift = lax.dot_general(
        shift_ref[...], pick.astype(jnp.float32).astype(jnp.bfloat16), (((0,), (0,)), ((), ())),
        preferred_element_type=jnp.float32,
    )
    raw = lax.dot_general(ads, user, (((1,), (1,)), ((), ())), preferred_element_type=jnp.float32)
    return user, ads, raw * scale - shift


def flash_kernel(
    half, scale, codes, mine, users, tiles, shift_ref, _zeroed,
    stats, masses, grads, list_ref, ubuf, tbuf, usem, tsem, acc, gout, gsem,
):
    nw = users.shape[0]
    ny = tiles.shape[0]
    rows = ubuf.shape[1]
    parts = tbuf.shape[1]
    t = mine[0]

    def gather(w, n):
        for i in range(2):
            for yp in range(ny):
                list_ref[0, n] = w * 2 + i
                list_ref[1, n] = yp * (2 * half) + codes[2 * w + 1, yp]
                n = n + (codes[2 * w, yp] == 2 * t + i).astype(jnp.int32)
        return n

    total = lax.fori_loop(0, nw, gather, jnp.int32(0))
    list_ref[0, total] = -1
    list_ref[1, total] = 0
    get = functools.partial(fetch, users, tiles, list_ref, ubuf, tbuf, usem, tsem, half)
    ahead = ubuf.shape[0] - 1
    for k in range(ahead):
        @pl.when(total > k)
        def _():
            for copy in get(k, k):
                copy.start()

    stats[:, :, :, 0] = jnp.full(stats.shape[:3] + stats.shape[4:], LOW, jnp.float32)
    stats[:, :, :, 1] = jnp.zeros(stats.shape[:3] + stats.shape[4:], jnp.float32)
    masses[...] = jnp.zeros_like(masses)

    def put(b, slot):
        return pltpu.make_async_copy(gout.at[slot], grads.at[b], gsem.at[slot])

    def step(e, n):
        slot = e % (ahead + 1)

        @pl.when(e + ahead < total)
        def _():
            for copy in get(e + ahead, (e + ahead) % (ahead + 1)):
                copy.start()

        for copy in get(e, slot):
            copy.wait()
        b, tile = list_ref[0, e], list_ref[1, e]
        fresh = jnp.logical_or(e == 0, list_ref[0, jnp.maximum(e - 1, 0)] != b)
        last = list_ref[0, e + 1] != b
        at = ((b // 2) % 2, b // 4, b % 2)
        user, ads, logits = scores(ubuf, tbuf, shift_ref, slot, tile, scale)
        logits = logits * LOG2E
        before = stats[at + (0, slice(None), pl.ds(0, rows))]
        held = stats[at + (1, slice(None), pl.ds(0, rows))]
        top = jnp.maximum(before, jnp.ceil(jnp.max(logits, axis=0, keepdims=True)))
        carry = jnp.exp2(before - top)
        terms = jnp.exp2(logits - top)
        stats[at + (0, slice(None), pl.ds(0, rows))] = top
        stats[at + (1, slice(None), pl.ds(0, rows))] = held * carry + jnp.sum(
            terms, axis=0, keepdims=True
        )
        probs = terms.astype(jnp.bfloat16)
        wide = probs.astype(jnp.float32).reshape(parts, probs.shape[0] // parts, rows)
        mass = jnp.sum(wide, axis=1)
        term = lax.dot_general(probs, ads, (((0,), (0,)), ((), ())), preferred_element_type=jnp.float32)

        @pl.when(fresh)
        def _():
            acc[...] = term

        @pl.when(jnp.logical_not(fresh))
        def _():
            acc[...] = acc[...] * as_column(carry) + term
            masses[b, :, :, 0:rows] = masses[b, :, :, 0:rows] * carry[None]

        masses[b, tile // (2 * half), 0:parts, 0:rows] = mass

        @pl.when(last)
        def _():
            to = n % 2

            @pl.when(n >= 2)
            def _():
                put(0, to).wait()

            gout[to] = acc[...].astype(jnp.bfloat16)
            put(b, to).start()

        return n + last.astype(jnp.int32)

    n = lax.fori_loop(0, total, step, jnp.int32(0))
    for k in range(2):
        @pl.when(n > k)
        def _():
            put(0, k).wait()


def as_row(column):
    n = column.shape[0]
    eye = lax.broadcasted_iota(jnp.int32, (n, n), 0) == lax.broadcasted_iota(jnp.int32, (n, n), 1)
    return jnp.sum(jnp.where(eye, column, 0.0), axis=0, keepdims=True)


def as_column(row):
    n = row.shape[1]
    eye = lax.broadcasted_iota(jnp.int32, (n, n), 0) == lax.broadcasted_iota(jnp.int32, (n, n), 1)
    return jnp.sum(jnp.where(eye, row, 0.0), axis=1, keepdims=True)


def diagonal(row):
    n = row.shape[1]
    eye = lax.broadcasted_iota(jnp.int32, (n, n), 0) == lax.broadcasted_iota(jnp.int32, (n, n), 1)
    return jnp.where(eye, row, 0.0).astype(jnp.bfloat16)


def return_kernel(
    sizes, scale, factor_scale, grads, stats, masses, names, users, positives,
    user_grad, centroid_grad, losses,
    own, sib, long_out, long_in, short_out, short_in,
    klong_out, klong_in, kshort_out, kshort_in,
    final, landed, parts, cluster, everyone, terms,
    across, joined, came, mine, got, beside, lost, factor, positive,
    own_sem, sib_s, sib_r, long_s, long_r, short_s, short_r,
    kl_s, kl_r, ks_s, ks_r, fin_s, fin_r, cl_s, cl_r,
    s0, r0, s1, r1, s2, r2, s3, r3, s4, r4, usem,
):
    nx, nz, ny, nc = sizes
    x, z, y, c = (lax.axis_index(a) for a in AXES)
    at_z = lambda d: lax.rem(z + d + nz, nz)
    above, below = {"z": at_z(1)}, {"z": at_z(-1)}
    sibling = {"c": 1 - c}
    rows, width = own.shape[2], own.shape[3]
    per, depth = cluster.shape[2], cluster.shape[3]
    steps = nz // 2
    pairs = [(dx, dy) for dx in range(nx) for dy in range(ny) if dx or dy]
    place = lambda dx, dy: (lax.rem(x + dx + nx, nx), lax.rem(y + dy + ny, ny))
    greet(
        [{"z": at_z(d)} for d in range(1, nz)]
        + [dict(zip(("x", "y"), place(dx, dy))) for dx, dy in pairs]
        + [sibling]
    )
    over = remote(stats.at[1 - c], across, s0, r0, 0, sibling)
    over.start()
    order = []
    for s in range(steps):
        order.append(steps - s)
        if s > 0:
            order.append(s - steps)
    order.append(0)
    index = {d: k for k, d in enumerate(order)}
    loads = [
        pltpu.make_async_copy(grads.at[at_z(d), c], own.at[k], own_sem.at[k])
        for k, d in enumerate(order)
    ]
    crossing = [
        remote(grads.at[at_z(d), 1 - c], sib.at[k], sib_s, sib_r, k, sibling)
        for k, d in enumerate(order)
    ]

    def begin(ks):
        for k in ks:
            loads[k].start()
            crossing[k].start()

    def ready(d):
        loads[index[d]].wait()
        crossing[index[d]].wait_recv()

    def merged(d, i, extra):
        k = index[d]
        items = [
            (stats[c, at_z(d), i, 0, :, pl.ds(0, rows)], own[k, i]),
            (across[at_z(d), i, 0, :, pl.ds(0, rows)], sib[k, i]),
        ] + extra
        top = items[0][0]
        for level, _ in items[1:]:
            top = jnp.maximum(top, level)
        whole = 0.0
        for level, value in items:
            whole = whole + jnp.dot(
                diagonal(jnp.exp2(level - top)), value, preferred_element_type=jnp.float32
            )
        return whole, top

    away = lambda i: above if i == 0 else below
    back = lambda i: below if i == 0 else above
    longs = lambda s, i: (
        remote(long_out.at[s, i], long_in.at[s, i], long_s, long_r, 2 * s + i, away(i)),
        remote(klong_out.at[s, i], klong_in.at[s, i], kl_s, kl_r, 2 * s + i, away(i)),
    )
    shorts = lambda s, i: (
        remote(short_out.at[s - 1, i], short_in.at[s - 1, i], short_s, short_r, 2 * s + i, back(i)),
        remote(kshort_out.at[s - 1, i], kshort_in.at[s - 1, i], ks_s, ks_r, 2 * s + i, back(i)),
    )

    def arrive(copies):
        for copy in copies:
            copy.wait_recv()

    part_of = lambda i: pl.ds(pl.multiple_of(i * 2 * rows, 2 * rows), 2 * rows)
    columns = lambda i: pl.ds(pl.multiple_of(i * depth, depth), depth)
    own_part = pltpu.make_async_copy(positives.at[part_of(x)], positive.at[:, columns(x)], usem.at[1])

    def positive_copy(d):
        px = lax.rem(x + d, nx)
        return remote(positives.at[part_of(px)], positive.at[:, columns(x)], s4, r4, d, {"x": px})

    def send_stats():
        begin(range(min(3, nz), nz))
        pltpu.make_async_copy(users.at[:, pl.ds(0, 2 * rows)], everyone, usem.at[0]).start()
        own_part.start()
        for d in range(1, nx):
            positive_copy(d).start()
        here = stats[pl.ds(c, 1)][0]
        there = across[...]
        tops = jnp.maximum(here[:, :, 0], there[:, :, 0])
        joined[:, :, 0] = tops
        joined[:, :, 1] = here[:, :, 1] * jnp.exp2(here[:, :, 0] - tops) + there[
            :, :, 1
        ] * jnp.exp2(there[:, :, 0] - tops)

        def out(d, _):
            p = lax.rem(z + d, nz)
            remote(joined.at[p], came.at[z], s1, r1, d, {"z": p}).start()
            return 0

        lax.fori_loop(1, nz, out, 0)
        came[pl.ds(z, 1)] = joined[pl.ds(z, 1)]
        mine[...] = jnp.zeros_like(mine)
        factor[...] = jnp.zeros_like(factor)
        lost[pl.ds(x, 1)] = jnp.zeros((1,) + lost.shape[1:], jnp.float32)

    def total():
        pltpu.make_async_copy(users.at[:, pl.ds(0, 2 * rows)], everyone, usem.at[0]).wait()
        own_part.wait()
        for d in range(1, nx):
            frm = lax.rem(x - d + nx, nx)
            landing = positive.at[:, columns(frm)]
            remote(landing, landing, s4, r4, d, {"x": frm}).wait_recv()

        def come(d, _):
            p = lax.rem(z + nz - d, nz)
            remote(came.at[p], came.at[p], s1, r1, d, {"z": p}).wait_recv()
            return 0

        lax.fori_loop(1, nz, come, 0)
        for i in range(2):
            u = everyone[z * nc + c, i * rows:(i + 1) * rows].astype(jnp.float32)
            v = positive[i * rows:(i + 1) * rows].astype(jnp.float32)
            dot = as_row(jnp.sum(u * v, axis=1, keepdims=True)) * (scale * LOG2E)
            tops = came[:, i, 0, :, 0:rows]
            sums = came[:, i, 1, :, 0:rows]
            ceiling = jnp.maximum(jnp.max(tops, axis=0), dot)
            whole = jnp.log(
                jnp.sum(sums * jnp.exp2(tops - ceiling[None]), axis=0) + jnp.exp2(dot - ceiling)
            )
            log_total = ceiling + whole * LOG2E
            mine[i, :, 0:rows] = log_total
            lost[pl.ds(x, 1), i, :, 0:rows] = (whole + (ceiling - dot) * LN2)[None]
            factor[i, :, 0:rows] = jnp.exp2(dot - log_total) - 1.0

        def give(d, _):
            p = lax.rem(z + d, nz)
            remote(mine, got.at[z], s2, r2, d, {"z": p}).start()
            return 0

        lax.fori_loop(1, nz, give, 0)
        for d in range(1, nx):
            remote(lost.at[x], lost.at[x], s3, r3, d, {"x": lax.rem(x + d, nx)}).start()
        got[pl.ds(z, 1)] = mine[...][None]

    beside_copy = remote(got, beside, s0, r0, 1, sibling)

    def spread():
        def done(d, _):
            p = lax.rem(z + nz - d, nz)
            remote(got.at[p], got.at[p], s2, r2, d, {"z": p}).wait_recv()
            return 0

        lax.fori_loop(1, nz, done, 0)
        beside_copy.start()

    def weigh(core, logs, first, count):
        def one(k, _):
            w = k * nc + core
            both = 0.0
            for i in range(2):
                level = stats[core, k, i, 0, :, pl.ds(0, rows)]
                share = jnp.exp2(level - logs[k, i, :, pl.ds(0, rows)])
                mass = masses[2 * w + i, :, :, pl.ds(0, rows)] * share[None]
                mass = mass.reshape(mass.shape[0] * mass.shape[1], rows).astype(jnp.bfloat16)
                both = both + jnp.dot(
                    mass, everyone[w, i * rows:(i + 1) * rows], preferred_element_type=jnp.float32
                )
            terms[w] = both
            return 0

        lax.fori_loop(first, first + count, one, 0)

    def cluster_copy(k):
        px, py = place(*pairs[k])
        return remote(cluster.at[py, px], parts.at[k], cl_s, cl_r, k, {"x": px, "y": py})

    def clusters():
        flat = terms[...].reshape(terms.shape[0] * terms.shape[1], width)
        pick = lax.broadcasted_iota(jnp.int32, (ny * per, flat.shape[0]), 0) == names[...]
        summed = jnp.dot(
            pick.astype(jnp.float32), flat, precision=lax.Precision.HIGHEST,
            preferred_element_type=jnp.float32,
        )
        for py in range(ny):
            for px in range(nx):
                cluster[py, px] = summed[py * per:(py + 1) * per, px * depth:(px + 1) * depth]
        for k in range(len(pairs)):
            cluster_copy(k).start()

    part = nz // 2
    tasks = [
        (0, send_stats),
        (2, total),
        (4, spread),
        (4, lambda: weigh(c, got, 0, part)),
        (5, lambda: weigh(c, got, part, nz - part)),
        (6, beside_copy.wait_recv),
        (6, lambda: weigh(1 - c, beside, 0, part)),
        (7, lambda: weigh(1 - c, beside, part, nz - part)),
        (7, clusters),
    ]

    begin(range(min(3, nz)))
    for levels in (klong_out, kshort_out):
        levels[...] = jnp.zeros_like(levels)
    over.wait_recv()
    for s in range(steps):
        ready(steps - s)
        if s > 0:
            ready(s - steps)
        for i in range(2):
            sign = 1 if i == 0 else -1
            extra = []
            if s > 0:
                arrive(longs(s - 1, i))
                extra = [(klong_in[s - 1, i, :, 0:rows], long_in[s - 1, i])]
            value, top = merged(sign * (steps - s) if s > 0 else steps, i, extra)
            long_out[s, i] = value.astype(jnp.bfloat16)
            klong_out[s, i, :, 0:rows] = top
            for copy in longs(s, i):
                copy.start()
            if s > 0:
                extra = []
                if s > 1:
                    arrive(shorts(s - 1, i))
                    extra = [(kshort_in[s - 2, i, :, 0:rows], short_in[s - 2, i])]
                value, top = merged(sign * (s - steps), i, extra)
                short_out[s - 1, i] = value.astype(jnp.bfloat16)
                kshort_out[s - 1, i, :, 0:rows] = top
                for copy in shorts(s, i):
                    copy.start()
        while tasks and (tasks[0][0] == s or s == steps - 1):
            tasks.pop(0)[1]()
    def end(d, i):
        px = lax.rem(x + d, nx)
        return remote(final.at[px, i], landed.at[x, i], fin_s, fin_r, 2 * d + i, {"x": px})

    ready(0)
    for i in range(2):
        arrive(shorts(steps - 1, i))
        arrive(longs(steps - 1, i))
        value, top = merged(
            0, i,
            [
                (klong_in[steps - 1, i, :, 0:rows], long_in[steps - 1, i]),
                (kshort_in[steps - 2, i, :, 0:rows], short_in[steps - 2, i]),
            ],
        )
        wide = positive[i * rows:(i + 1) * rows].astype(jnp.float32)
        value = value * as_column(jnp.exp2(top - mine[i, :, 0:rows]))
        value = (value + as_column(factor[i, :, 0:rows]) * wide) * factor_scale
        for k in range(nx):
            final[k, i] = value[:, k * depth:(k + 1) * depth]
        for d in range(1, nx):
            end(d, i).start()
    whole = cluster[y, x]
    for k in range(len(pairs)):
        cluster_copy(k).wait_recv()
        whole = whole + parts[k]
    centroid_grad[...] = whole * factor_scale
    user_grad[pl.ds(x, 1)] = final[pl.ds(x, 1)]
    for d in range(1, nx):
        frm = lax.rem(x - d + nx, nx)
        remote(lost.at[frm], lost.at[frm], s3, r3, d, {"x": frm}).wait_recv()
    losses[...] = lost[...]
    for i in range(2):
        for d in range(1, nx):
            frm = lax.rem(x - d + nx, nx)
            landing = landed.at[frm, i]
            remote(landing, landing, fin_s, fin_r, 2 * d + i, {"x": frm}).wait_recv()
            user_grad[pl.ds(frm, 1), i] = landed[pl.ds(frm, 1), i]

    for copy in crossing + [cluster_copy(k) for k in range(len(pairs))] + [over, beside_copy]:
        copy.wait_send()
    for i in range(2):
        for s in range(steps):
            for copy in longs(s, i) + (shorts(s, i) if s > 0 else ()):
                copy.wait_send()
        for d in range(1, nx):
            end(d, i).wait_send()

    def left(d, _):
        p = lax.rem(z + d, nz)
        remote(joined.at[p], came.at[z], s1, r1, d, {"z": p}).wait_send()
        remote(mine, got.at[z], s2, r2, d, {"z": p}).wait_send()
        return 0

    lax.fori_loop(1, nz, left, 0)
    for d in range(1, nx):
        remote(lost.at[x], lost.at[x], s3, r3, d, {"x": lax.rem(x + d, nx)}).wait_send()
        positive_copy(d).wait_send()


def params(identity=None, megabytes=48):
    return pltpu.CompilerParams(
        collective_id=identity,
        has_side_effects=identity is not None,
        vmem_limit_bytes=megabytes * 1024 * 1024,
    )


def lanes_of(rows):
    return -(-rows // 128) * 128


def buffers_of(rows, width, nx, quarter):
    return [
        pltpu.VMEM((SLOTS, rows, width), jnp.bfloat16),
        pltpu.VMEM((SLOTS, nx, quarter, width), jnp.bfloat16),
        pltpu.SemaphoreType.DMA((SLOTS,)),
        pltpu.SemaphoreType.DMA((SLOTS,)),
    ]


def flash_call(nw, ny, half, scale, rows, width, nx, quarter):
    sds = jax.ShapeDtypeStruct
    lanes = lanes_of(rows)
    return pl.pallas_call(
        functools.partial(flash_kernel, half, scale),
        out_shape=(
            sds((2, nw // 2, 2, 2, 1, lanes), jnp.float32),
            sds((2 * nw, ny, MASS_ROWS, lanes), jnp.float32),
            sds((2 * nw, rows, width), jnp.bfloat16),
        ),
        in_specs=[SMEM, SMEM, HBM, HBM, VMEM, HBM],
        out_specs=[VMEM, VMEM, HBM],
        input_output_aliases={5: 2},
        scratch_shapes=[pltpu.SMEM((2, nw * ny + 8), jnp.int32)]
        + buffers_of(rows, width, nx, quarter)
        + [
            pltpu.VMEM((rows, width), jnp.float32),
            pltpu.VMEM((2, rows, width), jnp.bfloat16),
            pltpu.SemaphoreType.DMA((2,)),
        ],
        compiler_params=params(None, 58),
        name="flash",
    )


def return_call(sizes, scale, rows, width, per):
    nx, nz, ny, nc = sizes
    lanes, depth, steps, nw = lanes_of(rows), width // nx, nz // 2, nz * nc
    sds = lambda *shape: jax.ShapeDtypeStruct(shape, jnp.float32)
    buffer = lambda *shape: pltpu.VMEM(shape, jnp.float32)
    ring = lambda n: pltpu.VMEM((n, 2, rows, width), jnp.bfloat16)
    dma = pltpu.SemaphoreType.DMA
    return pl.pallas_call(
        functools.partial(return_kernel, sizes, scale, LOSS_SCALE * scale),
        out_shape=(sds(nx, 2, rows, depth), sds(per, depth), sds(nx, 2, 1, lanes)),
        in_specs=[HBM, VMEM, VMEM, VMEM, HBM, HBM],
        out_specs=[VMEM] * 3,
        scratch_shapes=[
            ring(nz), ring(nz), ring(steps), ring(steps), ring(steps - 1), ring(steps - 1),
            buffer(steps, 2, 1, lanes), buffer(steps, 2, 1, lanes),
            buffer(steps - 1, 2, 1, lanes), buffer(steps - 1, 2, 1, lanes),
            buffer(nx, 2, rows, depth), buffer(nx, 2, rows, depth),
            buffer(max(nx * ny - 1, 1), per, depth), buffer(ny, nx, per, depth),
            pltpu.VMEM((nw, 2 * rows, width), jnp.bfloat16),
            buffer(nw, ny * MASS_ROWS, width),
            buffer(nz, 2, 2, 1, lanes), buffer(nz, 2, 2, 1, lanes), buffer(nz, 2, 2, 1, lanes),
            buffer(2, 1, lanes), buffer(nz, 2, 1, lanes), buffer(nz, 2, 1, lanes),
            buffer(nx, 2, 1, lanes), buffer(2, 1, lanes),
            pltpu.VMEM((2 * rows, width), jnp.bfloat16),
            dma((nz,)), dma((nz,)), dma((nz,)),
        ]
        + [dma((2 * steps,))] * 8
        + [dma((2 * nx,))] * 2
        + [dma((nx * ny,))] * 2
        + [dma((2,))] * 2
        + [dma((nz,))] * 4
        + [dma((nx,))] * 4
        + [dma((2,))],
        compiler_params=params(2, 58),
        name="return",
    )


def local(
    sizes, user_rows, positive_rows, centroids, residuals, block_lists, block_lengths,
    cluster_counts, ad_counts,
):
    nx, nz, ny, nc = sizes
    x, z, y, c = (lax.axis_index(a) for a in AXES)
    nw, shards = nz * nc, nz * ny * nc
    per, width = centroids.shape
    quarter = residuals.shape[1]
    tile = ad_counts.shape[1]
    blocks, listed = block_lists.shape
    rows = user_rows.shape[0] // blocks
    half = per // 2
    scale = 1.0 / math.sqrt(width)
    sds = jax.ShapeDtypeStruct
    dma = pltpu.SemaphoreType.DMA
    bf16, f32 = jnp.bfloat16, jnp.float32

    ad_rows = (centroids[:, None, :] + residuals.astype(f32)).astype(bf16)
    weights = ad_counts.astype(f32)
    expected = (
        cluster_counts.astype(f32)[:, None] * weights / jnp.sum(weights, axis=1, keepdims=True)
    )
    shift = jnp.log(expected).astype(bf16)
    flat = block_lists.reshape(blocks * listed)
    used = jnp.arange(listed)[None, :] < block_lengths[:, None]
    name = jnp.where(used, jnp.arange(blocks)[:, None] + 1, 0).reshape(blocks * listed)
    match = flat[:, None] // per == jnp.arange(shards)[None, :]
    block_of = jnp.sum(jnp.where(match, name[:, None], 0), axis=0) - 1
    place_of = jnp.sum(jnp.where(match, (flat % per)[:, None], 0), axis=0)
    codes = jnp.stack([block_of, place_of]).astype(f32).astype(bf16)
    codes = jnp.pad(codes, ((0, CODE_ROWS - 2), (0, width - shards)))

    steps = nz // 2
    copies = (nx - 1) + (ny - 1) + 8 + 4 + 12 + 16 + (nz - 1) + nz
    mine = 2 * rows
    all_tiles, all_users, all_shift, zeroed = pl.pallas_call(
        functools.partial(gather_kernel, sizes),
        out_shape=(
            sds((ny, nx, 2, half, quarter, width), bf16),
            sds((nz, nc, mine + CODE_ROWS, width), bf16),
            sds((ny, per, tile), bf16),
            sds((2 * nw, rows, width), bf16),
        ),
        in_specs=[HBM] * 4,
        out_specs=[HBM] * 4,
        scratch_shapes=[
            dma((copies,)), dma((copies,)), dma((4,)),
            pltpu.VMEM((4, rows, width), bf16), dma((nw // 2,)),
        ],
        compiler_params=params(0, 58),
        name="gather",
    )(ad_rows.reshape(2, half, quarter, width), user_rows, codes, shift)

    pick = jnp.arange(shards)[:, None] == z * ny * nc + jnp.arange(ny)[None, :] * nc + c
    found = all_users[:, :, mine:mine + 2, :shards].reshape(nw * 2, shards)
    places = jnp.dot(found, pick.astype(bf16), preferred_element_type=f32).astype(jnp.int32)
    flat_users = all_users.reshape(nw, mine + CODE_ROWS, width)
    flat_shift = all_shift.reshape(ny * per, tile)
    stats, masses, grads = flash_call(nw, ny, half, scale, rows, width, nx, quarter)(
        places, x.astype(jnp.int32).reshape(1), flat_users, all_tiles, flat_shift, zeroed
    )
    depth = width // nx
    names = places.reshape(nw, 2, ny)[:, 1] + per * jnp.arange(ny)[None, :]
    names = jnp.repeat(names.reshape(1, nw * ny), MASS_ROWS, axis=1)
    user_grad, centroid_grad, losses = return_call(sizes, scale, rows, width, per)(
        grads.reshape(nz, nc, 2, rows, width), stats, masses, names, flat_users, positive_rows
    )
    return (
        losses[:, :, 0, :rows].reshape(blocks * rows),
        user_grad.reshape(blocks * rows, depth),
        centroid_grad,
    )


def build(mesh, sizes):
    return jax.shard_map(
        functools.partial(local, sizes),
        mesh=mesh,
        in_specs=(
            P(("z", "y", "c"), "x"),
            P(("z", "y", "c"), "x"),
            P(("z", "y", "c"), None),
            P(("z", "y", "c"), "x", None),
            P(("z", "y", "c"), None),
            P(("z", "y", "c")),
            P(("z", "y", "c")),
            P(("z", "y", "c"), None),
        ),
        out_specs=(P(("z", "y", "c")), P(("z", "y", "c"), "x"), P(("z", "y", "c"), "x")),
        check_vma=False,
    )


def solution(mesh):
    sizes = (mesh.shape["tower"],) + SPLIT
    return build(Mesh(mesh.devices.reshape(sizes), AXES), sizes)
```

```python
import functools
import math

import jax
import jax.numpy as jnp
from jax import lax
from jax.experimental import pallas as pl
from jax.experimental.pallas import tpu as pltpu
from jax.sharding import Mesh, PartitionSpec as P

LOSS_SCALE = 16
AXES = ("x", "z", "y", "c")
SPLIT = (16, 4, 2)
LOW = -1e30
LOG2E = math.log2(math.e)
LN2 = math.log(2.0)
MESH = pl.DeviceIdType.MESH
HBM = pl.BlockSpec(memory_space=pl.ANY)
VMEM = pl.BlockSpec(memory_space=pltpu.VMEM)
SMEM = pl.BlockSpec(memory_space=pltpu.SMEM)
CODE_ROWS = 16
SLOTS = 8
MASS_ROWS = 8


def remote(src, dst, sends, recvs, k, where):
    return pltpu.make_async_remote_copy(
        src_ref=src,
        dst_ref=dst,
        send_sem=sends.at[k],
        recv_sem=recvs.at[k],
        device_id=where,
        device_id_type=MESH,
    )


def greet(peers):
    barrier = pltpu.get_barrier_semaphore()
    for where in peers:
        pl.semaphore_signal(barrier, inc=1, device_id=where, device_id_type=MESH)
    pl.semaphore_wait(barrier, len(peers))


def gather_kernel(
    sizes, tiles, users, codes, shift,
    all_tiles, all_users, all_shift, zeroed, sends, recvs, locals_, zbuf, zsem,
):
    nx, nz, ny, nc = sizes
    x, z, y, c = (lax.axis_index(a) for a in AXES)
    rows = users.shape[0] // nx
    depth = users.shape[1]
    half = tiles.shape[1]
    quarter = half // 2
    at_x = lambda d: lax.rem(x + d + nx, nx)
    at_y = lambda d: lax.rem(y + d + ny, ny)
    at_z = lambda d: lax.rem(z + d + nz, nz)
    to_x = lambda d: {"x": at_x(d)}
    to_y = lambda d: {"y": at_y(d)}
    to_z = lambda d: {"z": at_z(d)}
    sibling = {"c": 1 - c}

    greet(
        [to_x(d) for d in range(1, nx)]
        + [to_y(d) for d in range(1, ny)]
        + [to_z(1), to_z(-1), sibling]
    )

    count = [0]
    sent = []

    def push(src, dst, where, landing):
        k = count[0]
        count[0] += 1
        copy = remote(src, dst, sends, recvs, k, where)
        copy.start()
        sent.append(copy)
        return remote(landing, landing, sends, recvs, k, where)

    columns = lambda i: pl.ds(pl.multiple_of(i * depth, depth), depth)
    part = lambda i: pl.ds(pl.multiple_of(i * rows, rows), rows)
    home = all_users.at[z, c]

    def block(h, a, b):
        return all_tiles.at[at_y(b), at_x(a), h] if h == 0 else all_tiles.at[at_y(a), at_x(b), h]

    first = (to_x, to_y)
    second = (to_y, to_x)
    lower, upper = pl.ds(0, quarter), pl.ds(quarter, quarter)

    arrivals = []
    for d in range(1, nx):
        arrivals.append(
            push(
                users.at[part(at_x(d))], home.at[pl.ds(0, rows), columns(x)], to_x(d),
                home.at[pl.ds(0, rows), columns(at_x(-d))],
            )
        )
    p1 = {}
    for h in (0, 1):
        for d in (1, -1):
            p1[h, d] = push(tiles.at[h], block(h, 0, 0), first[h](d), block(h, -d, 0))
    own = [
        pltpu.make_async_copy(users.at[part(x)], home.at[pl.ds(0, rows), columns(x)], locals_.at[0]),
        pltpu.make_async_copy(codes, home.at[pl.ds(rows, CODE_ROWS)], locals_.at[1]),
        pltpu.make_async_copy(tiles, all_tiles.at[y, x], locals_.at[2]),
        pltpu.make_async_copy(shift, all_shift.at[y], locals_.at[3]),
    ]
    for copy in own:
        copy.start()
    zbuf[...] = jnp.zeros_like(zbuf)
    piece = zbuf.shape[0]
    zeros = [
        pltpu.make_async_copy(zbuf, zeroed.at[pl.ds(k * piece, piece)], zsem.at[k])
        for k in range(zeroed.shape[0] // piece)
    ]
    for copy in zeros:
        copy.start()
    late = []
    p2 = {}
    for h in (0, 1):
        for d in (1, -1):
            p2[h, 0, d] = push(tiles.at[h], block(h, 0, 0), second[h](d), block(h, 0, -d))
    for d in range(1, ny):
        late.append(push(shift, all_shift.at[y], to_y(d), all_shift.at[at_y(-d)]))

    for arrival in arrivals:
        arrival.wait_recv()
    own[0].wait()
    own[1].wait()

    chunk = lambda d: all_users.at[at_z(d), c]
    other = lambda d: all_users.at[at_z(d), 1 - c]
    steps = nz // 2
    up, down = {}, {}

    def ring(s):
        if s > 0:
            up[s - 1].wait_recv()
            if s - 1 in down:
                down[s - 1].wait_recv()
        if s < steps:
            up[s] = push(chunk(-s), chunk(-s), to_z(1), chunk(-s - 1))
        if s < steps - 1:
            down[s] = push(chunk(s), chunk(s), to_z(-1), chunk(s + 1))
        late.append(push(chunk(-s), chunk(-s), sibling, other(-s)))
        if 0 < s < steps:
            late.append(push(chunk(s), chunk(s), sibling, other(s)))

    turns = list(range(steps + 1))
    ring(turns.pop(0))
    while len(turns) > steps - 3 and turns:
        ring(turns.pop(0))

    for h in (0, 1):
        for d in (1, -1):
            p1[h, d].wait_recv()
    q = {}
    for h in (0, 1):
        for d in (1, -1):
            cut = lower if d == 1 else upper
            q[h, d] = push(
                block(h, -d, 0).at[cut], block(h, -d, 0).at[cut], first[h](d), block(h, -2 * d, 0).at[cut]
            )
    for j in (1, -1):
        for h in (0, 1):
            for d in (1, -1):
                p2[h, j, d] = push(block(h, j, 0), block(h, j, 0), second[h](d), block(h, j, -d))
    if turns:
        ring(turns.pop(0))

    def onward(j):
        for h in (0, 1):
            for d in (1, -1):
                p2[h, j, d].wait_recv()
                cut = lower if d == 1 else upper
                late.append(
                    push(
                        block(h, j, -d).at[cut], block(h, j, -d).at[cut], second[h](d),
                        block(h, j, -2 * d).at[cut],
                    )
                )

    onward(0)
    for h in (0, 1):
        for d in (1, -1):
            q[h, d].wait_recv()
    for h in (0, 1):
        for d in (1, -1):
            p2[h, 2, d] = push(block(h, 2, 0), block(h, 2, 0), second[h](d), block(h, 2, -d))
    if turns:
        ring(turns.pop(0))
    onward(1)
    while turns:
        ring(turns.pop(0))
    onward(-1)
    onward(2)
    for arrival in late:
        arrival.wait_recv()
    for copy in own[2:] + zeros:
        copy.wait()
    for copy in sent:
        copy.wait_send()
    assert count[0] == sends.shape[0], count[0]


def fetch(users, tiles, entry, ubuf, tbuf, usem, tsem, half, e, slot):
    b, tile = entry(e)
    per = 2 * half
    yp, cl = tile // per, tile % per
    w, i = b // 2, b % 2
    rows = ubuf.shape[1]
    return (
        pltpu.make_async_copy(
            users.at[w, pl.ds(pl.multiple_of(i * rows, rows), rows)], ubuf.at[slot], usem.at[slot]
        ),
        pltpu.make_async_copy(
            tiles.at[yp, :, cl // half, cl % half], tbuf.at[slot], tsem.at[slot]
        ),
    )


def ads_of(tbuf, slot):
    return tbuf[slot].reshape(tbuf.shape[1] * tbuf.shape[2], tbuf.shape[3])


def scores(ubuf, tbuf, shift_ref, slot, tile, scale):
    user = ubuf[slot]
    ads = ads_of(tbuf, slot)
    pick = lax.broadcasted_iota(jnp.int32, (shift_ref.shape[0], user.shape[0]), 0) == tile
    shift = lax.dot_general(
        shift_ref[...], pick.astype(jnp.float32).astype(jnp.bfloat16), (((0,), (0,)), ((), ())),
        preferred_element_type=jnp.float32,
    )
    raw = lax.dot_general(ads, user, (((1,), (1,)), ((), ())), preferred_element_type=jnp.float32)
    return raw * scale - shift


def flash_kernel(
    half, scale, codes, mine, users, tiles, shift_ref, _zeroed,
    stats, masses, grads, list_ref, ubuf, tbuf, usem, tsem, acc, gout, gsem,
):
    nw = users.shape[0]
    ny = tiles.shape[0]
    rows = ubuf.shape[1]
    parts = tbuf.shape[1]
    t = mine[0]
    tiles_all = ny * 2 * half

    def entry(e):
        return list_ref[e] // tiles_all, list_ref[e] % tiles_all

    def gather(w, n):
        for i in range(2):
            for yp in range(ny):
                list_ref[n] = (w * 2 + i) * tiles_all + yp * (2 * half) + codes[2 * w + 1, yp]
                n = n + (codes[2 * w, yp] == 2 * t + i).astype(jnp.int32)
        return n

    total = lax.fori_loop(0, nw, gather, jnp.int32(0))
    list_ref[total] = 2 * nw * tiles_all
    get = functools.partial(fetch, users, tiles, entry, ubuf, tbuf, usem, tsem, half)
    ahead = ubuf.shape[0] - 1
    for k in range(ahead):
        @pl.when(total > k)
        def _():
            for copy in get(k, k):
                copy.start()

    stats[:, :, :, 0] = jnp.full(stats.shape[:3] + stats.shape[4:], LOW, jnp.float32)
    stats[:, :, :, 1] = jnp.zeros(stats.shape[:3] + stats.shape[4:], jnp.float32)
    masses[...] = jnp.zeros_like(masses)

    def put(b, slot):
        return pltpu.make_async_copy(gout.at[slot], grads.at[b], gsem.at[slot])

    def score(e):
        return scores(ubuf, tbuf, shift_ref, e % (ahead + 1), entry(e)[1], scale)

    @pl.when(total > 0)
    def _():
        for copy in get(0, 0):
            copy.wait()

    def step(e, held_over):
        n, logits = held_over
        slot = e % (ahead + 1)

        @pl.when(e + ahead < total)
        def _():
            for copy in get(e + ahead, (e + ahead) % (ahead + 1)):
                copy.start()

        @pl.when(e + 1 < total)
        def _():
            for copy in get(e + 1, (e + 1) % (ahead + 1)):
                copy.wait()

        b, tile = entry(e)
        fresh = jnp.logical_or(e == 0, entry(jnp.maximum(e - 1, 0))[0] != b)
        last = entry(e + 1)[0] != b
        at = ((b // 2) % 2, b // 4, b % 2)
        later = score(e + 1)
        ads = ads_of(tbuf, slot)
        logits = logits * LOG2E
        before = stats[at + (0, slice(None), pl.ds(0, rows))]
        held = stats[at + (1, slice(None), pl.ds(0, rows))]
        top = jnp.maximum(before, jnp.ceil(jnp.max(logits, axis=0, keepdims=True)))
        carry = jnp.exp2(before - top)
        terms = jnp.exp2(logits - top)
        stats[at + (0, slice(None), pl.ds(0, rows))] = top
        stats[at + (1, slice(None), pl.ds(0, rows))] = held * carry + jnp.sum(
            terms, axis=0, keepdims=True
        )
        probs = terms.astype(jnp.bfloat16)
        wide = probs.astype(jnp.float32).reshape(parts, probs.shape[0] // parts, rows)
        mass = jnp.sum(wide, axis=1)
        term = lax.dot_general(probs, ads, (((0,), (0,)), ((), ())), preferred_element_type=jnp.float32)

        @pl.when(fresh)
        def _():
            acc[...] = term

        @pl.when(jnp.logical_not(fresh))
        def _():
            acc[...] = acc[...] * as_column(carry) + term
            masses[b, :, :, 0:rows] = masses[b, :, :, 0:rows] * carry[None]

        masses[b, tile // (2 * half), 0:parts, 0:rows] = mass

        @pl.when(last)
        def _():
            to = n % 2

            @pl.when(n >= 2)
            def _():
                put(0, to).wait()

            gout[to] = acc[...].astype(jnp.bfloat16)
            put(b, to).start()

        return n + last.astype(jnp.int32), later

    n, _ = lax.fori_loop(0, total, step, (jnp.int32(0), score(0)))
    for k in range(2):
        @pl.when(n > k)
        def _():
            put(0, k).wait()


def as_row(column):
    n = column.shape[0]
    eye = lax.broadcasted_iota(jnp.int32, (n, n), 0) == lax.broadcasted_iota(jnp.int32, (n, n), 1)
    return jnp.sum(jnp.where(eye, column, 0.0), axis=0, keepdims=True)


def as_column(row):
    n = row.shape[1]
    eye = lax.broadcasted_iota(jnp.int32, (n, n), 0) == lax.broadcasted_iota(jnp.int32, (n, n), 1)
    return jnp.sum(jnp.where(eye, row, 0.0), axis=1, keepdims=True)


def diagonal(row):
    n = row.shape[1]
    eye = lax.broadcasted_iota(jnp.int32, (n, n), 0) == lax.broadcasted_iota(jnp.int32, (n, n), 1)
    return jnp.where(eye, row, 0.0).astype(jnp.bfloat16)


def return_kernel(
    sizes, scale, factor_scale, grads, stats, masses, names, users, positives,
    user_grad, centroid_grad, losses,
    own, sib, long_out, long_in, short_out, short_in,
    klong_out, klong_in, kshort_out, kshort_in,
    final, landed, parts, cluster, everyone, terms,
    across, joined, came, mine, got, beside, lost, factor, positive,
    own_sem, sib_s, sib_r, long_s, long_r, short_s, short_r,
    kl_s, kl_r, ks_s, ks_r, fin_s, fin_r, cl_s, cl_r,
    s0, r0, s1, r1, s2, r2, s3, r3, s4, r4, usem,
):
    nx, nz, ny, nc = sizes
    x, z, y, c = (lax.axis_index(a) for a in AXES)
    at_z = lambda d: lax.rem(z + d + nz, nz)
    above, below = {"z": at_z(1)}, {"z": at_z(-1)}
    sibling = {"c": 1 - c}
    rows, width = own.shape[2], own.shape[3]
    per, depth = cluster.shape[2], cluster.shape[3]
    steps = nz // 2
    pairs = [(dx, dy) for dx in range(nx) for dy in range(ny) if dx or dy]
    place = lambda dx, dy: (lax.rem(x + dx + nx, nx), lax.rem(y + dy + ny, ny))
    greet(
        [{"z": at_z(d)} for d in range(1, nz)]
        + [dict(zip(("x", "y"), place(dx, dy))) for dx, dy in pairs]
        + [sibling]
    )
    over = remote(stats.at[1 - c], across, s0, r0, 0, sibling)
    over.start()
    order = []
    for s in range(steps):
        order.append(steps - s)
        if s > 0:
            order.append(s - steps)
    order.append(0)
    index = {d: k for k, d in enumerate(order)}
    loads = [
        pltpu.make_async_copy(grads.at[at_z(d), c], own.at[k], own_sem.at[k])
        for k, d in enumerate(order)
    ]
    crossing = [
        remote(grads.at[at_z(d), 1 - c], sib.at[k], sib_s, sib_r, k, sibling)
        for k, d in enumerate(order)
    ]

    def begin(ks):
        for k in ks:
            loads[k].start()
            crossing[k].start()

    def ready(d):
        loads[index[d]].wait()
        crossing[index[d]].wait_recv()

    def merged(d, i, extra):
        k = index[d]
        items = [
            (stats[c, at_z(d), i, 0, :, pl.ds(0, rows)], own[k, i]),
            (across[at_z(d), i, 0, :, pl.ds(0, rows)], sib[k, i]),
        ] + extra
        top = items[0][0]
        for level, _ in items[1:]:
            top = jnp.maximum(top, level)
        whole = 0.0
        for level, value in items:
            whole = whole + jnp.dot(
                diagonal(jnp.exp2(level - top)), value, preferred_element_type=jnp.float32
            )
        return whole, top

    away = lambda i: above if i == 0 else below
    back = lambda i: below if i == 0 else above
    longs = lambda s, i: (
        remote(long_out.at[s, i], long_in.at[s, i], long_s, long_r, 2 * s + i, away(i)),
        remote(klong_out.at[s, i], klong_in.at[s, i], kl_s, kl_r, 2 * s + i, away(i)),
    )
    shorts = lambda s, i: (
        remote(short_out.at[s - 1, i], short_in.at[s - 1, i], short_s, short_r, 2 * s + i, back(i)),
        remote(kshort_out.at[s - 1, i], kshort_in.at[s - 1, i], ks_s, ks_r, 2 * s + i, back(i)),
    )

    def arrive(copies):
        for copy in copies:
            copy.wait_recv()

    part_of = lambda i: pl.ds(pl.multiple_of(i * 2 * rows, 2 * rows), 2 * rows)
    columns = lambda i: pl.ds(pl.multiple_of(i * depth, depth), depth)
    own_part = pltpu.make_async_copy(positives.at[part_of(x)], positive.at[:, columns(x)], usem.at[1])

    def positive_copy(d):
        px = lax.rem(x + d, nx)
        return remote(positives.at[part_of(px)], positive.at[:, columns(x)], s4, r4, d, {"x": px})

    def send_stats():
        begin(range(min(3, nz), nz))
        pltpu.make_async_copy(users.at[:, pl.ds(0, 2 * rows)], everyone, usem.at[0]).start()
        own_part.start()
        for d in range(1, nx):
            positive_copy(d).start()
        here = stats[pl.ds(c, 1)][0]
        there = across[...]
        tops = jnp.maximum(here[:, :, 0], there[:, :, 0])
        joined[:, :, 0] = tops
        joined[:, :, 1] = here[:, :, 1] * jnp.exp2(here[:, :, 0] - tops) + there[
            :, :, 1
        ] * jnp.exp2(there[:, :, 0] - tops)

        def out(d, _):
            p = lax.rem(z + d, nz)
            remote(joined.at[p], came.at[z], s1, r1, d, {"z": p}).start()
            return 0

        lax.fori_loop(1, nz, out, 0)
        came[pl.ds(z, 1)] = joined[pl.ds(z, 1)]
        mine[...] = jnp.zeros_like(mine)
        factor[...] = jnp.zeros_like(factor)
        lost[pl.ds(x, 1)] = jnp.zeros((1,) + lost.shape[1:], jnp.float32)

    def total():
        pltpu.make_async_copy(users.at[:, pl.ds(0, 2 * rows)], everyone, usem.at[0]).wait()
        own_part.wait()
        for d in range(1, nx):
            frm = lax.rem(x - d + nx, nx)
            landing = positive.at[:, columns(frm)]
            remote(landing, landing, s4, r4, d, {"x": frm}).wait_recv()

        def come(d, _):
            p = lax.rem(z + nz - d, nz)
            remote(came.at[p], came.at[p], s1, r1, d, {"z": p}).wait_recv()
            return 0

        lax.fori_loop(1, nz, come, 0)
        for i in range(2):
            u = everyone[z * nc + c, i * rows:(i + 1) * rows].astype(jnp.float32)
            v = positive[i * rows:(i + 1) * rows].astype(jnp.float32)
            dot = as_row(jnp.sum(u * v, axis=1, keepdims=True)) * (scale * LOG2E)
            tops = came[:, i, 0, :, 0:rows]
            sums = came[:, i, 1, :, 0:rows]
            ceiling = jnp.maximum(jnp.max(tops, axis=0), dot)
            whole = jnp.log(
                jnp.sum(sums * jnp.exp2(tops - ceiling[None]), axis=0) + jnp.exp2(dot - ceiling)
            )
            log_total = ceiling + whole * LOG2E
            mine[i, :, 0:rows] = log_total
            lost[pl.ds(x, 1), i, :, 0:rows] = (whole + (ceiling - dot) * LN2)[None]
            factor[i, :, 0:rows] = jnp.exp2(dot - log_total) - 1.0

        def give(d, _):
            p = lax.rem(z + d, nz)
            remote(mine, got.at[z], s2, r2, d, {"z": p}).start()
            return 0

        lax.fori_loop(1, nz, give, 0)
        for d in range(1, nx):
            remote(lost.at[x], lost.at[x], s3, r3, d, {"x": lax.rem(x + d, nx)}).start()
        got[pl.ds(z, 1)] = mine[...][None]

    beside_copy = remote(got, beside, s0, r0, 1, sibling)

    def spread():
        def done(d, _):
            p = lax.rem(z + nz - d, nz)
            remote(got.at[p], got.at[p], s2, r2, d, {"z": p}).wait_recv()
            return 0

        lax.fori_loop(1, nz, done, 0)
        beside_copy.start()

    def weigh(core, logs, first, count):
        def one(k, _):
            w = k * nc + core
            both = 0.0
            for i in range(2):
                level = stats[core, k, i, 0, :, pl.ds(0, rows)]
                share = jnp.exp2(level - logs[k, i, :, pl.ds(0, rows)])
                mass = masses[2 * w + i, :, :, pl.ds(0, rows)] * share[None]
                mass = mass.reshape(mass.shape[0] * mass.shape[1], rows).astype(jnp.bfloat16)
                both = both + jnp.dot(
                    mass, everyone[w, i * rows:(i + 1) * rows], preferred_element_type=jnp.float32
                )
            terms[w] = both
            return 0

        lax.fori_loop(first, first + count, one, 0)

    def cluster_copy(k):
        px, py = place(*pairs[k])
        return remote(cluster.at[py, px], parts.at[k], cl_s, cl_r, k, {"x": px, "y": py})

    def clusters():
        flat = terms[...].reshape(terms.shape[0] * terms.shape[1], width)
        pick = lax.broadcasted_iota(jnp.int32, (ny * per, flat.shape[0]), 0) == names[...]
        summed = jnp.dot(
            pick.astype(jnp.float32), flat, precision=lax.Precision.HIGHEST,
            preferred_element_type=jnp.float32,
        )
        for py in range(ny):
            for px in range(nx):
                cluster[py, px] = summed[py * per:(py + 1) * per, px * depth:(px + 1) * depth]
        for k in range(len(pairs)):
            cluster_copy(k).start()

    part = nz // 2
    tasks = [
        (0, send_stats),
        (2, total),
        (4, spread),
        (4, lambda: weigh(c, got, 0, part)),
        (5, lambda: weigh(c, got, part, nz - part)),
        (6, beside_copy.wait_recv),
        (6, lambda: weigh(1 - c, beside, 0, part)),
        (7, lambda: weigh(1 - c, beside, part, nz - part)),
        (7, clusters),
    ]

    begin(range(min(3, nz)))
    for levels in (klong_out, kshort_out):
        levels[...] = jnp.zeros_like(levels)
    over.wait_recv()
    for s in range(steps):
        ready(steps - s)
        if s > 0:
            ready(s - steps)
        for i in range(2):
            sign = 1 if i == 0 else -1
            extra = []
            if s > 0:
                arrive(longs(s - 1, i))
                extra = [(klong_in[s - 1, i, :, 0:rows], long_in[s - 1, i])]
            value, top = merged(sign * (steps - s) if s > 0 else steps, i, extra)
            long_out[s, i] = value.astype(jnp.bfloat16)
            klong_out[s, i, :, 0:rows] = top
            for copy in longs(s, i):
                copy.start()
            if s > 0:
                extra = []
                if s > 1:
                    arrive(shorts(s - 1, i))
                    extra = [(kshort_in[s - 2, i, :, 0:rows], short_in[s - 2, i])]
                value, top = merged(sign * (s - steps), i, extra)
                short_out[s - 1, i] = value.astype(jnp.bfloat16)
                kshort_out[s - 1, i, :, 0:rows] = top
                for copy in shorts(s, i):
                    copy.start()
        while tasks and (tasks[0][0] == s or s == steps - 1):
            tasks.pop(0)[1]()
    def end(d, i):
        px = lax.rem(x + d, nx)
        return remote(final.at[px, i], landed.at[x, i], fin_s, fin_r, 2 * d + i, {"x": px})

    ready(0)
    for i in range(2):
        arrive(shorts(steps - 1, i))
        arrive(longs(steps - 1, i))
        value, top = merged(
            0, i,
            [
                (klong_in[steps - 1, i, :, 0:rows], long_in[steps - 1, i]),
                (kshort_in[steps - 2, i, :, 0:rows], short_in[steps - 2, i]),
            ],
        )
        wide = positive[i * rows:(i + 1) * rows].astype(jnp.float32)
        value = value * as_column(jnp.exp2(top - mine[i, :, 0:rows]))
        value = (value + as_column(factor[i, :, 0:rows]) * wide) * factor_scale
        for k in range(nx):
            final[k, i] = value[:, k * depth:(k + 1) * depth]
        for d in sorted(range(1, nx), key=lambda d: abs(2 * d - nx)):
            end(d, i).start()
    whole = cluster[y, x]
    for k in range(len(pairs)):
        cluster_copy(k).wait_recv()
        whole = whole + parts[k]
    centroid_grad[...] = whole * factor_scale
    user_grad[pl.ds(x, 1)] = final[pl.ds(x, 1)]
    for d in range(1, nx):
        frm = lax.rem(x - d + nx, nx)
        remote(lost.at[frm], lost.at[frm], s3, r3, d, {"x": frm}).wait_recv()
    losses[...] = lost[...]
    for i in range(2):
        for d in range(1, nx):
            frm = lax.rem(x - d + nx, nx)
            landing = landed.at[frm, i]
            remote(landing, landing, fin_s, fin_r, 2 * d + i, {"x": frm}).wait_recv()
            user_grad[pl.ds(frm, 1), i] = landed[pl.ds(frm, 1), i]

    for copy in crossing + [cluster_copy(k) for k in range(len(pairs))] + [over, beside_copy]:
        copy.wait_send()
    for i in range(2):
        for s in range(steps):
            for copy in longs(s, i) + (shorts(s, i) if s > 0 else ()):
                copy.wait_send()
        for d in range(1, nx):
            end(d, i).wait_send()

    def left(d, _):
        p = lax.rem(z + d, nz)
        remote(joined.at[p], came.at[z], s1, r1, d, {"z": p}).wait_send()
        remote(mine, got.at[z], s2, r2, d, {"z": p}).wait_send()
        return 0

    lax.fori_loop(1, nz, left, 0)
    for d in range(1, nx):
        remote(lost.at[x], lost.at[x], s3, r3, d, {"x": lax.rem(x + d, nx)}).wait_send()
        positive_copy(d).wait_send()


def params(identity=None, megabytes=48):
    return pltpu.CompilerParams(
        collective_id=identity,
        has_side_effects=identity is not None,
        vmem_limit_bytes=megabytes * 1024 * 1024,
    )


def lanes_of(rows):
    return -(-rows // 128) * 128


def buffers_of(rows, width, nx, quarter):
    return [
        pltpu.VMEM((SLOTS, rows, width), jnp.bfloat16),
        pltpu.VMEM((SLOTS, nx, quarter, width), jnp.bfloat16),
        pltpu.SemaphoreType.DMA((SLOTS,)),
        pltpu.SemaphoreType.DMA((SLOTS,)),
    ]


def flash_call(nw, ny, half, scale, rows, width, nx, quarter):
    sds = jax.ShapeDtypeStruct
    lanes = lanes_of(rows)
    return pl.pallas_call(
        functools.partial(flash_kernel, half, scale),
        out_shape=(
            sds((2, nw // 2, 2, 2, 1, lanes), jnp.float32),
            sds((2 * nw, ny, MASS_ROWS, lanes), jnp.float32),
            sds((2 * nw, rows, width), jnp.bfloat16),
        ),
        in_specs=[SMEM, SMEM, HBM, HBM, VMEM, HBM],
        out_specs=[VMEM, VMEM, HBM],
        input_output_aliases={5: 2},
        scratch_shapes=[pltpu.SMEM((nw * ny + 8,), jnp.int32)]
        + buffers_of(rows, width, nx, quarter)
        + [
            pltpu.VMEM((rows, width), jnp.float32),
            pltpu.VMEM((2, rows, width), jnp.bfloat16),
            pltpu.SemaphoreType.DMA((2,)),
        ],
        compiler_params=params(None, 58),
        name="flash",
    )


def return_call(sizes, scale, rows, width, per):
    nx, nz, ny, nc = sizes
    lanes, depth, steps, nw = lanes_of(rows), width // nx, nz // 2, nz * nc
    sds = lambda *shape: jax.ShapeDtypeStruct(shape, jnp.float32)
    buffer = lambda *shape: pltpu.VMEM(shape, jnp.float32)
    ring = lambda n: pltpu.VMEM((n, 2, rows, width), jnp.bfloat16)
    dma = pltpu.SemaphoreType.DMA
    return pl.pallas_call(
        functools.partial(return_kernel, sizes, scale, LOSS_SCALE * scale),
        out_shape=(sds(nx, 2, rows, depth), sds(per, depth), sds(nx, 2, 1, lanes)),
        in_specs=[HBM, VMEM, VMEM, VMEM, HBM, HBM],
        out_specs=[VMEM] * 3,
        scratch_shapes=[
            ring(nz), ring(nz), ring(steps), ring(steps), ring(steps - 1), ring(steps - 1),
            buffer(steps, 2, 1, lanes), buffer(steps, 2, 1, lanes),
            buffer(steps - 1, 2, 1, lanes), buffer(steps - 1, 2, 1, lanes),
            buffer(nx, 2, rows, depth), buffer(nx, 2, rows, depth),
            buffer(max(nx * ny - 1, 1), per, depth), buffer(ny, nx, per, depth),
            pltpu.VMEM((nw, 2 * rows, width), jnp.bfloat16),
            buffer(nw, ny * MASS_ROWS, width),
            buffer(nz, 2, 2, 1, lanes), buffer(nz, 2, 2, 1, lanes), buffer(nz, 2, 2, 1, lanes),
            buffer(2, 1, lanes), buffer(nz, 2, 1, lanes), buffer(nz, 2, 1, lanes),
            buffer(nx, 2, 1, lanes), buffer(2, 1, lanes),
            pltpu.VMEM((2 * rows, width), jnp.bfloat16),
            dma((nz,)), dma((nz,)), dma((nz,)),
        ]
        + [dma((2 * steps,))] * 8
        + [dma((2 * nx,))] * 2
        + [dma((nx * ny,))] * 2
        + [dma((2,))] * 2
        + [dma((nz,))] * 4
        + [dma((nx,))] * 4
        + [dma((2,))],
        compiler_params=params(2, 58),
        name="return",
    )


def local(
    sizes, user_rows, positive_rows, centroids, residuals, block_lists, block_lengths,
    cluster_counts, ad_counts,
):
    nx, nz, ny, nc = sizes
    x, z, y, c = (lax.axis_index(a) for a in AXES)
    nw, shards = nz * nc, nz * ny * nc
    per, width = centroids.shape
    quarter = residuals.shape[1]
    tile = ad_counts.shape[1]
    blocks, listed = block_lists.shape
    rows = user_rows.shape[0] // blocks
    half = per // 2
    scale = 1.0 / math.sqrt(width)
    sds = jax.ShapeDtypeStruct
    dma = pltpu.SemaphoreType.DMA
    bf16, f32 = jnp.bfloat16, jnp.float32

    ad_rows = (centroids[:, None, :] + residuals.astype(f32)).astype(bf16)
    weights = ad_counts.astype(f32)
    expected = (
        cluster_counts.astype(f32)[:, None] * weights / jnp.sum(weights, axis=1, keepdims=True)
    )
    shift = jnp.log(expected).astype(bf16)
    flat = block_lists.reshape(blocks * listed)
    used = jnp.arange(listed)[None, :] < block_lengths[:, None]
    name = jnp.where(used, jnp.arange(blocks)[:, None] + 1, 0).reshape(blocks * listed)
    match = flat[:, None] // per == jnp.arange(shards)[None, :]
    block_of = jnp.sum(jnp.where(match, name[:, None], 0), axis=0) - 1
    place_of = jnp.sum(jnp.where(match, (flat % per)[:, None], 0), axis=0)
    codes = jnp.stack([block_of, place_of]).astype(f32).astype(bf16)
    codes = jnp.pad(codes, ((0, CODE_ROWS - 2), (0, width - shards)))

    steps = nz // 2
    copies = (nx - 1) + (ny - 1) + 8 + 4 + 12 + 16 + (nz - 1) + nz
    mine = 2 * rows
    all_tiles, all_users, all_shift, zeroed = pl.pallas_call(
        functools.partial(gather_kernel, sizes),
        out_shape=(
            sds((ny, nx, 2, half, quarter, width), bf16),
            sds((nz, nc, mine + CODE_ROWS, width), bf16),
            sds((ny, per, tile), bf16),
            sds((2 * nw, rows, width), bf16),
        ),
        in_specs=[HBM] * 4,
        out_specs=[HBM] * 4,
        scratch_shapes=[
            dma((copies,)), dma((copies,)), dma((4,)),
            pltpu.VMEM((4, rows, width), bf16), dma((nw // 2,)),
        ],
        compiler_params=params(0, 58),
        name="gather",
    )(ad_rows.reshape(2, half, quarter, width), user_rows, codes, shift)

    pick = jnp.arange(shards)[:, None] == z * ny * nc + jnp.arange(ny)[None, :] * nc + c
    found = all_users[:, :, mine:mine + 2, :shards].reshape(nw * 2, shards)
    places = jnp.dot(found, pick.astype(bf16), preferred_element_type=f32).astype(jnp.int32)
    flat_users = all_users.reshape(nw, mine + CODE_ROWS, width)
    flat_shift = all_shift.reshape(ny * per, tile)
    stats, masses, grads = flash_call(nw, ny, half, scale, rows, width, nx, quarter)(
        places, x.astype(jnp.int32).reshape(1), flat_users, all_tiles, flat_shift, zeroed
    )
    depth = width // nx
    names = places.reshape(nw, 2, ny)[:, 1] + per * jnp.arange(ny)[None, :]
    names = jnp.repeat(names.reshape(1, nw * ny), MASS_ROWS, axis=1)
    user_grad, centroid_grad, losses = return_call(sizes, scale, rows, width, per)(
        grads.reshape(nz, nc, 2, rows, width), stats, masses, names, flat_users, positive_rows
    )
    return (
        losses[:, :, 0, :rows].reshape(blocks * rows),
        user_grad.reshape(blocks * rows, depth),
        centroid_grad,
    )


def build(mesh, sizes):
    return jax.shard_map(
        functools.partial(local, sizes),
        mesh=mesh,
        in_specs=(
            P(("z", "y", "c"), "x"),
            P(("z", "y", "c"), "x"),
            P(("z", "y", "c"), None),
            P(("z", "y", "c"), "x", None),
            P(("z", "y", "c"), None),
            P(("z", "y", "c")),
            P(("z", "y", "c")),
            P(("z", "y", "c"), None),
        ),
        out_specs=(P(("z", "y", "c")), P(("z", "y", "c"), "x"), P(("z", "y", "c"), "x")),
        check_vma=False,
    )


def solution(mesh):
    sizes = (mesh.shape["tower"],) + SPLIT
    return build(Mesh(mesh.devices.reshape(sizes), AXES), sizes)
```

```python
import functools
import math

import jax
import jax.numpy as jnp
from jax import lax
from jax.experimental import pallas as pl
from jax.experimental.pallas import tpu as pltpu
from jax.sharding import Mesh, PartitionSpec as P

LOSS_SCALE = 16
AXES = ("x", "z", "y", "c")
SPLIT = (16, 4, 2)
LOW = -1e30
LOG2E = math.log2(math.e)
LN2 = math.log(2.0)
MESH = pl.DeviceIdType.MESH
HBM = pl.BlockSpec(memory_space=pl.ANY)
VMEM = pl.BlockSpec(memory_space=pltpu.VMEM)
SMEM = pl.BlockSpec(memory_space=pltpu.SMEM)
CODE_ROWS = 16
SLOTS = 8
MASS_ROWS = 8


def remote(src, dst, sends, recvs, k, where):
    return pltpu.make_async_remote_copy(
        src_ref=src,
        dst_ref=dst,
        send_sem=sends.at[k],
        recv_sem=recvs.at[k],
        device_id=where,
        device_id_type=MESH,
    )


def greet(peers):
    barrier = pltpu.get_barrier_semaphore()
    for where in peers:
        pl.semaphore_signal(barrier, inc=1, device_id=where, device_id_type=MESH)
    pl.semaphore_wait(barrier, len(peers))


def gather_kernel(
    sizes, tiles, users, codes, shift,
    all_tiles, all_users, all_shift, zeroed, sends, recvs, locals_, zbuf, zsem,
):
    nx, nz, ny, nc = sizes
    x, z, y, c = (lax.axis_index(a) for a in AXES)
    rows = users.shape[0] // nx
    depth = users.shape[1]
    half = tiles.shape[1]
    quarter = half // 2
    at_x = lambda d: lax.rem(x + d + nx, nx)
    at_y = lambda d: lax.rem(y + d + ny, ny)
    at_z = lambda d: lax.rem(z + d + nz, nz)
    to_x = lambda d: {"x": at_x(d)}
    to_y = lambda d: {"y": at_y(d)}
    to_z = lambda d: {"z": at_z(d)}
    sibling = {"c": 1 - c}

    greet(
        [to_x(d) for d in range(1, nx)]
        + [to_y(d) for d in range(1, ny)]
        + [to_z(1), to_z(-1), sibling]
    )

    count = [0]
    sent = []

    def push(src, dst, where, landing):
        k = count[0]
        count[0] += 1
        copy = remote(src, dst, sends, recvs, k, where)
        copy.start()
        sent.append(copy)
        return remote(landing, landing, sends, recvs, k, where)

    columns = lambda i: pl.ds(pl.multiple_of(i * depth, depth), depth)
    part = lambda i: pl.ds(pl.multiple_of(i * rows, rows), rows)
    home = all_users.at[z, c]

    def block(h, a, b):
        return all_tiles.at[at_y(b), at_x(a), h] if h == 0 else all_tiles.at[at_y(a), at_x(b), h]

    first = (to_x, to_y)
    second = (to_y, to_x)
    lower, upper = pl.ds(0, quarter), pl.ds(quarter, quarter)

    arrivals = []
    for d in range(1, nx):
        arrivals.append(
            push(
                users.at[part(at_x(d))], home.at[pl.ds(0, rows), columns(x)], to_x(d),
                home.at[pl.ds(0, rows), columns(at_x(-d))],
            )
        )
    p1 = {}
    for h in (0, 1):
        for d in (1, -1):
            p1[h, d] = push(tiles.at[h], block(h, 0, 0), first[h](d), block(h, -d, 0))
    own = [
        pltpu.make_async_copy(users.at[part(x)], home.at[pl.ds(0, rows), columns(x)], locals_.at[0]),
        pltpu.make_async_copy(codes, home.at[pl.ds(rows, CODE_ROWS)], locals_.at[1]),
        pltpu.make_async_copy(tiles, all_tiles.at[y, x], locals_.at[2]),
        pltpu.make_async_copy(shift, all_shift.at[y], locals_.at[3]),
    ]
    for copy in own:
        copy.start()
    zbuf[...] = jnp.zeros_like(zbuf)
    piece = zbuf.shape[0]
    zeros = [
        pltpu.make_async_copy(zbuf, zeroed.at[pl.ds(k * piece, piece)], zsem.at[k])
        for k in range(zeroed.shape[0] // piece)
    ]
    for copy in zeros:
        copy.start()
    late = []
    p2 = {}
    for h in (0, 1):
        for d in (1, -1):
            p2[h, 0, d] = push(tiles.at[h], block(h, 0, 0), second[h](d), block(h, 0, -d))
    for d in range(1, ny):
        late.append(push(shift, all_shift.at[y], to_y(d), all_shift.at[at_y(-d)]))

    for arrival in arrivals:
        arrival.wait_recv()
    own[0].wait()
    own[1].wait()

    chunk = lambda d: all_users.at[at_z(d), c]
    other = lambda d: all_users.at[at_z(d), 1 - c]
    steps = nz // 2
    up, down = {}, {}

    def ring(s):
        if s > 0:
            up[s - 1].wait_recv()
            if s - 1 in down:
                down[s - 1].wait_recv()
        if s < steps:
            up[s] = push(chunk(-s), chunk(-s), to_z(1), chunk(-s - 1))
        if s < steps - 1:
            down[s] = push(chunk(s), chunk(s), to_z(-1), chunk(s + 1))
        late.append(push(chunk(-s), chunk(-s), sibling, other(-s)))
        if 0 < s < steps:
            late.append(push(chunk(s), chunk(s), sibling, other(s)))

    turns = list(range(steps + 1))
    ring(turns.pop(0))
    while len(turns) > steps - 3 and turns:
        ring(turns.pop(0))

    for h in (0, 1):
        for d in (1, -1):
            p1[h, d].wait_recv()
    q = {}
    for h in (0, 1):
        for d in (1, -1):
            cut = lower if d == 1 else upper
            q[h, d] = push(
                block(h, -d, 0).at[cut], block(h, -d, 0).at[cut], first[h](d), block(h, -2 * d, 0).at[cut]
            )
    for j in (1, -1):
        for h in (0, 1):
            for d in (1, -1):
                p2[h, j, d] = push(block(h, j, 0), block(h, j, 0), second[h](d), block(h, j, -d))
    if turns:
        ring(turns.pop(0))

    def onward(j):
        for h in (0, 1):
            for d in (1, -1):
                p2[h, j, d].wait_recv()
                cut = lower if d == 1 else upper
                late.append(
                    push(
                        block(h, j, -d).at[cut], block(h, j, -d).at[cut], second[h](d),
                        block(h, j, -2 * d).at[cut],
                    )
                )

    onward(0)
    for h in (0, 1):
        for d in (1, -1):
            q[h, d].wait_recv()
    for h in (0, 1):
        for d in (1, -1):
            p2[h, 2, d] = push(block(h, 2, 0), block(h, 2, 0), second[h](d), block(h, 2, -d))
    if turns:
        ring(turns.pop(0))
    onward(1)
    while turns:
        ring(turns.pop(0))
    onward(-1)
    onward(2)
    for arrival in late:
        arrival.wait_recv()
    for copy in own[2:] + zeros:
        copy.wait()
    for copy in sent:
        copy.wait_send()
    assert count[0] == sends.shape[0], count[0]


def fetch(users, tiles, entry, ubuf, tbuf, usem, tsem, half, e, slot):
    b, tile = entry(e)
    per = 2 * half
    yp, cl = tile // per, tile % per
    w, i = b // 2, b % 2
    rows = ubuf.shape[1]
    return (
        pltpu.make_async_copy(
            users.at[w, pl.ds(pl.multiple_of(i * rows, rows), rows)], ubuf.at[slot], usem.at[slot]
        ),
        pltpu.make_async_copy(
            tiles.at[yp, :, cl // half, cl % half], tbuf.at[slot], tsem.at[slot]
        ),
    )


def ads_of(tbuf, slot):
    return tbuf[slot].reshape(tbuf.shape[1] * tbuf.shape[2], tbuf.shape[3])


def scores(ubuf, tbuf, shift_ref, slot, tile, scale):
    user = ubuf[slot]
    ads = ads_of(tbuf, slot)
    pick = lax.broadcasted_iota(jnp.int32, (shift_ref.shape[0], user.shape[0]), 0) == tile
    shift = lax.dot_general(
        shift_ref[...], pick.astype(jnp.float32).astype(jnp.bfloat16), (((0,), (0,)), ((), ())),
        preferred_element_type=jnp.float32,
    )
    raw = lax.dot_general(ads, user, (((1,), (1,)), ((), ())), preferred_element_type=jnp.float32)
    return raw * scale - shift


def flash_kernel(
    half, scale, codes, mine, users, tiles, shift_ref, _zeroed,
    stats, masses, grads, list_ref, ubuf, tbuf, usem, tsem, acc, gout, gsem,
):
    nw = users.shape[0]
    ny = tiles.shape[0]
    rows = ubuf.shape[1]
    parts = tbuf.shape[1]
    t = mine[0]
    tiles_all = ny * 2 * half

    def entry(e):
        return list_ref[e] // tiles_all, list_ref[e] % tiles_all

    def gather(w, n):
        for i in range(2):
            for yp in range(ny):
                list_ref[n] = (w * 2 + i) * tiles_all + yp * (2 * half) + codes[2 * w + 1, yp]
                n = n + (codes[2 * w, yp] == 2 * t + i).astype(jnp.int32)
        return n

    total = lax.fori_loop(0, nw, gather, jnp.int32(0))
    list_ref[total] = 2 * nw * tiles_all
    get = functools.partial(fetch, users, tiles, entry, ubuf, tbuf, usem, tsem, half)
    ahead = ubuf.shape[0] - 1
    for k in range(ahead):
        @pl.when(total > k)
        def _():
            for copy in get(k, k):
                copy.start()

    stats[:, :, :, 0] = jnp.full(stats.shape[:3] + stats.shape[4:], LOW, jnp.float32)
    stats[:, :, :, 1] = jnp.zeros(stats.shape[:3] + stats.shape[4:], jnp.float32)
    masses[...] = jnp.zeros_like(masses)

    def put(b, slot):
        return pltpu.make_async_copy(gout.at[slot], grads.at[b], gsem.at[slot])

    def score(e):
        return scores(ubuf, tbuf, shift_ref, e % (ahead + 1), entry(e)[1], scale)

    @pl.when(total > 0)
    def _():
        for copy in get(0, 0):
            copy.wait()

    def step(e, held_over):
        n, logits = held_over
        slot = e % (ahead + 1)

        @pl.when(e + ahead < total)
        def _():
            for copy in get(e + ahead, (e + ahead) % (ahead + 1)):
                copy.start()

        @pl.when(e + 1 < total)
        def _():
            for copy in get(e + 1, (e + 1) % (ahead + 1)):
                copy.wait()

        b, tile = entry(e)
        fresh = jnp.logical_or(e == 0, entry(jnp.maximum(e - 1, 0))[0] != b)
        last = entry(e + 1)[0] != b
        at = ((b // 2) % 2, b // 4, b % 2)
        later = score(e + 1)
        ads = ads_of(tbuf, slot)
        logits = logits * LOG2E
        before = stats[at + (0, slice(None), pl.ds(0, rows))]
        held = stats[at + (1, slice(None), pl.ds(0, rows))]
        top = jnp.maximum(before, jnp.ceil(jnp.max(logits, axis=0, keepdims=True)))
        carry = jnp.exp2(before - top)
        terms = jnp.exp2(logits - top)
        stats[at + (0, slice(None), pl.ds(0, rows))] = top
        stats[at + (1, slice(None), pl.ds(0, rows))] = held * carry + jnp.sum(
            terms, axis=0, keepdims=True
        )
        probs = terms.astype(jnp.bfloat16)
        wide = probs.astype(jnp.float32).reshape(parts, probs.shape[0] // parts, rows)
        mass = jnp.sum(wide, axis=1)
        term = lax.dot_general(probs, ads, (((0,), (0,)), ((), ())), preferred_element_type=jnp.float32)

        @pl.when(fresh)
        def _():
            acc[...] = term

        @pl.when(jnp.logical_not(fresh))
        def _():
            acc[...] = acc[...] * as_column(carry) + term
            masses[b, :, :, 0:rows] = masses[b, :, :, 0:rows] * carry[None]

        masses[b, tile // (2 * half), 0:parts, 0:rows] = mass

        @pl.when(last)
        def _():
            to = n % 2

            @pl.when(n >= 2)
            def _():
                put(0, to).wait()

            gout[to] = acc[...].astype(jnp.bfloat16)
            put(b, to).start()

        return n + last.astype(jnp.int32), later

    n, _ = lax.fori_loop(0, total, step, (jnp.int32(0), score(0)))
    for k in range(2):
        @pl.when(n > k)
        def _():
            put(0, k).wait()


def as_row(column):
    n = column.shape[0]
    eye = lax.broadcasted_iota(jnp.int32, (n, n), 0) == lax.broadcasted_iota(jnp.int32, (n, n), 1)
    return jnp.sum(jnp.where(eye, column, 0.0), axis=0, keepdims=True)


def as_column(row):
    n = row.shape[1]
    eye = lax.broadcasted_iota(jnp.int32, (n, n), 0) == lax.broadcasted_iota(jnp.int32, (n, n), 1)
    return jnp.sum(jnp.where(eye, row, 0.0), axis=1, keepdims=True)


def diagonal(row):
    n = row.shape[1]
    eye = lax.broadcasted_iota(jnp.int32, (n, n), 0) == lax.broadcasted_iota(jnp.int32, (n, n), 1)
    return jnp.where(eye, row, 0.0).astype(jnp.bfloat16)


def return_kernel(
    sizes, scale, factor_scale, grads, stats, masses, names, users, positives,
    user_grad, centroid_grad, losses,
    own, sib, long_out, long_in, short_out, short_in,
    klong_out, klong_in, kshort_out, kshort_in,
    final, packed, landed, parts, cluster, everyone, terms,
    across, joined, came, mine, got, beside, lost, factor, positive,
    own_sem, sib_s, sib_r, long_s, long_r, short_s, short_r,
    kl_s, kl_r, ks_s, ks_r, fin_s, fin_r, cl_s, cl_r,
    s0, r0, s1, r1, s2, r2, s3, r3, s4, r4, usem,
):
    nx, nz, ny, nc = sizes
    x, z, y, c = (lax.axis_index(a) for a in AXES)
    at_z = lambda d: lax.rem(z + d + nz, nz)
    above, below = {"z": at_z(1)}, {"z": at_z(-1)}
    sibling = {"c": 1 - c}
    rows, width = own.shape[2], own.shape[3]
    per, depth = cluster.shape[2], cluster.shape[3]
    steps = nz // 2
    pairs = [(dx, dy) for dx in range(nx) for dy in range(ny) if dx or dy]
    place = lambda dx, dy: (lax.rem(x + dx + nx, nx), lax.rem(y + dy + ny, ny))
    greet(
        [{"z": at_z(d)} for d in range(1, nz)]
        + [dict(zip(("x", "y"), place(dx, dy))) for dx, dy in pairs]
        + [sibling]
    )
    over = remote(stats.at[1 - c], across, s0, r0, 0, sibling)
    over.start()
    order = []
    for s in range(steps):
        order.append(steps - s)
        if s > 0:
            order.append(s - steps)
    order.append(0)
    index = {d: k for k, d in enumerate(order)}
    loads = [
        pltpu.make_async_copy(grads.at[at_z(d), c], own.at[k], own_sem.at[k])
        for k, d in enumerate(order)
    ]
    crossing = [
        remote(grads.at[at_z(d), 1 - c], sib.at[k], sib_s, sib_r, k, sibling)
        for k, d in enumerate(order)
    ]

    def begin(ks):
        for k in ks:
            loads[k].start()
            crossing[k].start()

    def ready(d):
        loads[index[d]].wait()
        crossing[index[d]].wait_recv()

    def merged(d, i, extra):
        k = index[d]
        items = [
            (stats[c, at_z(d), i, 0, :, pl.ds(0, rows)], own[k, i]),
            (across[at_z(d), i, 0, :, pl.ds(0, rows)], sib[k, i]),
        ] + extra
        top = items[0][0]
        for level, _ in items[1:]:
            top = jnp.maximum(top, level)
        whole = 0.0
        for level, value in items:
            whole = whole + jnp.dot(
                diagonal(jnp.exp2(level - top)), value, preferred_element_type=jnp.float32
            )
        return whole, top

    away = lambda i: above if i == 0 else below
    back = lambda i: below if i == 0 else above
    longs = lambda s, i: (
        remote(long_out.at[s, i], long_in.at[s, i], long_s, long_r, 2 * s + i, away(i)),
        remote(klong_out.at[s, i], klong_in.at[s, i], kl_s, kl_r, 2 * s + i, away(i)),
    )
    shorts = lambda s, i: (
        remote(short_out.at[s - 1, i], short_in.at[s - 1, i], short_s, short_r, 2 * s + i, back(i)),
        remote(kshort_out.at[s - 1, i], kshort_in.at[s - 1, i], ks_s, ks_r, 2 * s + i, back(i)),
    )

    def arrive(copies):
        for copy in copies:
            copy.wait_recv()

    part_of = lambda i: pl.ds(pl.multiple_of(i * 2 * rows, 2 * rows), 2 * rows)
    columns = lambda i: pl.ds(pl.multiple_of(i * depth, depth), depth)
    own_part = pltpu.make_async_copy(positives.at[part_of(x)], positive.at[:, columns(x)], usem.at[1])

    def positive_copy(d):
        px = lax.rem(x + d, nx)
        return remote(positives.at[part_of(px)], positive.at[:, columns(x)], s4, r4, d, {"x": px})

    def send_stats():
        begin(range(min(3, nz), nz))
        pltpu.make_async_copy(users.at[:, pl.ds(0, 2 * rows)], everyone, usem.at[0]).start()
        own_part.start()
        for d in range(1, nx):
            positive_copy(d).start()
        here = stats[pl.ds(c, 1)][0]
        there = across[...]
        tops = jnp.maximum(here[:, :, 0], there[:, :, 0])
        joined[:, :, 0] = tops
        joined[:, :, 1] = here[:, :, 1] * jnp.exp2(here[:, :, 0] - tops) + there[
            :, :, 1
        ] * jnp.exp2(there[:, :, 0] - tops)

        def out(d, _):
            p = lax.rem(z + d, nz)
            remote(joined.at[p], came.at[z], s1, r1, d, {"z": p}).start()
            return 0

        lax.fori_loop(1, nz, out, 0)
        came[pl.ds(z, 1)] = joined[pl.ds(z, 1)]
        mine[...] = jnp.zeros_like(mine)
        factor[...] = jnp.zeros_like(factor)
        lost[pl.ds(x, 1)] = jnp.zeros((1,) + lost.shape[1:], jnp.float32)

    def total():
        pltpu.make_async_copy(users.at[:, pl.ds(0, 2 * rows)], everyone, usem.at[0]).wait()
        own_part.wait()
        for d in range(1, nx):
            frm = lax.rem(x - d + nx, nx)
            landing = positive.at[:, columns(frm)]
            remote(landing, landing, s4, r4, d, {"x": frm}).wait_recv()

        def come(d, _):
            p = lax.rem(z + nz - d, nz)
            remote(came.at[p], came.at[p], s1, r1, d, {"z": p}).wait_recv()
            return 0

        lax.fori_loop(1, nz, come, 0)
        for i in range(2):
            u = everyone[z * nc + c, i * rows:(i + 1) * rows].astype(jnp.float32)
            v = positive[i * rows:(i + 1) * rows].astype(jnp.float32)
            dot = as_row(jnp.sum(u * v, axis=1, keepdims=True)) * (scale * LOG2E)
            tops = came[:, i, 0, :, 0:rows]
            sums = came[:, i, 1, :, 0:rows]
            ceiling = jnp.maximum(jnp.max(tops, axis=0), dot)
            whole = jnp.log(
                jnp.sum(sums * jnp.exp2(tops - ceiling[None]), axis=0) + jnp.exp2(dot - ceiling)
            )
            log_total = ceiling + whole * LOG2E
            mine[i, :, 0:rows] = log_total
            lost[pl.ds(x, 1), i, :, 0:rows] = (whole + (ceiling - dot) * LN2)[None]
            factor[i, :, 0:rows] = jnp.exp2(dot - log_total) - 1.0

        def give(d, _):
            p = lax.rem(z + d, nz)
            remote(mine, got.at[z], s2, r2, d, {"z": p}).start()
            return 0

        lax.fori_loop(1, nz, give, 0)
        for d in range(1, nx):
            remote(lost.at[x], lost.at[x], s3, r3, d, {"x": lax.rem(x + d, nx)}).start()
        got[pl.ds(z, 1)] = mine[...][None]

    beside_copy = remote(got, beside, s0, r0, 1, sibling)

    def spread():
        def done(d, _):
            p = lax.rem(z + nz - d, nz)
            remote(got.at[p], got.at[p], s2, r2, d, {"z": p}).wait_recv()
            return 0

        lax.fori_loop(1, nz, done, 0)
        beside_copy.start()

    def weigh(core, logs, first, count):
        def one(k, _):
            w = k * nc + core
            both = 0.0
            for i in range(2):
                level = stats[core, k, i, 0, :, pl.ds(0, rows)]
                share = jnp.exp2(level - logs[k, i, :, pl.ds(0, rows)])
                mass = masses[2 * w + i, :, :, pl.ds(0, rows)] * share[None]
                mass = mass.reshape(mass.shape[0] * mass.shape[1], rows).astype(jnp.bfloat16)
                both = both + jnp.dot(
                    mass, everyone[w, i * rows:(i + 1) * rows], preferred_element_type=jnp.float32
                )
            terms[w] = both
            return 0

        lax.fori_loop(first, first + count, one, 0)

    def cluster_copy(k):
        px, py = place(*pairs[k])
        return remote(cluster.at[py, px], parts.at[k], cl_s, cl_r, k, {"x": px, "y": py})

    def clusters():
        flat = terms[...].reshape(terms.shape[0] * terms.shape[1], width)
        pick = lax.broadcasted_iota(jnp.int32, (ny * per, flat.shape[0]), 0) == names[...]
        summed = jnp.dot(
            pick.astype(jnp.float32), flat, precision=lax.Precision.HIGHEST,
            preferred_element_type=jnp.float32,
        )
        for py in range(ny):
            for px in range(nx):
                cluster[py, px] = summed[py * per:(py + 1) * per, px * depth:(px + 1) * depth]
        for k in range(len(pairs)):
            cluster_copy(k).start()

    part = nz // 2
    tasks = [
        (0, send_stats),
        (2, total),
        (4, spread),
        (4, lambda: weigh(c, got, 0, part)),
        (5, lambda: weigh(c, got, part, nz - part)),
        (6, beside_copy.wait_recv),
        (6, lambda: weigh(1 - c, beside, 0, part)),
        (7, lambda: weigh(1 - c, beside, part, nz - part)),
        (7, clusters),
    ]

    begin(range(min(3, nz)))
    for levels in (klong_out, kshort_out):
        levels[...] = jnp.zeros_like(levels)
    over.wait_recv()
    for s in range(steps):
        ready(steps - s)
        if s > 0:
            ready(s - steps)
        for i in range(2):
            sign = 1 if i == 0 else -1
            extra = []
            if s > 0:
                arrive(longs(s - 1, i))
                extra = [(klong_in[s - 1, i, :, 0:rows], long_in[s - 1, i])]
            value, top = merged(sign * (steps - s) if s > 0 else steps, i, extra)
            long_out[s, i] = value.astype(jnp.bfloat16)
            klong_out[s, i, :, 0:rows] = top
            for copy in longs(s, i):
                copy.start()
            if s > 0:
                extra = []
                if s > 1:
                    arrive(shorts(s - 1, i))
                    extra = [(kshort_in[s - 2, i, :, 0:rows], short_in[s - 2, i])]
                value, top = merged(sign * (s - steps), i, extra)
                short_out[s - 1, i] = value.astype(jnp.bfloat16)
                kshort_out[s - 1, i, :, 0:rows] = top
                for copy in shorts(s, i):
                    copy.start()
        while tasks and (tasks[0][0] == s or s == steps - 1):
            tasks.pop(0)[1]()
    def end(d, i):
        px = lax.rem(x + d, nx)
        return remote(packed.at[px, i], landed.at[x, i], fin_s, fin_r, 2 * d + i, {"x": px})

    ready(0)
    for i in range(2):
        arrive(shorts(steps - 1, i))
        arrive(longs(steps - 1, i))
        value, top = merged(
            0, i,
            [
                (klong_in[steps - 1, i, :, 0:rows], long_in[steps - 1, i]),
                (kshort_in[steps - 2, i, :, 0:rows], short_in[steps - 2, i]),
            ],
        )
        wide = positive[i * rows:(i + 1) * rows].astype(jnp.float32)
        value = value * as_column(jnp.exp2(top - mine[i, :, 0:rows]))
        value = (value + as_column(factor[i, :, 0:rows]) * wide) * factor_scale
        for k in range(nx):
            final[k, i] = value[:, k * depth:(k + 1) * depth]
            packed[k, i] = final[k, i].astype(jnp.bfloat16)
        for d in sorted(range(1, nx), key=lambda d: abs(2 * d - nx)):
            end(d, i).start()
    whole = cluster[y, x]
    for k in range(len(pairs)):
        cluster_copy(k).wait_recv()
        whole = whole + parts[k]
    centroid_grad[...] = whole * factor_scale
    user_grad[pl.ds(x, 1)] = final[pl.ds(x, 1)]
    for d in range(1, nx):
        frm = lax.rem(x - d + nx, nx)
        remote(lost.at[frm], lost.at[frm], s3, r3, d, {"x": frm}).wait_recv()
    losses[...] = lost[...]
    for i in range(2):
        for d in range(1, nx):
            frm = lax.rem(x - d + nx, nx)
            landing = landed.at[frm, i]
            remote(landing, landing, fin_s, fin_r, 2 * d + i, {"x": frm}).wait_recv()
            user_grad[pl.ds(frm, 1), i] = landed[pl.ds(frm, 1), i].astype(jnp.float32)

    for copy in crossing + [cluster_copy(k) for k in range(len(pairs))] + [over, beside_copy]:
        copy.wait_send()
    for i in range(2):
        for s in range(steps):
            for copy in longs(s, i) + (shorts(s, i) if s > 0 else ()):
                copy.wait_send()
        for d in range(1, nx):
            end(d, i).wait_send()

    def left(d, _):
        p = lax.rem(z + d, nz)
        remote(joined.at[p], came.at[z], s1, r1, d, {"z": p}).wait_send()
        remote(mine, got.at[z], s2, r2, d, {"z": p}).wait_send()
        return 0

    lax.fori_loop(1, nz, left, 0)
    for d in range(1, nx):
        remote(lost.at[x], lost.at[x], s3, r3, d, {"x": lax.rem(x + d, nx)}).wait_send()
        positive_copy(d).wait_send()


def params(identity=None, megabytes=48):
    return pltpu.CompilerParams(
        collective_id=identity,
        has_side_effects=identity is not None,
        vmem_limit_bytes=megabytes * 1024 * 1024,
    )


def lanes_of(rows):
    return -(-rows // 128) * 128


def buffers_of(rows, width, nx, quarter):
    return [
        pltpu.VMEM((SLOTS, rows, width), jnp.bfloat16),
        pltpu.VMEM((SLOTS, nx, quarter, width), jnp.bfloat16),
        pltpu.SemaphoreType.DMA((SLOTS,)),
        pltpu.SemaphoreType.DMA((SLOTS,)),
    ]


def flash_call(nw, ny, half, scale, rows, width, nx, quarter):
    sds = jax.ShapeDtypeStruct
    lanes = lanes_of(rows)
    return pl.pallas_call(
        functools.partial(flash_kernel, half, scale),
        out_shape=(
            sds((2, nw // 2, 2, 2, 1, lanes), jnp.float32),
            sds((2 * nw, ny, MASS_ROWS, lanes), jnp.float32),
            sds((2 * nw, rows, width), jnp.bfloat16),
        ),
        in_specs=[SMEM, SMEM, HBM, HBM, VMEM, HBM],
        out_specs=[VMEM, VMEM, HBM],
        input_output_aliases={5: 2},
        scratch_shapes=[pltpu.SMEM((nw * ny + 8,), jnp.int32)]
        + buffers_of(rows, width, nx, quarter)
        + [
            pltpu.VMEM((rows, width), jnp.float32),
            pltpu.VMEM((2, rows, width), jnp.bfloat16),
            pltpu.SemaphoreType.DMA((2,)),
        ],
        compiler_params=params(None, 58),
        name="flash",
    )


def return_call(sizes, scale, rows, width, per):
    nx, nz, ny, nc = sizes
    lanes, depth, steps, nw = lanes_of(rows), width // nx, nz // 2, nz * nc
    sds = lambda *shape: jax.ShapeDtypeStruct(shape, jnp.float32)
    buffer = lambda *shape: pltpu.VMEM(shape, jnp.float32)
    ring = lambda n: pltpu.VMEM((n, 2, rows, width), jnp.bfloat16)
    dma = pltpu.SemaphoreType.DMA
    return pl.pallas_call(
        functools.partial(return_kernel, sizes, scale, LOSS_SCALE * scale),
        out_shape=(sds(nx, 2, rows, depth), sds(per, depth), sds(nx, 2, 1, lanes)),
        in_specs=[HBM, VMEM, VMEM, VMEM, HBM, HBM],
        out_specs=[VMEM] * 3,
        scratch_shapes=[
            ring(nz), ring(nz), ring(steps), ring(steps), ring(steps - 1), ring(steps - 1),
            buffer(steps, 2, 1, lanes), buffer(steps, 2, 1, lanes),
            buffer(steps - 1, 2, 1, lanes), buffer(steps - 1, 2, 1, lanes),
            buffer(nx, 2, rows, depth),
            pltpu.VMEM((nx, 2, rows, depth), jnp.bfloat16),
            pltpu.VMEM((nx, 2, rows, depth), jnp.bfloat16),
            buffer(max(nx * ny - 1, 1), per, depth), buffer(ny, nx, per, depth),
            pltpu.VMEM((nw, 2 * rows, width), jnp.bfloat16),
            buffer(nw, ny * MASS_ROWS, width),
            buffer(nz, 2, 2, 1, lanes), buffer(nz, 2, 2, 1, lanes), buffer(nz, 2, 2, 1, lanes),
            buffer(2, 1, lanes), buffer(nz, 2, 1, lanes), buffer(nz, 2, 1, lanes),
            buffer(nx, 2, 1, lanes), buffer(2, 1, lanes),
            pltpu.VMEM((2 * rows, width), jnp.bfloat16),
            dma((nz,)), dma((nz,)), dma((nz,)),
        ]
        + [dma((2 * steps,))] * 8
        + [dma((2 * nx,))] * 2
        + [dma((nx * ny,))] * 2
        + [dma((2,))] * 2
        + [dma((nz,))] * 4
        + [dma((nx,))] * 4
        + [dma((2,))],
        compiler_params=params(2, 58),
        name="return",
    )


def local(
    sizes, user_rows, positive_rows, centroids, residuals, block_lists, block_lengths,
    cluster_counts, ad_counts,
):
    nx, nz, ny, nc = sizes
    x, z, y, c = (lax.axis_index(a) for a in AXES)
    nw, shards = nz * nc, nz * ny * nc
    per, width = centroids.shape
    quarter = residuals.shape[1]
    tile = ad_counts.shape[1]
    blocks, listed = block_lists.shape
    rows = user_rows.shape[0] // blocks
    half = per // 2
    scale = 1.0 / math.sqrt(width)
    sds = jax.ShapeDtypeStruct
    dma = pltpu.SemaphoreType.DMA
    bf16, f32 = jnp.bfloat16, jnp.float32

    ad_rows = (centroids[:, None, :] + residuals.astype(f32)).astype(bf16)
    weights = ad_counts.astype(f32)
    expected = (
        cluster_counts.astype(f32)[:, None] * weights / jnp.sum(weights, axis=1, keepdims=True)
    )
    shift = jnp.log(expected).astype(bf16)
    flat = block_lists.reshape(blocks * listed)
    used = jnp.arange(listed)[None, :] < block_lengths[:, None]
    name = jnp.where(used, jnp.arange(blocks)[:, None] + 1, 0).reshape(blocks * listed)
    match = flat[:, None] // per == jnp.arange(shards)[None, :]
    block_of = jnp.sum(jnp.where(match, name[:, None], 0), axis=0) - 1
    place_of = jnp.sum(jnp.where(match, (flat % per)[:, None], 0), axis=0)
    codes = jnp.stack([block_of, place_of]).astype(f32).astype(bf16)
    codes = jnp.pad(codes, ((0, CODE_ROWS - 2), (0, width - shards)))

    steps = nz // 2
    copies = (nx - 1) + (ny - 1) + 8 + 4 + 12 + 16 + (nz - 1) + nz
    mine = 2 * rows
    all_tiles, all_users, all_shift, zeroed = pl.pallas_call(
        functools.partial(gather_kernel, sizes),
        out_shape=(
            sds((ny, nx, 2, half, quarter, width), bf16),
            sds((nz, nc, mine + CODE_ROWS, width), bf16),
            sds((ny, per, tile), bf16),
            sds((2 * nw, rows, width), bf16),
        ),
        in_specs=[HBM] * 4,
        out_specs=[HBM] * 4,
        scratch_shapes=[
            dma((copies,)), dma((copies,)), dma((4,)),
            pltpu.VMEM((4, rows, width), bf16), dma((nw // 2,)),
        ],
        compiler_params=params(0, 58),
        name="gather",
    )(ad_rows.reshape(2, half, quarter, width), user_rows, codes, shift)

    pick = jnp.arange(shards)[:, None] == z * ny * nc + jnp.arange(ny)[None, :] * nc + c
    found = all_users[:, :, mine:mine + 2, :shards].reshape(nw * 2, shards)
    places = jnp.dot(found, pick.astype(bf16), preferred_element_type=f32).astype(jnp.int32)
    flat_users = all_users.reshape(nw, mine + CODE_ROWS, width)
    flat_shift = all_shift.reshape(ny * per, tile)
    stats, masses, grads = flash_call(nw, ny, half, scale, rows, width, nx, quarter)(
        places, x.astype(jnp.int32).reshape(1), flat_users, all_tiles, flat_shift, zeroed
    )
    depth = width // nx
    names = places.reshape(nw, 2, ny)[:, 1] + per * jnp.arange(ny)[None, :]
    names = jnp.repeat(names.reshape(1, nw * ny), MASS_ROWS, axis=1)
    user_grad, centroid_grad, losses = return_call(sizes, scale, rows, width, per)(
        grads.reshape(nz, nc, 2, rows, width), stats, masses, names, flat_users, positive_rows
    )
    return (
        losses[:, :, 0, :rows].reshape(blocks * rows),
        user_grad.reshape(blocks * rows, depth),
        centroid_grad,
    )


def build(mesh, sizes):
    return jax.shard_map(
        functools.partial(local, sizes),
        mesh=mesh,
        in_specs=(
            P(("z", "y", "c"), "x"),
            P(("z", "y", "c"), "x"),
            P(("z", "y", "c"), None),
            P(("z", "y", "c"), "x", None),
            P(("z", "y", "c"), None),
            P(("z", "y", "c")),
            P(("z", "y", "c")),
            P(("z", "y", "c"), None),
        ),
        out_specs=(P(("z", "y", "c")), P(("z", "y", "c"), "x"), P(("z", "y", "c"), "x")),
        check_vma=False,
    )


def solution(mesh):
    sizes = (mesh.shape["tower"],) + SPLIT
    return build(Mesh(mesh.devices.reshape(sizes), AXES), sizes)
```
